32 devices in a mesh: section: 2 (over y), dp: 16 (over z, x, core).
Axes of the slice: x: 2, y: 2, z: 4, core: 2. Of those that a mesh axis runs over, the one named last changes fastest.
Arguments:
- inputs: bfloat16 [2, 32, 1024, 512], P('section', 'dp'), may hold values from -6 to 6
- cotangent: bfloat16 [2, 32, 1024, 512], P('section', 'dp'), may hold values from -6 to 6
- lengths: int32 [32, 8], P('dp'), may hold values from 1 to 256, 1024 in all within a row
- norm1_gain: float32 [2, 512], P('section'), may hold values from 0.25 to 1.75
- norm1_bias: float32 [2, 512], P('section'), may hold values from -1 to 1
- weight_qkv: bfloat16 [2, 512, 1536], P('section'), may hold values from -0.25 to 0.25
- weight_out: bfloat16 [2, 512, 512], P('section'), may hold values from -0.75 to 0.75
- bias_out: float32 [2, 512], P('section'), may hold values from -1 to 1
- norm2_gain: float32 [2, 512], P('section'), may hold values from 0.25 to 1.75
- norm2_bias: float32 [2, 512], P('section'), may hold values from -1 to 1
- weight_up: bfloat16 [2, 512, 2048], P('section'), may hold values from -0.25 to 0.25
- bias_up: float32 [2, 2048], P('section'), may hold values from -1 to 1
- weight_down: bfloat16 [2, 2048, 512], P('section'), may hold values from -0.125 to 0.125
- bias_down: float32 [2, 512], P('section'), may hold values from -1 to 1
Outputs:
- outputs: bfloat16 [2, 32, 1024, 512], P('section', 'dp')
- input_grad: float32 [2, 32, 1024, 512], P('section', 'dp')
- grad_norm1_gain: float32 [2, 512], P('section')
- grad_norm1_bias: float32 [2, 512], P('section')
- grad_weight_qkv: float32 [2, 512, 1536], P('section')
- grad_weight_out: float32 [2, 512, 512], P('section')
- grad_bias_out: float32 [2, 512], P('section')
- grad_norm2_gain: float32 [2, 512], P('section')
- grad_norm2_bias: float32 [2, 512], P('section')
- grad_weight_up: float32 [2, 512, 2048], P('section')
- grad_bias_up: float32 [2, 2048], P('section')
- grad_weight_down: float32 [2, 2048, 512], P('section')
- grad_bias_down: float32 [2, 512], P('section')
The draws below stay inside these ranges and needn't reach their ends.
Inputs may be any that keep to these rules, and one draw needn't show every extreme that they name: Each row of lengths holds 8 span lengths that sum to 1024; the last span of each row is its padded tail.
All inputs are finite; a program needn't handle non-finite values.
Results may differ from the reference program's by a relative error of at most 0.014.
Values may be sent and summed in bfloat16 or wider, within the bound.
A program may use at most 448 MiB of HBM per device.

```python
import math
import jax
import jax.numpy as jnp
import numpy as np
from jax import lax

D = 512
HEADS = 8
HEAD_DIM = 64
FF = 2048
L = 1024
SPANS = 8
MAX_SPAN = 256
ROWS = 32


def shard_levels(rng, shape, cuts, smallest, top_value):
    gain = 1.0
    for axis_at, blocks in cuts:
        heights = jax.random.uniform(jax.random.fold_in(jax.random.fold_in(rng, 6), axis_at), (blocks,), jnp.float32, smallest / len(cuts), top_value / len(cuts))
        gain = gain * jnp.repeat(jnp.exp(heights), shape[axis_at] // blocks).reshape((-1,) + (1,) * (len(shape) - 1 - axis_at))
    return gain


def split_up(amount, total, bound, lean):
    weights = [(1 << 20) // math.isqrt(rank ** lean) + 1 for rank in range(2, amount + 1)]
    surplus, given = total - bound - (amount - 1), [1] * (amount - 1)
    while surplus > 0:
        movable = [i for i in range(amount - 1) if given[i] < bound]
        whole, remaining = sum([weights[i] for i in movable]), surplus
        for i in movable:
            addition = min(bound - given[i], max(1, remaining * weights[i] // whole), surplus)
            given[i] = given[i] + addition
            surplus = surplus - addition
    return np.array([bound] + given)


def uneven(own_key, count, total, bound, slope):
    if count == 2:
        one = jax.random.randint(own_key, (), max(1, total - bound), min(bound, total - 1) + 1)
        return jnp.stack([one, total - one])
    tallies = jnp.asarray(split_up(count, total, bound, slope), jnp.int32)
    couples = (count - 1) // 2
    source_of, taker = tallies[1:1 + 2 * couples:2], tallies[2:2 + 2 * couples:2]
    slack = jnp.minimum(source_of - 1, bound - taker)
    passed = jax.random.randint(jax.random.fold_in(own_key, 1), (couples,), 0, 1 << 20) % (slack + 1)
    tallies = tallies.at[1:1 + 2 * couples:2].set(source_of - passed).at[2:2 + 2 * couples:2].set(taker + passed)
    return tallies[jax.random.permutation(jax.random.fold_in(own_key, 2), count)]


def noise(key, dims, deviation, reach, split=(), held_as=jnp.bfloat16):
    entries = deviation * jax.random.normal(key, dims, jnp.float32)
    if split:
        entries = entries * shard_levels(key, dims, split, -0.22, 0.18)
    return jnp.clip(entries, -reach, reach).astype(held_as)


def setup_inputs(seed: int = 0) -> dict:
    key_of = jax.random.split(jax.random.key(seed), 15)
    return {
        "inputs": noise(key_of[0], (2, ROWS, L, D), 1.0, 6.0, ((0, 2), (1, 16))),
        "cotangent": noise(key_of[1], (2, ROWS, L, D), 1.0, 6.0, ((0, 2), (1, 16))),
        "lengths": jax.vmap(lambda own: uneven(own, SPANS, L, MAX_SPAN, 1))(jax.random.split(key_of[2], ROWS)).reshape((ROWS, SPANS)).astype(jnp.int32),
        "norm1_gain": jnp.clip(1.0 + 0.15 * jax.random.normal(key_of[3], (2, D), jnp.float32), 0.25, 1.75),
        "norm1_bias": noise(key_of[4], (2, D), 0.2, 1.0, ((0, 2),), jnp.float32),
        "weight_qkv": noise(key_of[5], (2, D, 3 * D), D ** -0.5, 0.25, ((0, 2),)),
        "weight_out": noise(key_of[6], (2, D, D), (D // 8) ** -0.5, 0.75, ((0, 2),)),
        "bias_out": noise(key_of[7], (2, D), 0.2, 1.0, ((0, 2),), jnp.float32),
        "norm2_gain": jnp.clip(1.0 + 0.15 * jax.random.normal(key_of[8], (2, D), jnp.float32), 0.25, 1.75),
        "norm2_bias": noise(key_of[9], (2, D), 0.2, 1.0, ((0, 2),), jnp.float32),
        "weight_up": noise(key_of[10], (2, D, FF), D ** -0.5, 0.25, ((0, 2),)),
        "bias_up": noise(key_of[11], (2, FF), 0.2, 1.0, ((0, 2),), jnp.float32),
        "weight_down": noise(key_of[12], (2, FF, D), FF ** -0.5, 0.125, ((0, 2),)),
        "bias_down": noise(key_of[13], (2, D), 0.2, 1.0, ((0, 2),), jnp.float32),
    }


EPSILON = 1e-05
SCORE_SCALE = 0.125
MASKED_SCORE = -1e+30
HIGHEST_PRECISION = lax.Precision.HIGHEST

@jax.custom_vjp
def low(v):
    return lax.optimization_barrier(v.astype(jnp.bfloat16)).astype(jnp.float32)

@jax.custom_vjp
def low_back(v):
    return v

def low_keep(v):
    return (low(v), None)

def low_pass(kept, grad):
    return (grad,)

def back_keep(v):
    return (v, None)

def back_low(kept, grad):
    return (low(grad),)
low.defvjp(low_keep, low_pass)
low_back.defvjp(back_keep, back_low)

def matmul(form, left, right):
    return jnp.einsum(form, left, right, precision=HIGHEST_PRECISION)

def layer_norm(hidden, norm_gain, norm_bias):
    centred = hidden - lax.optimization_barrier(jnp.mean(hidden, -1, keepdims=True))
    scaled = centred * lax.rsqrt(lax.optimization_barrier(jnp.mean(centred * centred, -1, keepdims=True)) + EPSILON)
    return scaled * norm_gain + norm_bias

def segment_ids(lengths):
    ends = jnp.cumsum(lengths, -1).astype(jnp.int32)
    position = jnp.arange(L, dtype=jnp.int32)
    return lax.optimization_barrier(jnp.sum((position[None, :, None] >= ends[:, None, :]).astype(jnp.int32), -1, dtype=jnp.int32))

def layer_row(params, hidden, segments):
    norm1_gain, norm1_bias, weight_qkv, weight_out, bias_out, norm2_gain, norm2_bias, weight_up, bias_up, weight_down, bias_down = params
    first = low(layer_norm(hidden, norm1_gain, norm1_bias))
    projected = low(low_back(matmul('ld,de->le', first, weight_qkv)))
    queries = projected[:, :D].reshape(L, HEADS, HEAD_DIM)
    keys_all = projected[:, D:2 * D].reshape(L, HEADS, HEAD_DIM)
    values_all = projected[:, 2 * D:].reshape(L, HEADS, HEAD_DIM)
    scores = low_back(matmul('qhd,khd->hqk', queries, keys_all) * SCORE_SCALE)
    allowed = segments[:, None] == segments[None, :]
    scores = jnp.where(allowed[None], scores, MASKED_SCORE)
    highest = lax.optimization_barrier(jnp.max(scores, -1, keepdims=True))
    raised = jnp.exp(scores - highest)
    probs = low(raised / lax.optimization_barrier(jnp.sum(raised, -1, keepdims=True)))
    mixed = low(low_back(matmul('hqk,khd->qhd', probs, values_all).reshape(L, D)))
    attended = hidden + low_back(matmul('ld,de->le', mixed, weight_out)) + bias_out
    second = low(layer_norm(attended, norm2_gain, norm2_bias))
    upward = low_back(matmul('ld,df->lf', second, weight_up)) + bias_up
    gelu_out = low(jax.nn.gelu(upward, approximate=True))
    return attended + low_back(matmul('lf,fd->ld', gelu_out, weight_down)) + bias_down

def run_rows(params, hidden_rows, segment_rows):
    row_fn = jax.checkpoint(lambda hidden, segments: layer_row(params, hidden, segments))

    def step(carry, pair):
        return (carry, row_fn(pair[0], pair[1]))
    return lax.scan(step, None, (hidden_rows, segment_rows))[1]

def reference(inputs, cotangent, lengths, norm1_gain, norm1_bias, weight_qkv, weight_out, bias_out, norm2_gain, norm2_bias, weight_up, bias_up, weight_down, bias_down):
    segments = segment_ids(lengths)
    in_text = (segments < SPANS - 1).astype(jnp.float32)[..., None]
    weights = (norm1_gain, norm1_bias, weight_qkv, weight_out, bias_out, norm2_gain, norm2_bias, weight_up, bias_up, weight_down, bias_down)
    enc_params = tuple((weight[0].astype(jnp.float32) for weight in weights))
    den_params = tuple((weight[1].astype(jnp.float32) for weight in weights))

    def forward(enc_weights, den_weights, enc_in, den_in):
        enc_out = run_rows(enc_weights, enc_in, segments)
        den_out = run_rows(den_weights, den_in + low(low_back(enc_out)), segments)
        return (enc_out, den_out)
    (enc_out, den_out), pull = jax.vjp(forward, enc_params, den_params, inputs[0].astype(jnp.float32), inputs[1].astype(jnp.float32))
    enc_grads, den_grads, enc_in_grad, den_in_grad = pull((cotangent[0].astype(jnp.float32) * in_text, cotangent[1].astype(jnp.float32) * in_text))
    stacked = [jnp.stack([first_one, second_one]) for first_one, second_one in zip(enc_grads, den_grads)]
    outputs = jnp.stack([enc_out, den_out]).astype(jnp.bfloat16)
    input_grad = jnp.stack([enc_in_grad, den_in_grad])
    return (outputs, input_grad, stacked[0], stacked[1], stacked[2], stacked[3], stacked[4], stacked[5], stacked[6], stacked[7], stacked[8], stacked[9], stacked[10])
```

```python
import functools

import jax
import jax.numpy as jnp
from jax import lax
from jax.experimental import pallas as pl
from jax.experimental.pallas import tpu as pltpu
from jax.sharding import PartitionSpec as P

EPSILON = 1e-05
GELU_C = 0.7978845608028654
MASKED = -1e30
TILE = 256
CHUNK = 512
BF = jnp.bfloat16
F32 = jnp.float32
MESH = pl.DeviceIdType.MESH
ANY = pl.BlockSpec(memory_space=pl.ANY)
VMEM = pl.BlockSpec(memory_space=pltpu.VMEM)
SMEM = pl.BlockSpec(memory_space=pltpu.SMEM)


def dot(a, b):
    return jnp.dot(a, b, preferred_element_type=F32)


def dot_nt(a, b):
    return lax.dot_general(a, b, (((1,), (1,)), ((), ())), preferred_element_type=F32)


def dot_tn(a, b):
    return lax.dot_general(a, b, (((0,), (0,)), ((), ())), preferred_element_type=F32)


def norm_parts(v):
    centred = v - jnp.mean(v, -1, keepdims=True)
    rstd = lax.rsqrt(jnp.mean(centred * centred, -1, keepdims=True) + EPSILON)
    return centred * rstd, rstd


def norm_pull(grad, hat, rstd, gain):
    scaled = grad * gain
    return rstd * (
        scaled
        - jnp.mean(scaled, -1, keepdims=True)
        - hat * jnp.mean(scaled * hat, -1, keepdims=True)
    )


def colsum(v):
    return jnp.sum(v, 0, keepdims=True)


def stack_pair(block):
    lane = lax.broadcasted_iota(jnp.int32, block.shape, 1)
    zero = jnp.zeros_like(block)
    low = lane < 64
    return jnp.concatenate([jnp.where(low, block, zero), jnp.where(low, zero, block)], 0)


def unstack_pair(both):
    rows = both.shape[0] // 2
    lane = lax.broadcasted_iota(jnp.int32, (rows, 128), 1)
    return jnp.where(lane < 64, both[:rows], both[rows:])


def tile_rows(t):
    return pl.ds(pl.multiple_of(t * TILE, TILE), TILE)


def for_spans(lengths, row, length, run):
    def body(s, first):
        last = first + lengths[row, s]
        base = (first // 16) * 16
        need = last - base

        def case(above, window):
            @pl.when((need > above) & (need <= window))
            def _():
                start = pl.multiple_of(jnp.minimum(base, length - window), 16)
                run(start, first, last, window)

        case(0, 128)
        case(128, 256)
        case(256, 384)
        return last

    lax.fori_loop(0, lengths.shape[1], body, 0)


def pick(pair):
    return pair[0] + lax.axis_index("section") * (pair[1] - pair[0])


def forward_kernel(rows_of, *refs):
    n_alias = len(refs) - 15 - 6 - 13
    (lengths, x_any, arr_any, wqkv_any, wo_any, wu_any, wd_any, n1g, n1b, bo, n2g, n2b, bu, bd) = refs[:14]
    (out_any, proj_any, mixed_any, att_any, up_any, snd_any,
     x, arr, wqkv, wo, wu, wd, proj, mixed, out, att, up, sem_in, sem_out) = refs[len(refs) - 19:]
    row = pick(rows_of)
    T, D = x.shape
    FF = up.shape[1]
    n_tiles = T // TILE
    second_section = lax.axis_index("section") == 1

    @pl.when(row >= 0)
    def _():
        copies = [
            pltpu.make_async_copy(s, d, sem_in.at[k])
            for k, (s, d) in enumerate(
                [(x_any.at[row], x), (wqkv_any, wqkv), (wo_any, wo), (wu_any, wu), (wd_any, wd), (arr_any, arr)]
            )
        ]

        @pl.when(second_section)
        def _():
            copies[5].start()

        for c in copies[:5]:
            c.start()

        @pl.when(second_section)
        def _():
            copies[5].wait()

        @pl.when(jnp.logical_not(second_section))
        def _():
            arr[...] = jnp.zeros_like(arr)

        copies[0].wait()
        copies[1].wait()

        def sends(t, group, pairs):
            rows = tile_rows(t)
            return [pltpu.make_async_copy(s.at[rows], d.at[rows], sem_out.at[group + k, t])
                    for k, (s, d) in enumerate(pairs)]

        pairs_a = [(proj, proj_any.at[row])]
        pairs_b = [(out, out_any.at[row]), (out, snd_any), (att, att_any.at[row]), (up, up_any.at[row])]

        def qkv_tile(t, carry):
            rows = tile_rows(t)
            h = x[rows, :].astype(F32) + arr[rows, :].astype(F32)
            first = (norm_parts(h)[0] * n1g[...] + n1b[...]).astype(BF)
            for c in range(0, 3 * D, CHUNK):
                proj[rows, c:c + CHUNK] = dot(first, wqkv[:, c:c + CHUNK]).astype(BF)
            for c in sends(t, 0, pairs_a):
                c.start()
            return carry

        lax.fori_loop(0, n_tiles, qkv_tile, 0)

        def run(start, first, last, window):
            rows = pl.ds(start, window)
            pos = start + lax.broadcasted_iota(jnp.int32, (1, window), 1)
            kmask = jnp.where((pos >= first) & (pos < last), 0.0, MASKED)
            qpos = start + lax.broadcasted_iota(jnp.int32, (window, 128), 0)
            keep = (qpos >= first) & (qpos < last)
            ones = jnp.ones((window, 128), BF)
            for p in range(D // 128):
                cq = slice(p * 128, p * 128 + 128)
                q = stack_pair(proj[rows, cq] * jnp.asarray(0.125, BF))
                k = proj[rows, D + p * 128:D + p * 128 + 128]
                v = proj[rows, 2 * D + p * 128:2 * D + p * 128 + 128]
                s = dot_nt(q, k) + kmask
                e = jnp.exp(s - jnp.max(s, -1, keepdims=True)).astype(BF)
                o = dot(e, jnp.concatenate([v, ones], 1))
                o = unstack_pair(o[:, :128] / o[:, 128:])
                mixed[rows, cq] = jnp.where(keep, o.astype(BF), mixed[rows, cq])

        for_spans(lengths, row, T, run)
        mixed_out = pltpu.make_async_copy(mixed, mixed_any.at[row], sem_out.at[5, 0])
        mixed_out.start()
        for c in copies[2:5]:
            c.wait()

        def post_tile(t, carry):
            rows = tile_rows(t)
            h = x[rows, :].astype(F32) + arr[rows, :].astype(F32)
            a = h + dot(mixed[rows, :], wo[...]) + bo[...]
            att[rows, :] = a
            second = (norm_parts(a)[0] * n2g[...] + n2b[...]).astype(BF)
            total = a + bd[...]
            for c in range(0, FF, CHUNK):
                u = dot(second, wu[:, c:c + CHUNK]) + bu[:, c:c + CHUNK]
                up[rows, c:c + CHUNK] = u.astype(BF)
                total = total + dot(jax.nn.gelu(u, approximate=True).astype(BF), wd[c:c + CHUNK, :])
            out[rows, :] = total.astype(BF)
            for c in sends(t, 1, pairs_b):
                c.start()
            return carry

        lax.fori_loop(0, n_tiles, post_tile, 0)
        mixed_out.wait()
        for t in range(n_tiles):
            for c in sends(t, 0, pairs_a) + sends(t, 1, pairs_b):
                c.wait()


def forward(rows_of, lengths, x, arr, w, saved):
    n, T, D = x.shape
    FF = w["wu"].shape[1]
    S, V = jax.ShapeDtypeStruct, pltpu.VMEM
    outs = [S((n, T, D), BF), S((n, T, 3 * D), BF), S((n, T, D), BF), S((n, T, D), F32), S((n, T, FF), BF), S((T, D), BF)]
    return pl.pallas_call(
        functools.partial(forward_kernel, rows_of),
        out_shape=outs,
        in_specs=[SMEM] + [ANY] * 6 + [VMEM] * 7 + [ANY] * len(saved),
        out_specs=[ANY] * 6,
        input_output_aliases={14 + i: i for i in range(len(saved))},
        scratch_shapes=[
            V((T, D), BF), V((T, D), BF), V((D, 3 * D), BF), V((D, D), BF), V((D, FF), BF), V((FF, D), BF),
            V((T, 3 * D), BF), V((T, D), BF), V((T, D), BF), V((T, D), F32), V((T, FF), BF),
            pltpu.SemaphoreType.DMA((6,)), pltpu.SemaphoreType.DMA((6, T // TILE)),
        ],
        compiler_params=pltpu.CompilerParams(vmem_limit_bytes=48 * 2**20),
        cost_estimate=pl.CostEstimate(flops=8 * 10**9, bytes_accessed=20 * 2**20, transcendentals=0),
        name="row_forward",
    )(lengths, x, arr, w["wqkv"], w["wo"], w["wu"], w["wd"], w["n1g"], w["n1b"], w["bo"], w["n2g"], w["n2b"],
      w["bu"], w["bd"], *saved)


def backward_kernel(rows_of, *refs):
    (lengths, x_any, arr_any, cot_any, ret_any, proj_any, att_any, up_any,
     wqkv_any, wo_any, wu_any, wd_any, n1g, n1b, n2g, n2b) = refs[:16]
    (dh_any, first_any, dproj_any, al_any, second_any, ul_any, gelu_any, gl_any, snd_any, vec_out,
     x, arr, cot, ret, proj, att, up, wqkv, wo, wu, wd,
     dproj, dmix, da, first, al, second, ul, gl, dh, snd, sem_in, sem_out) = refs[len(refs) - 33:]
    row = pick(rows_of)
    T, D = x.shape
    FF = up.shape[1]
    n_tiles = T // TILE
    second_section = lax.axis_index("section") == 1
    vec_out[...] = jnp.zeros_like(vec_out)

    @pl.when(row >= 0)
    def _():
        def load(k, source, target):
            return pltpu.make_async_copy(source, target, sem_in.at[k])

        def load_up(t):
            return load(t, up_any.at[row, tile_rows(t)], up.at[tile_rows(t)])

        k0 = n_tiles
        c_cot = load(k0, cot_any.at[row], cot)
        c_wd = load(k0 + 1, wd_any, wd)
        c_wu = load(k0 + 2, wu_any, wu)
        c_att = load(k0 + 3, att_any.at[row], att)
        c_wo = load(k0 + 4, wo_any, wo)
        c_proj = load(k0 + 5, proj_any.at[row], proj)
        c_x = load(k0 + 6, x_any.at[row], x)
        c_wqkv = load(k0 + 7, wqkv_any, wqkv)
        c_arr = load(k0 + 8, arr_any, arr)
        c_ret = load(k0 + 9, ret_any, ret)

        @pl.when(jnp.logical_not(second_section))
        def _():
            c_ret.start()

        for c in [c_cot, c_wd, load_up(0), c_wu, c_att, c_wo] + [load_up(t) for t in range(1, n_tiles)]:
            c.start()
        for c in [c_proj, c_wqkv, c_x]:
            c.start()

        @pl.when(second_section)
        def _():
            c_arr.start()
            ret[...] = jnp.zeros_like(ret)

        @pl.when(jnp.logical_not(second_section))
        def _():
            arr[...] = jnp.zeros_like(arr)
            c_ret.wait()

        for c in (c_cot, c_wd, c_wu, c_att, c_wo):
            c.wait()

        def sends(t, group, pairs):
            rows = tile_rows(t)
            return [pltpu.make_async_copy(s.at[rows], d.at[rows], sem_out.at[group + k, t])
                    for k, (s, d) in enumerate(pairs)]

        pairs_a = [(s, d.at[row]) for s, d in
                   [(gl, gl_any), (up, gelu_any), (ul, ul_any), (second, second_any), (al, al_any)]]
        pairs_b = [(first, first_any.at[row]), (dproj, dproj_any.at[row]), (dh, dh_any.at[row]), (snd, snd_any)]
        text_end = T - lengths[row, lengths.shape[1] - 1]

        def pre_tile(t, carry):
            rows = tile_rows(t)
            load_up(t).wait()
            pos = t * TILE + lax.broadcasted_iota(jnp.int32, (TILE, 1), 0)
            in_text = (pos < text_end).astype(F32)
            g = cot[rows, :].astype(F32) * in_text + ret[rows, :].astype(F32)
            g_low = g.astype(BF)
            gl[rows, :] = g_low
            vec_out[5:6, :] += colsum(g)
            sg = jnp.zeros((TILE, D), F32)
            for c in range(0, FF, CHUNK):
                cc = slice(c, c + CHUNK)
                u = up[rows, cc].astype(F32)
                uu = u * u
                th = jnp.tanh(u * (GELU_C + (GELU_C * 0.044715) * uu))
                half = 0.5 * (1.0 + th)
                up[rows, cc] = (u * half).astype(BF)
                slope = half + (0.5 * u) * (1.0 - th * th) * (GELU_C + (3.0 * GELU_C * 0.044715) * uu)
                ug = dot_nt(g_low, wd[cc, :]) * slope
                vec_out[6 + c // CHUNK:7 + c // CHUNK, :] += colsum(ug)
                ug_low = ug.astype(BF)
                ul[rows, cc] = ug_low
                sg = sg + dot_nt(ug_low, wu[:, cc])
            hat, rstd = norm_parts(att[rows, :])
            second[rows, :] = (hat * n2g[...] + n2b[...]).astype(BF)
            vec_out[3:4, :] += colsum(sg * hat)
            vec_out[4:5, :] += colsum(sg)
            a = g + norm_pull(sg, hat, rstd, n2g[...])
            vec_out[2:3, :] += colsum(a)
            da[rows, :] = a
            a_low = a.astype(BF)
            al[rows, :] = a_low
            dmix[rows, :] = dot_nt(a_low, wo[...]).astype(BF)
            for c in sends(t, 0, pairs_a):
                c.start()
            return carry

        lax.fori_loop(0, n_tiles, pre_tile, 0)
        c_proj.wait()

        def run(start, first_pos, last_pos, window):
            rows = pl.ds(start, window)
            pos = start + lax.broadcasted_iota(jnp.int32, (window, 128), 0)
            keep = (pos >= first_pos) & (pos < last_pos)
            kcol = start + lax.broadcasted_iota(jnp.int32, (window, 1), 0)
            kmask = jnp.where((kcol >= first_pos) & (kcol < last_pos), 0.0, MASKED)
            zero = jnp.zeros((window, 128), BF)
            eighth = jnp.asarray(0.125, BF)
            for p in range(D // 128):
                cq = slice(p * 128, p * 128 + 128)
                ck = slice(D + p * 128, D + p * 128 + 128)
                cv = slice(2 * D + p * 128, 2 * D + p * 128 + 128)
                q = stack_pair(proj[rows, cq] * eighth)
                k = proj[rows, ck]
                v = proj[rows, cv]
                do = stack_pair(jnp.where(keep, dmix[rows, cq], zero))
                s = dot_nt(k, q) + kmask
                e = jnp.exp(s - jnp.max(s, 0, keepdims=True))
                prob = e * (1.0 / jnp.sum(e, 0, keepdims=True))
                dp = dot_nt(v, do)
                inner = jnp.sum(dp * prob, 0, keepdims=True)
                ds = (prob * (dp - inner)).astype(BF)
                dv = dot(prob.astype(BF), do)
                dk = dot(ds, q)
                dq = unstack_pair(dot_tn(ds, k * eighth))
                dproj[rows, cq] = jnp.where(keep, dq.astype(BF), dproj[rows, cq])
                dproj[rows, ck] = jnp.where(keep, dk.astype(BF), dproj[rows, ck])
                dproj[rows, cv] = jnp.where(keep, dv.astype(BF), dproj[rows, cv])

        for_spans(lengths, row, T, run)
        c_wqkv.wait()
        c_x.wait()

        @pl.when(second_section)
        def _():
            c_arr.wait()

        def fin_tile(t, carry):
            rows = tile_rows(t)
            fg = dot_nt(dproj[rows, :], wqkv[...])
            hat, rstd = norm_parts(x[rows, :].astype(F32) + arr[rows, :].astype(F32))
            first[rows, :] = (hat * n1g[...] + n1b[...]).astype(BF)
            vec_out[0:1, :] += colsum(fg * hat)
            vec_out[1:2, :] += colsum(fg)
            d = da[rows, :] + norm_pull(fg, hat, rstd, n1g[...])
            dh[rows, :] = d
            snd[rows, :] = d.astype(BF)
            for c in sends(t, 5, pairs_b):
                c.start()
            return carry

        lax.fori_loop(0, n_tiles, fin_tile, 0)
        for t in range(n_tiles):
            for c in sends(t, 0, pairs_a) + sends(t, 5, pairs_b):
                c.wait()


def backward(rows_of, lengths, x, arr, cot, ret, saved, w, kept):
    proj, mixed, att, up = saved
    n, T, D = x.shape
    FF = up.shape[2]
    S, V = jax.ShapeDtypeStruct, pltpu.VMEM
    outs = [
        S((n, T, D), F32), S((n, T, D), BF), S((n, T, 3 * D), BF), S((n, T, D), BF), S((n, T, D), BF),
        S((n, T, FF), BF), S((n, T, FF), BF), S((n, T, D), BF), S((T, D), BF), S((16, CHUNK), F32),
    ]
    return pl.pallas_call(
        functools.partial(backward_kernel, rows_of),
        out_shape=outs,
        in_specs=[SMEM] + [ANY] * 11 + [VMEM] * 4 + [ANY] * len(kept),
        out_specs=[ANY] * 9 + [VMEM],
        input_output_aliases={16 + i: i for i in range(len(kept))},
        scratch_shapes=[
            V((T, D), BF), V((T, D), BF), V((T, D), BF), V((T, D), BF), V((T, 3 * D), BF), V((T, D), F32), V((T, FF), BF),
            V((D, 3 * D), BF), V((D, D), BF), V((D, FF), BF), V((FF, D), BF),
            V((T, 3 * D), BF), V((T, D), BF), V((T, D), F32), V((T, D), BF), V((T, D), BF), V((T, D), BF), V((T, FF), BF),
            V((T, D), BF), V((T, D), F32), V((T, D), BF),
            pltpu.SemaphoreType.DMA((10 + T // TILE,)), pltpu.SemaphoreType.DMA((9, T // TILE)),
        ],
        compiler_params=pltpu.CompilerParams(vmem_limit_bytes=56 * 2**20),
        cost_estimate=pl.CostEstimate(flops=14 * 10**9, bytes_accessed=37 * 2**20, transcendentals=0),
        name="row_backward",
    )(lengths, x, arr, cot, ret, proj, att, up, w["wqkv"], w["wo"], w["wu"], w["wd"], w["n1g"], w["n1b"], w["n2g"],
      w["n2b"], *kept)


def reduce_kernel(n, *refs):
    bits = n.bit_length() - 1
    (gelu_any, gl_any, second_any, ul_any, mixed_any, al_any, first_any, dproj_any, vec_a, vec_b, vec_c) = refs[:11]
    (wd_out, wu_out, wo_out, wqkv_out, vec_out) = refs[11:16]
    left, right, total, final, *rest = refs[16:]
    inbox = rest[:bits]
    (vec_box, stage, vec_tmp, sem_load, sem_store, rs_send, rs_recv, ag_send, ag_recv, vec_send, vec_recv) = rest[bits:]
    n_chunks = total.shape[0]
    FF = gelu_any.shape[2]
    D = gl_any.shape[2]
    T = gl_any.shape[1]
    rows = gl_any.shape[0]
    ff_chunks = FF // CHUNK
    me = lax.axis_index("dp")
    value = [(me // 2**b) % 2 for b in range(bits)]
    partner = [me + (1 - 2 * value[b]) * 2**b for b in range(bits)]
    size = total.shape[1]

    barrier = pltpu.get_barrier_semaphore()
    for b in range(bits):
        pl.semaphore_signal(barrier, inc=1, device_id={"dp": partner[b]}, device_id_type=MESH)
    pl.semaphore_wait(barrier, bits)

    base = [0]
    for b in range(bits):
        base.append(base[-1] + value[b] * (size >> (b + 1)))

    def halve(c, b):
        half = size >> (b + 1)
        away = pl.multiple_of(base[b] + (1 - value[b]) * half, half)
        return pltpu.make_async_remote_copy(
            src_ref=total.at[c, pl.ds(away, half)], dst_ref=inbox[b].at[c],
            send_sem=rs_send.at[c, b], recv_sem=rs_recv.at[c, b],
            device_id={"dp": partner[b]}, device_id_type=MESH,
        )

    def double(c, b):
        half = size >> (b + 1)
        here = final.at[c, pl.ds(pl.multiple_of(base[b + 1], half), half)]
        return pltpu.make_async_remote_copy(
            src_ref=here, dst_ref=here,
            send_sem=ag_send.at[c, b], recv_sem=ag_recv.at[c, b],
            device_id={"dp": partner[b]}, device_id_type=MESH,
        )

    def add_in(c, b):
        half = size >> (b + 1)
        mine = pl.ds(pl.multiple_of(base[b + 1], half), half)
        target = total if b + 1 < bits else final
        target[c, mine, :] = (total[c, mine, :].astype(F32) + inbox[b][c].astype(F32)).astype(BF)

    def load(c, slot, act):
        def both(a, b):
            for k, (source, target) in enumerate(((a, left), (b, right))):
                act(pltpu.make_async_copy(source, target.at[slot], sem_load.at[k, slot]))

        def cols(ref, j):
            return ref.at[:, :, pl.ds(pl.multiple_of(j * CHUNK, CHUNK), CHUNK)]

        @pl.when(c < ff_chunks)
        def _():
            both(cols(gelu_any, c), gl_any)

        @pl.when((c >= ff_chunks) & (c < 2 * ff_chunks))
        def _():
            both(second_any, cols(ul_any, c - ff_chunks))

        @pl.when(c == 2 * ff_chunks)
        def _():
            both(mixed_any, al_any)

        @pl.when((c > 2 * ff_chunks) & (c < n_chunks))
        def _():
            both(first_any, cols(dproj_any, c - 2 * ff_chunks - 1))

    def store(c, slot, act):
        def block(target):
            act(pltpu.make_async_copy(stage.at[slot], target, sem_store.at[slot]))

        def cols(ref, j):
            return ref.at[:, pl.ds(pl.multiple_of(j * CHUNK, CHUNK), CHUNK)]

        @pl.when((c >= 0) & (c < ff_chunks))
        def _():
            block(wd_out.at[pl.ds(pl.multiple_of(c * CHUNK, CHUNK), CHUNK)])

        @pl.when((c >= ff_chunks) & (c < 2 * ff_chunks))
        def _():
            block(cols(wu_out, c - ff_chunks))

        @pl.when(c == 2 * ff_chunks)
        def _():
            block(wo_out)

        @pl.when(c > 2 * ff_chunks)
        def _():
            block(cols(wqkv_out, c - 2 * ff_chunks - 1))

    def vec_copy(b):
        return pltpu.make_async_remote_copy(
            src_ref=vec_tmp.at[b], dst_ref=vec_box.at[b],
            send_sem=vec_send.at[b], recv_sem=vec_recv.at[b],
            device_id={"dp": partner[b]}, device_id_type=MESH,
        )

    vec_tmp[0] = vec_a[...] + vec_b[...] + vec_c[...]
    vec_copy(0).start()
    load(jnp.int32(0), 0, lambda c: c.start())

    def slot_step(t, carry):
        def stage_of(lag, act):
            c = t - lag

            @pl.when((c >= 0) & (c < n_chunks))
            def _():
                act(c)

        def make(c):
            slot = lax.rem(c, 2)
            load(c + 1, 1 - slot, lambda d: d.start())
            load(c, slot, lambda d: d.wait())
            a = left[slot].reshape(rows * T, CHUNK)
            b = right[slot].reshape(rows * T, CHUNK)
            g = dot_tn(a, b).astype(BF)
            total[c, :CHUNK, :] = g[:, :CHUNK // 2]
            total[c, CHUNK:, :] = g[:, CHUNK // 2:]
            halve(c, 0).start()

        def reduce_step(b):
            def act(c):
                halve(c, b).wait()
                add_in(c, b)
                if b + 1 < bits:
                    halve(c, b + 1).start()
                else:
                    double(c, b).start()
            return act

        def gather_step(b):
            def act(c):
                double(c, b).wait()
                double(c, b - 1).start()
            return act

        def finish(c):
            slot = lax.rem(c, 2)
            double(c, 0).wait()

            @pl.when(c >= 2)
            def _():
                store(c - 2, slot, lambda d: d.wait())

            stage[slot, :, :CHUNK // 2] = final[c, :CHUNK, :]
            stage[slot, :, CHUNK // 2:] = final[c, CHUNK:, :]
            store(c, slot, lambda d: d.start())

        stage_of(0, make)
        stage_of(1, reduce_step(0))
        for b in range(bits - 1, 0, -1):
            stage_of(bits + (bits - b), gather_step(b))
        for b in range(1, bits):
            stage_of(1 + b, reduce_step(b))
        stage_of(2 * bits, finish)
        return carry

    lax.fori_loop(0, n_chunks + 2 * bits, slot_step, 0)
    for b in range(bits):
        vec_copy(b).wait()
        merged = vec_tmp[b] + vec_box[b]
        if b + 1 < bits:
            vec_tmp[b + 1] = merged
            vec_copy(b + 1).start()
        else:
            vec_out[...] = merged
    for c in (n_chunks - 2, n_chunks - 1):
        store(jnp.int32(c), c % 2, lambda d: d.wait())


def weight_grads(n, mixed, kept, vecs):
    dh, first, dproj, al, second, ul, gelu, gl = kept
    rows, T, D = gl.shape
    FF = ul.shape[2]
    bits = n.bit_length() - 1
    n_chunks = 2 * (FF // CHUNK) + 1 + 3 * D // CHUNK
    size = CHUNK * 2
    S, V, DMA = jax.ShapeDtypeStruct, pltpu.VMEM, pltpu.SemaphoreType.DMA
    return pl.pallas_call(
        functools.partial(reduce_kernel, n),
        out_shape=[S((FF, D), BF), S((D, FF), BF), S((D, D), BF), S((D, 3 * D), BF), S((16, CHUNK), F32)],
        in_specs=[ANY] * 8 + [VMEM] * 3,
        out_specs=[ANY] * 4 + [VMEM],
        scratch_shapes=[
            V((2, rows, T, CHUNK), BF), V((2, rows, T, CHUNK), BF), V((n_chunks, size, CHUNK // 2), BF),
            V((n_chunks, size, CHUNK // 2), BF),
            *[V((n_chunks, size >> (b + 1), CHUNK // 2), BF) for b in range(bits)],
            V((bits, 16, CHUNK), F32), V((2, CHUNK, CHUNK), BF), V((bits, 16, CHUNK), F32),
            DMA((2, 2)), DMA((2,)), DMA((n_chunks, bits)), DMA((n_chunks, bits)), DMA((n_chunks, bits)),
            DMA((n_chunks, bits)), DMA((bits,)), DMA((bits,)),
        ],
        compiler_params=pltpu.CompilerParams(vmem_limit_bytes=52 * 2**20, collective_id=0, has_side_effects=True),
        cost_estimate=pl.CostEstimate(flops=13 * 10**9, bytes_accessed=60 * 2**20, transcendentals=0),
        name="weight_grads",
    )(gelu, gl, second, ul, mixed, al, first, dproj, *vecs)


NONE = -4


def body(inputs, cotangent, lengths, norm1_gain, norm1_bias, weight_qkv, weight_out, bias_out, norm2_gain, norm2_bias,
         weight_up, bias_up, weight_down, bias_down):
    w = dict(n1g=norm1_gain, n1b=norm1_bias, wqkv=weight_qkv[0], wo=weight_out[0], bo=bias_out, n2g=norm2_gain,
             n2b=norm2_bias, wu=weight_up[0], bu=bias_up, wd=weight_down[0], bd=bias_down)
    x, cot = inputs[0], cotangent[0]
    n = lax.axis_size("dp")

    def ahead(block):
        return lax.ppermute(block, "section", [(0, 1)])

    def back(block):
        return lax.ppermute(block, "section", [(1, 0)])

    *kept_a, send_a = forward((0, NONE), lengths, x, x[0], w, [])
    row_0 = ahead(send_a)
    *kept_b, send_b = forward((1, 0), lengths, x, row_0, w, kept_a)
    row_1 = ahead(send_b)
    *grads_c, send_c, vec_c = backward((NONE, 0), lengths, x, row_0, cot, row_0, kept_b[1:], w, [])
    ret_0 = back(send_c)
    *kept_d, _ = forward((NONE, 1), lengths, x, row_1, w, kept_b)
    outputs, *saved = kept_d
    *grads_e, send_e, vec_e = backward((0, 1), lengths, x, row_1, cot, ret_0, saved, w, grads_c)
    ret_1 = back(send_e)
    *grads_g, _, vec_g = backward((1, NONE), lengths, x, row_1, cot, ret_1, saved, w, grads_e)
    wd, wu, wo, wqkv, vec = weight_grads(n, saved[1], grads_g, (vec_c, vec_e, vec_g))

    def wide(v):
        return v.astype(F32)[None]

    return (outputs[None], grads_g[0][None], vec[0:1], vec[1:2], wide(wqkv), wide(wo), vec[2:3], vec[3:4], vec[4:5],
            wide(wu), vec[6:10].reshape(1, -1), wide(wd), vec[5:6])


def solution(mesh):
    matrix, row = P("section", None, None), P("section", None)
    data = P("section", "dp", None, None)
    return jax.shard_map(
        body,
        mesh=mesh,
        in_specs=(data, data, P("dp", None), row, row, matrix, matrix, row, row, row, matrix, row, matrix, row),
        out_specs=(data, data, row, row, matrix, matrix, row, row, row, matrix, row, matrix, row),
        check_vma=False,
    )
```

```python
import functools

import jax
import jax.numpy as jnp
from jax import lax
from jax.experimental import pallas as pl
from jax.experimental.pallas import tpu as pltpu
from jax.sharding import PartitionSpec as P

EPSILON = 1e-05
GELU_C = 0.7978845608028654
MASKED = -1e30
TILE = 512
CHUNK = 512
NONE = -4
BF = jnp.bfloat16
F32 = jnp.float32
MESH = pl.DeviceIdType.MESH
ANY = pl.BlockSpec(memory_space=pl.ANY)
VMEM = pl.BlockSpec(memory_space=pltpu.VMEM)
SMEM = pl.BlockSpec(memory_space=pltpu.SMEM)


def dot(a, b):
    return jnp.dot(a, b, preferred_element_type=F32)


def dot_nt(a, b):
    return lax.dot_general(a, b, (((1,), (1,)), ((), ())), preferred_element_type=F32)


def dot_tn(a, b):
    return lax.dot_general(a, b, (((0,), (0,)), ((), ())), preferred_element_type=F32)


def norm_parts(v):
    centred = v - jnp.mean(v, -1, keepdims=True)
    rstd = lax.rsqrt(jnp.mean(centred * centred, -1, keepdims=True) + EPSILON)
    return centred * rstd, rstd


def norm_pull(grad, hat, rstd, gain):
    scaled = grad * gain
    return rstd * (
        scaled
        - jnp.mean(scaled, -1, keepdims=True)
        - hat * jnp.mean(scaled * hat, -1, keepdims=True)
    )


def colsum(v):
    return jnp.sum(v, 0, keepdims=True)


def stack_pair(block):
    lane = lax.broadcasted_iota(jnp.int32, block.shape, 1)
    zero = jnp.zeros_like(block)
    low = lane < 64
    return jnp.concatenate([jnp.where(low, block, zero), jnp.where(low, zero, block)], 0)


def unstack_pair(both):
    rows = both.shape[0] // 2
    lane = lax.broadcasted_iota(jnp.int32, (rows, 128), 1)
    return jnp.where(lane < 64, both[:rows], both[rows:])


def tile_rows(t):
    return pl.ds(pl.multiple_of(t * TILE, TILE), TILE)


def for_spans(lengths, row, length, run):
    def body(s, first):
        last = first + lengths[row, s]
        base = (first // 16) * 16
        need = last - base

        def keep_of(window, low, high):
            def keep(width):
                pos = lax.broadcasted_iota(jnp.int32, (window, width), 0)
                return (pos >= low) & (pos < high)

            return keep

        def put(ref, rows, cols, keep, value):
            ref[rows, cols] = jnp.where(keep, value.astype(BF), ref[rows, cols])

        def case(above, window):
            @pl.when((need > above) & (need <= window))
            def _():
                start = pl.multiple_of(jnp.minimum(base, length - window), 16)
                rows = pl.ds(start, window)
                keep = keep_of(window, first - start, last - start)
                run(lambda ref, cols: ref[rows, cols],
                    lambda ref, cols, value: put(ref, rows, cols, keep(128), value), keep, window)

        case(0, 128)
        case(128, 256)

        @pl.when(need > 256)
        def _():
            start = pl.multiple_of(base, 16)
            shift = first - base
            rows = pl.ds(start, 272)

            def load(ref, cols):
                return pltpu.roll(ref[rows, cols].astype(F32), 272 - shift, 0)[:256].astype(BF)

            def store(ref, cols, value):
                wide = jnp.concatenate([value.astype(F32), jnp.zeros((16, value.shape[1]), F32)], 0)
                put(ref, rows, cols, keep_of(272, shift, last - base)(128), pltpu.roll(wide, shift, 0))

            run(load, store, keep_of(256, 0, last - first), 256)

        return last

    lax.fori_loop(0, lengths.shape[1], body, 0)


def pick(pair):
    return pair[0] + lax.axis_index("section") * (pair[1] - pair[0])


def row_kernel(f_rows, b_rows, names, *refs):
    r = dict(zip(names, refs))
    lengths = r["lengths"]
    fused = b_rows[1] >= 0
    both = f_rows[0] >= 0 and f_rows[1] >= 0
    with_arr = f_rows[1] >= 0
    v_x = r["v_x"]
    T, D = v_x.shape
    FF = r["w_up"].shape[1]
    n_tiles = T // TILE
    sem_in, sem_out = r["sem_in"], r["sem_out"]
    section = lax.axis_index("section")
    v_proj, v_att, v_up = r["v_proj"], r["v_att"], r["v_up"]
    w_qkv, w_out, w_up, w_down = r["w_qkv"], r["w_out"], r["w_up"], r["w_down"]
    ins, outs = {}, {}

    def load(key, source, target):
        k = ins.setdefault(key, len(ins))
        return pltpu.make_async_copy(source, target, sem_in.at[k])

    def load_tile(key, source, target, t):
        return load((key, t), source.at[tile_rows(t)], target.at[tile_rows(t)])

    def sends(t, pairs):
        rows = tile_rows(t)
        copies = []
        for key, source, target in pairs:
            k = outs.setdefault(key, len(outs))
            copies.append(pltpu.make_async_copy(source.at[rows], target.at[rows], sem_out.at[k, t]))
        return copies

    if "vec" in r:
        r["vec"][...] = jnp.zeros_like(r["vec"])

    def hidden(rows):
        h = v_x[rows, :].astype(F32)
        return h + r["v_arr"][rows, :].astype(F32) if with_arr else h

    def forward(row):
        c_x = [load_tile("x", r["x"].at[row], v_x, t) for t in range(n_tiles)]
        c_qkv = load("wqkv", r["wqkv"], w_qkv)
        later = [load("wo", r["wo"], w_out), load("wu", r["wu"], w_up), load("wd", r["wd"], w_down)]
        for c in c_x + [c_qkv]:
            c.start()
        if with_arr:
            c_arr = [load_tile("arr", r["arr"], r["v_arr"], t) for t in range(n_tiles)]

            @pl.when(section == 1)
            def _():
                for c in c_arr:
                    c.start()

            if both:
                @pl.when(section == 0)
                def _():
                    r["v_arr"][...] = jnp.zeros_like(r["v_arr"])
        for c in later:
            c.start()
        if fused:
            @pl.when(section == 1)
            def _():
                for t in range(n_tiles):
                    load_tile("cot", r["cot"].at[row], r["v_cot"], t).start()
        v_mixed = r["v_mixed"]
        pairs_a = [("proj", v_proj, r["proj"].at[row])] if f_rows[0] >= 0 else []
        pairs_b = [("out", r["v_out"], r["out"].at[row])]
        pairs_c = []
        if f_rows[0] >= 0:
            pairs_c = [("snd", r["v_out"], r["snd"]), ("att", v_att, r["att"].at[row]), ("up", v_up, r["up"].at[row])]

        def keep_for_encoder(t, pairs, act):
            if pairs:
                @pl.when(section == 0)
                def _():
                    for c in sends(t, pairs):
                        act(c)

        for t in range(n_tiles):
            c_x[t].wait()
            if with_arr:
                @pl.when(section == 1)
                def _():
                    c_arr[t].wait()
            if t == 0:
                c_qkv.wait()
            rows = pl.ds(t * TILE, TILE)
            first = (norm_parts(hidden(rows))[0] * r["n1g"][...] + r["n1b"][...]).astype(BF)
            v_proj[rows, :] = dot(first, w_qkv[...]).astype(BF)
            keep_for_encoder(t, pairs_a, lambda c: c.start())

        def run(load, store, keep, window):
            kmask = jnp.where(keep(128), 0.0, MASKED)
            pairs = range(D // 128)
            q = [stack_pair(load(v_proj, slice(p * 128, p * 128 + 128)) * jnp.asarray(0.125, BF)) for p in pairs]
            k = [load(v_proj, slice(D + p * 128, D + p * 128 + 128)) for p in pairs]
            v = [load(v_proj, slice(2 * D + p * 128, 2 * D + p * 128 + 128)) for p in pairs]
            score = [dot_nt(k[p], q[p]) for p in pairs]
            raised, sums = [], []
            for p in pairs:
                parts = []
                for j in range(0, 2 * window, 128):
                    block = score[p][:, j:j + 128] + kmask
                    e = jnp.exp(block - jnp.max(block, 0, keepdims=True))
                    sums.append(jnp.sum(e, 0, keepdims=True))
                    parts.append(e.astype(BF))
                raised.append(jnp.concatenate(parts, 1))
            outs = [dot_tn(v[p], raised[p]) for p in pairs]
            blocks = 2 * window // 128
            for p in pairs:
                o = outs[p] * (1.0 / jnp.concatenate(sums[p * blocks:(p + 1) * blocks], 1))
                o = jnp.concatenate([o[:64, :window], o[64:, window:]], 0).T
                store(v_mixed, slice(p * 128, p * 128 + 128), o)

        for_spans(lengths, row, T, run)
        c_mixed = pltpu.make_async_copy(v_mixed, r["mixed"].at[row], r["sem_mixed"].at[0])
        c_mixed.start()
        for c in later:
            c.wait()

        def post_tile(t, carry):
            rows = tile_rows(t)
            a = hidden(rows) + dot(v_mixed[rows, :], w_out[...]) + r["bo"][...]
            v_att[rows, :] = a
            second = (norm_parts(a)[0] * r["n2g"][...] + r["n2b"][...]).astype(BF)
            u = dot(second, w_up[...]) + r["bu"][...]
            v_up[rows, :] = u.astype(BF)
            g = jax.nn.gelu(u, approximate=True).astype(BF)
            r["v_out"][rows, :] = (a + r["bd"][...] + dot(g, w_down[...])).astype(BF)
            for c in sends(t, pairs_b):
                c.start()
            keep_for_encoder(t, pairs_c, lambda c: c.start())
            return carry

        lax.fori_loop(0, n_tiles, post_tile, 0)

        def finish():
            c_mixed.wait()
            for t in range(n_tiles):
                for c in sends(t, pairs_b):
                    c.wait()
                keep_for_encoder(t, pairs_a + pairs_c, lambda c: c.wait())

        return finish

    def backward(row):
        v_cot, v_gl, v_ul, v_second, v_al = [r["v_" + k] for k in ("cot", "gl", "ul", "second", "al")]
        v_da, v_dmix, v_dproj, v_first, v_dh, vec = [r[k] for k in ("v_da", "v_dmix", "v_dproj", "v_first", "v_dh", "vec")]
        if not fused:
            c_wd = load("wd", r["wd"], w_down)
            c_wu = load("wu", r["wu"], w_up)
            c_wo = load("wo", r["wo"], w_out)
            c_att = load("att", r["att"].at[row], v_att)
            late = [load("proj", r["proj"].at[row], v_proj), load("wqkv", r["wqkv"], w_qkv), load("x", r["x"].at[row], v_x)]

            def tile_loads(t):
                return [load_tile("cot", r["cot"].at[row], v_cot, t), load_tile("ret", r["ret"], r["v_ret"], t),
                        load_tile("up", r["up"].at[row], v_up, t)]

            for c in tile_loads(0) + [c_wd, c_wu, c_att, c_wo]:
                c.start()
            for t in range(1, n_tiles):
                for c in tile_loads(t):
                    c.start()
            for c in late:
                c.start()

        pairs_a = [("gl", v_gl, r["gl"].at[row]), ("gelu", v_up, r["gelu"].at[row]), ("ul", v_ul, r["ul"].at[row]),
                   ("second", v_second, r["second"].at[row]), ("al", v_al, r["al"].at[row])]
        pairs_b = [("first", v_first, r["first"].at[row]), ("dproj", v_dproj, r["dproj"].at[row]),
                   ("dh", v_dh, r["dh"].at[row])]
        if fused:
            pairs_b.append(("bsnd", r["v_bsnd"], r["bsnd"]))
        text_end = T - lengths[row, lengths.shape[1] - 1]

        def pre_tile(t):
            rows = pl.ds(t * TILE, TILE)
            if fused:
                load_tile("cot", r["cot"].at[row], v_cot, t).wait()
            else:
                for c in tile_loads(t):
                    c.wait()
                if t == 0:
                    c_wd.wait()
            pos = t * TILE + lax.broadcasted_iota(jnp.int32, (TILE, 1), 0)
            in_text = (pos < text_end).astype(F32)
            g = v_cot[rows, :].astype(F32) * in_text
            if not fused:
                g = g + r["v_ret"][rows, :].astype(F32)
            g_low = g.astype(BF)
            v_gl[rows, :] = g_low
            vec[5:6, :] += colsum(g)
            sg = jnp.zeros((TILE, D), F32)
            for c in range(0, FF, CHUNK):
                cc = slice(c, c + CHUNK)
                u = v_up[rows, cc].astype(F32)
                uu = u * u
                th = jnp.tanh(u * (GELU_C + (GELU_C * 0.044715) * uu))
                half = 0.5 * (1.0 + th)
                v_up[rows, cc] = (u * half).astype(BF)
                slope = half + (0.5 * u) * (1.0 - th * th) * (GELU_C + (3.0 * GELU_C * 0.044715) * uu)
                ug = dot_nt(g_low, w_down[cc, :]) * slope
                vec[6 + c // CHUNK:7 + c // CHUNK, :] += colsum(ug)
                ug_low = ug.astype(BF)
                v_ul[rows, cc] = ug_low
                if not fused and t == 0 and c == 0:
                    c_wu.wait()
                sg = sg + dot_nt(ug_low, w_up[:, cc])
            if not fused and t == 0:
                c_att.wait()
                c_wo.wait()
            hat, rstd = norm_parts(v_att[rows, :])
            v_second[rows, :] = (hat * r["n2g"][...] + r["n2b"][...]).astype(BF)
            vec[3:4, :] += colsum(sg * hat)
            vec[4:5, :] += colsum(sg)
            a = g + norm_pull(sg, hat, rstd, r["n2g"][...])
            vec[2:3, :] += colsum(a)
            v_da[rows, :] = a
            a_low = a.astype(BF)
            v_al[rows, :] = a_low
            v_dmix[rows, :] = dot_nt(a_low, w_out[...]).astype(BF)
            for c in sends(t, pairs_a):
                c.start()

        for t in range(n_tiles):
            pre_tile(t)
        if not fused:
            late[0].wait()

        def run(load, store, keep, window):
            kmask = jnp.where(keep(128), 0.0, MASKED)
            inside = keep(128)
            zero = jnp.zeros((window, 128), BF)
            eighth = jnp.asarray(0.125, BF)
            pairs = range(D // 128)

            def cols(third, p):
                return slice(third * D + p * 128, third * D + p * 128 + 128)

            q = [stack_pair(load(v_proj, cols(0, p)) * eighth) for p in pairs]
            k = [load(v_proj, cols(1, p)) for p in pairs]
            v = [load(v_proj, cols(2, p)) for p in pairs]
            do = [stack_pair(jnp.where(inside, load(v_dmix, cols(0, p)), zero)) for p in pairs]
            score = [dot_nt(k[p], q[p]) for p in pairs]
            pulls = [dot_nt(v[p], do[p]) for p in pairs]
            def soft(p):
                prob_parts, ds_parts = [], []
                for j in range(0, 2 * window, 128):
                    block = score[p][:, j:j + 128] + kmask
                    e = jnp.exp(block - jnp.max(block, 0, keepdims=True))
                    prob = e * (1.0 / jnp.sum(e, 0, keepdims=True))
                    pull = pulls[p][:, j:j + 128]
                    inner = jnp.sum(pull * prob, 0, keepdims=True)
                    ds_parts.append((prob * (pull - inner)).astype(BF))
                    prob_parts.append(prob.astype(BF))
                return jnp.concatenate(prob_parts, 1), jnp.concatenate(ds_parts, 1)

            def mix(p, prob, push):
                store(v_dproj, cols(2, p), dot(prob, do[p]))
                store(v_dproj, cols(1, p), dot(push, q[p]))
                dq = dot_tn(k[p] * eighth, push)
                store(v_dproj, cols(0, p), jnp.concatenate([dq[:64, :window], dq[64:, window:]], 0).T)

            ahead = soft(0)
            for p in pairs:
                now = ahead
                if p + 1 < len(pairs):
                    ahead = soft(p + 1)
                mix(p, *now)

        for_spans(lengths, row, T, run)
        if not fused:
            late[1].wait()
            late[2].wait()

        def fin_tile(t, carry):
            rows = tile_rows(t)
            fg = dot_nt(v_dproj[rows, :], w_qkv[...])
            hat, rstd = norm_parts(hidden(rows))
            v_first[rows, :] = (hat * r["n1g"][...] + r["n1b"][...]).astype(BF)
            vec[0:1, :] += colsum(fg * hat)
            vec[1:2, :] += colsum(fg)
            d = v_da[rows, :] + norm_pull(fg, hat, rstd, r["n1g"][...])
            v_dh[rows, :] = d
            if fused:
                r["v_bsnd"][rows, :] = d.astype(BF)
            for c in sends(t, pairs_b):
                c.start()
            return carry

        lax.fori_loop(0, n_tiles, fin_tile, 0)
        for t in range(n_tiles):
            for c in sends(t, pairs_a) + sends(t, pairs_b):
                c.wait()

    if f_rows != (NONE, NONE):
        f_row = pick(f_rows)

        @pl.when(f_row >= 0)
        def _():
            finish = forward(f_row)
            if fused:
                @pl.when(section == 1)
                def _():
                    backward(f_row)
            finish()
    else:
        b_row = pick(b_rows)

        @pl.when(b_row >= 0)
        def _():
            backward(b_row)


def row_slot(f_rows, b_rows, lengths, x, cot, arr, ret, w, bufs):
    n, T, D = x.shape
    FF = w["wu"].shape[1]
    S, V = jax.ShapeDtypeStruct, pltpu.VMEM
    does_f, does_b = max(f_rows) >= 0, max(b_rows) >= 0
    saves = f_rows[0] >= 0
    fused = b_rows[1] >= 0
    ins = {"lengths": (lengths, SMEM), "x": (x, ANY)}
    if does_b:
        ins["cot"] = (cot, ANY)
    if arr is not None:
        ins["arr"] = (arr, ANY)
    if ret is not None:
        ins["ret"] = (ret, ANY)
        ins.update({k: (bufs[k], ANY) for k in ("proj", "att", "up")})
    ins.update({k: (w[k], ANY) for k in ("wqkv", "wo", "wu", "wd")})
    ins.update({k: (w[k], VMEM) for k in ("n1g", "n1b", "bo", "n2g", "n2b", "bu", "bd")})
    wide = {"out": (D, BF), "mixed": (D, BF), "proj": (3 * D, BF), "att": (D, F32), "up": (FF, BF), "dh": (D, F32),
            "first": (D, BF), "dproj": (3 * D, BF), "al": (D, BF), "second": (D, BF), "ul": (FF, BF), "gelu": (FF, BF),
            "gl": (D, BF)}
    keys = (["out", "mixed"] if does_f else []) + (["proj", "att", "up"] if saves else [])
    if does_b:
        keys += ["dh", "first", "dproj", "al", "second", "ul", "gelu", "gl"]
    outs = {k: (S((n, T, wide[k][0]), wide[k][1]), ANY) for k in keys}
    if saves:
        outs["snd"] = (S((T, D), BF), ANY)
    if fused:
        outs["bsnd"] = (S((T, D), BF), ANY)
    if does_b:
        outs["vec"] = (S((16, CHUNK), F32), VMEM)
    alias = [k for k in keys if k in bufs]
    scratch = {"v_x": V((T, D), BF), "w_qkv": V((D, 3 * D), BF), "w_out": V((D, D), BF), "w_up": V((D, FF), BF),
               "w_down": V((FF, D), BF), "v_proj": V((T, 3 * D), BF), "v_att": V((T, D), F32), "v_up": V((T, FF), BF)}
    if arr is not None:
        scratch["v_arr"] = V((T, D), BF)
    if ret is not None:
        scratch["v_ret"] = V((T, D), BF)
    if does_f:
        scratch.update({"v_mixed": V((T, D), BF), "v_out": V((T, D), BF)})
    if does_b:
        scratch.update({"v_" + k: V((T, wide[k][0]), wide[k][1])
                        for k in ("dh", "first", "dproj", "al", "second", "ul", "gl")})
        scratch.update({"v_cot": V((T, D), BF), "v_dmix": V((T, D), BF), "v_da": V((T, D), F32)})
    if fused:
        scratch["v_bsnd"] = V((T, D), BF)
    scratch.update({"sem_in": pltpu.SemaphoreType.DMA((24,)), "sem_out": pltpu.SemaphoreType.DMA((18, T // TILE)),
                    "sem_mixed": pltpu.SemaphoreType.DMA((1,))})
    names = list(ins) + ["alias_" + k for k in alias] + list(outs) + list(scratch)
    values = [v for v, _ in ins.values()] + [bufs[k] for k in alias]
    results = pl.pallas_call(
        functools.partial(row_kernel, f_rows, b_rows, names),
        out_shape=[o for o, _ in outs.values()],
        in_specs=[m for _, m in ins.values()] + [ANY] * len(alias),
        out_specs=[m for _, m in outs.values()],
        input_output_aliases={len(ins) + i: list(outs).index(k) for i, k in enumerate(alias)},
        scratch_shapes=list(scratch.values()),
        compiler_params=pltpu.CompilerParams(vmem_limit_bytes=58 * 2**20),
        cost_estimate=pl.CostEstimate(flops=8 * 10**9 * does_f + 14 * 10**9 * does_b, bytes_accessed=20 * 2**20,
                                      transcendentals=0),
        name="row_" + "f" * does_f + "b" * does_b,
    )(*values)
    got = dict(zip(outs, results))
    send = (got.get("snd"), got.get("bsnd"))
    if None in send:
        send = send[0] if send[1] is None else send[1]
    return {**bufs, **{k: got[k] for k in keys}}, send, got.get("vec")


def reduce_kernel(n, *refs):
    bits = n.bit_length() - 1
    (gelu_any, gl_any, second_any, ul_any, mixed_any, al_any, first_any, dproj_any, vec_a, vec_b, vec_c, vec_d) = refs[:12]
    (wd_out, wu_out, wo_out, wqkv_out, vec_out) = refs[12:17]
    left, right, total, final, *rest = refs[17:]
    inbox = rest[:bits]
    (vec_box, vec_tmp, sem_load, sem_store, rs_send, rs_recv, ag_send, ag_recv, vec_send, vec_recv) = rest[bits:]
    n_chunks = total.shape[0]
    FF = gelu_any.shape[2]
    D = gl_any.shape[2]
    T = gl_any.shape[1]
    rows = gl_any.shape[0]
    ff_chunks = FF // CHUNK
    me = lax.axis_index("dp")
    size = total.shape[1]
    value = [(me // 2**b) % 2 for b in range(bits)]
    partner = [me + (1 - 2 * value[b]) * 2**b for b in range(bits)]
    base = [sum(value[i] * (size >> (i + 1)) for i in range(b)) for b in range(bits + 1)]

    barrier = pltpu.get_barrier_semaphore()
    for b in range(bits):
        pl.semaphore_signal(barrier, inc=1, device_id={"dp": partner[b]}, device_id_type=MESH)
    pl.semaphore_wait(barrier, bits)

    def halve(c, b):
        half = size >> (b + 1)
        away = pl.multiple_of(base[b] + (1 - value[b]) * half, half)
        return pltpu.make_async_remote_copy(
            src_ref=total.at[c, pl.ds(away, half)], dst_ref=inbox[b].at[c],
            send_sem=rs_send.at[c, b], recv_sem=rs_recv.at[c, b],
            device_id={"dp": partner[b]}, device_id_type=MESH,
        )

    def double(c, b):
        half = size >> (b + 1)
        here = final.at[c, pl.ds(pl.multiple_of(base[b + 1], half), half)]
        return pltpu.make_async_remote_copy(
            src_ref=here, dst_ref=here,
            send_sem=ag_send.at[c, b], recv_sem=ag_recv.at[c, b],
            device_id={"dp": partner[b]}, device_id_type=MESH,
        )

    def add_in(c, b):
        half = size >> (b + 1)
        mine = pl.ds(pl.multiple_of(base[b + 1], half), half)
        target = total if b + 1 < bits else final
        target[c, mine, :] = (total[c, mine, :].astype(F32) + inbox[b][c].astype(F32)).astype(BF)

    def load(c, slot, act):
        def both(a, b):
            for k, (source, target) in enumerate(((a, left), (b, right))):
                act(pltpu.make_async_copy(source, target.at[slot], sem_load.at[k, slot]))

        def cols(ref, j):
            return ref.at[:, :, pl.ds(pl.multiple_of(j * CHUNK, CHUNK), CHUNK)]

        @pl.when(c < ff_chunks)
        def _():
            both(cols(gelu_any, c), gl_any)

        @pl.when((c >= ff_chunks) & (c < 2 * ff_chunks))
        def _():
            both(second_any, cols(ul_any, c - ff_chunks))

        @pl.when(c == 2 * ff_chunks)
        def _():
            both(mixed_any, al_any)

        @pl.when((c > 2 * ff_chunks) & (c < n_chunks))
        def _():
            both(first_any, cols(dproj_any, c - 2 * ff_chunks - 1))

    def store(c, act):
        def block(target):
            act(pltpu.make_async_copy(final.at[c], target, sem_store.at[c]))

        def cols(ref, j):
            return ref.at[:, pl.ds(pl.multiple_of(j * CHUNK, CHUNK), CHUNK)]

        @pl.when((c >= 0) & (c < ff_chunks))
        def _():
            block(wd_out.at[pl.ds(pl.multiple_of(c * CHUNK, CHUNK), CHUNK)])

        @pl.when((c >= ff_chunks) & (c < 2 * ff_chunks))
        def _():
            block(cols(wu_out, c - ff_chunks))

        @pl.when(c == 2 * ff_chunks)
        def _():
            block(wo_out)

        @pl.when(c > 2 * ff_chunks)
        def _():
            block(cols(wqkv_out, c - 2 * ff_chunks - 1))

    def vec_copy(b):
        return pltpu.make_async_remote_copy(
            src_ref=vec_tmp.at[b], dst_ref=vec_box.at[b],
            send_sem=vec_send.at[b], recv_sem=vec_recv.at[b],
            device_id={"dp": partner[b]}, device_id_type=MESH,
        )

    vec_tmp[0] = vec_a[...] + vec_b[...] + vec_c[...] + vec_d[...]
    vec_copy(0).start()
    load(jnp.int32(0), 0, lambda c: c.start())

    gaps = [1, 2] + [1 + b % 2 for b in range(2, bits)]
    lags = [0]
    for gap in gaps[:bits] + gaps[bits - 1::-1]:
        lags.append(lags[-1] + gap)

    def slot_step(t, carry):
        def stage_of(lag, act):
            c = t - lag

            @pl.when((c >= 0) & (c < n_chunks))
            def _():
                act(c)

        def make(c):
            slot = lax.rem(c, 2)
            load(c + 1, 1 - slot, lambda d: d.start())
            load(c, slot, lambda d: d.wait())
            a = left[slot].reshape(rows * T, CHUNK)
            b = right[slot].reshape(rows * T, CHUNK)
            total[c] = dot_tn(a, b).astype(BF)
            halve(c, 0).start()

        def reduce_step(b):
            def act(c):
                halve(c, b).wait()
                add_in(c, b)
                if b + 1 < bits:
                    halve(c, b + 1).start()
                else:
                    double(c, b).start()
            return act

        def gather_step(b):
            def act(c):
                double(c, b).wait()
                double(c, b - 1).start()
            return act

        def finish(c):
            double(c, 0).wait()
            store(c, lambda d: d.start())

        acts = [make] + [reduce_step(b) for b in range(bits)] + [gather_step(b) for b in range(bits - 1, 0, -1)] + [finish]
        for lag, act in zip(lags, acts):
            stage_of(lag, act)
        return carry

    lax.fori_loop(0, n_chunks + lags[-1], slot_step, 0)
    for b in range(bits):
        vec_copy(b).wait()
        merged = vec_tmp[b] + vec_box[b]
        if b + 1 < bits:
            vec_tmp[b + 1] = merged
            vec_copy(b + 1).start()
        else:
            vec_out[...] = merged
    for c in range(n_chunks):
        store(jnp.int32(c), lambda d: d.wait())


def weight_grads(n, bufs, vecs):
    gl, ul = bufs["gl"], bufs["ul"]
    rows, T, D = gl.shape
    FF = ul.shape[2]
    bits = n.bit_length() - 1
    n_chunks = 2 * (FF // CHUNK) + 1 + 3 * D // CHUNK
    size = CHUNK
    S, V, DMA = jax.ShapeDtypeStruct, pltpu.VMEM, pltpu.SemaphoreType.DMA
    return pl.pallas_call(
        functools.partial(reduce_kernel, n),
        out_shape=[S((FF, D), BF), S((D, FF), BF), S((D, D), BF), S((D, 3 * D), BF), S((16, CHUNK), F32)],
        in_specs=[ANY] * 8 + [VMEM] * 4,
        out_specs=[ANY] * 4 + [VMEM],
        scratch_shapes=[
            V((2, rows, T, CHUNK), BF), V((2, rows, T, CHUNK), BF), V((n_chunks, size, CHUNK), BF),
            V((n_chunks, size, CHUNK), BF),
            *[V((n_chunks, size >> (b + 1), CHUNK), BF) for b in range(bits)],
            V((bits, 16, CHUNK), F32), V((bits, 16, CHUNK), F32),
            DMA((2, 2)), DMA((n_chunks,)), DMA((n_chunks, bits)), DMA((n_chunks, bits)), DMA((n_chunks, bits)),
            DMA((n_chunks, bits)), DMA((bits,)), DMA((bits,)),
        ],
        compiler_params=pltpu.CompilerParams(vmem_limit_bytes=52 * 2**20, collective_id=0, has_side_effects=True),
        cost_estimate=pl.CostEstimate(flops=13 * 10**9, bytes_accessed=60 * 2**20, transcendentals=0),
        name="weight_grads",
    )(*[bufs[k] for k in ("gelu", "gl", "second", "ul", "mixed", "al", "first", "dproj")], *vecs)


def body(inputs, cotangent, lengths, norm1_gain, norm1_bias, weight_qkv, weight_out, bias_out, norm2_gain, norm2_bias,
         weight_up, bias_up, weight_down, bias_down):
    w = dict(n1g=norm1_gain, n1b=norm1_bias, wqkv=weight_qkv[0], wo=weight_out[0], bo=bias_out, n2g=norm2_gain,
             n2b=norm2_bias, wu=weight_up[0], bu=bias_up, wd=weight_down[0], bd=bias_down)
    x, cot = inputs[0], cotangent[0]
    n = lax.axis_size("dp")

    def ahead(block):
        return lax.ppermute(block, "section", [(0, 1)])

    def back(block):
        return lax.ppermute(block, "section", [(1, 0)])

    bufs, send_a, _ = row_slot((0, NONE), (NONE, NONE), lengths, x, cot, None, None, w, {})
    row_0 = ahead(send_a)
    bufs, (send_b, back_b), vec_b = row_slot((1, 0), (NONE, 0), lengths, x, cot, row_0, None, w, bufs)
    row_1 = ahead(send_b)
    ret_0 = back(back_b)
    bufs, back_d, vec_d = row_slot((NONE, 1), (NONE, 1), lengths, x, cot, row_1, None, w, bufs)
    ret_1 = back(back_d)
    bufs, _, vec_e = row_slot((NONE, NONE), (0, NONE), lengths, x, cot, None, ret_0, w, bufs)
    bufs, _, vec_g = row_slot((NONE, NONE), (1, NONE), lengths, x, cot, None, ret_1, w, bufs)
    wd, wu, wo, wqkv, vec = weight_grads(n, bufs, (vec_b, vec_d, vec_e, vec_g))

    def wide(v):
        return v.astype(F32)[None]

    return (bufs["out"][None], bufs["dh"][None], vec[0:1], vec[1:2], wide(wqkv), wide(wo), vec[2:3], vec[3:4], vec[4:5],
            wide(wu), vec[6:10].reshape(1, -1), wide(wd), vec[5:6])


def solution(mesh):
    matrix, row = P("section", None, None), P("section", None)
    data = P("section", "dp", None, None)
    return jax.shard_map(
        body,
        mesh=mesh,
        in_specs=(data, data, P("dp", None), row, row, matrix, matrix, row, row, row, matrix, row, matrix, row),
        out_specs=(data, data, row, row, matrix, matrix, row, row, row, matrix, row, matrix, row),
        check_vma=False,
    )
```

```python
import functools

import jax
import jax.numpy as jnp
from jax import lax
from jax.experimental import pallas as pl
from jax.experimental.pallas import tpu as pltpu
from jax.sharding import PartitionSpec as P

EPSILON = 1e-05
GELU_C = 0.7978845608028654
MASKED = -1e30
TILE = 512
CHUNK = 512
JOIN = 3
NONE = -4
BF = jnp.bfloat16
F32 = jnp.float32
MESH = pl.DeviceIdType.MESH
ANY = pl.BlockSpec(memory_space=pl.ANY)
VMEM = pl.BlockSpec(memory_space=pltpu.VMEM)
SMEM = pl.BlockSpec(memory_space=pltpu.SMEM)


def dot(a, b):
    return jnp.dot(a, b, preferred_element_type=F32)


def dot_nt(a, b):
    return lax.dot_general(a, b, (((1,), (1,)), ((), ())), preferred_element_type=F32)


def dot_tn(a, b):
    return lax.dot_general(a, b, (((0,), (0,)), ((), ())), preferred_element_type=F32)


def norm_parts(v):
    centred = v - jnp.mean(v, -1, keepdims=True)
    rstd = lax.rsqrt(jnp.mean(centred * centred, -1, keepdims=True) + EPSILON)
    return centred * rstd, rstd


def norm_pull(grad, hat, rstd, gain):
    scaled = grad * gain
    return rstd * (
        scaled
        - jnp.mean(scaled, -1, keepdims=True)
        - hat * jnp.mean(scaled * hat, -1, keepdims=True)
    )


def colsum(v):
    return jnp.sum(v, 0, keepdims=True)


def stack_pair(block):
    lane = lax.broadcasted_iota(jnp.int32, block.shape, 1)
    zero = jnp.zeros_like(block)
    low = lane < 64
    return jnp.concatenate([jnp.where(low, block, zero), jnp.where(low, zero, block)], 0)


def unstack_pair(both):
    rows = both.shape[0] // 2
    lane = lax.broadcasted_iota(jnp.int32, (rows, 128), 1)
    return jnp.where(lane < 64, both[:rows], both[rows:])


def mask_lanes(keep, window):
    lane = lax.broadcasted_iota(jnp.int32, (window, 128), 1)
    mask = jnp.where(keep(128) | (lane > 0), 0.0, MASKED).astype(BF)
    one = jnp.where(lax.broadcasted_iota(jnp.int32, (2 * window, 128), 1) == 0, 1.0, 0.0).astype(BF)
    return mask, one


def tile_rows(t):
    return pl.ds(pl.multiple_of(t * TILE, TILE), TILE)


def for_spans(lengths, row, length, spots, run):
    n_spans = lengths.shape[1]

    def keep_of(window, low, high):
        def keep(width):
            pos = lax.broadcasted_iota(jnp.int32, (window, width), 0)
            return (pos >= low) & (pos < high)

        return keep

    def put(ref, rows, cols, keep, value):
        ref[rows, cols] = jnp.where(keep, value.astype(BF), ref[rows, cols])

    def view(s, first, last, window):
        start = pl.multiple_of(jnp.minimum((first // 16) * 16, length - window), 16)
        rows = pl.ds(start, window)
        keep = keep_of(window, first - start, last - start)
        return (s, lambda ref, cols: ref[rows, cols],
                lambda ref, cols, value: put(ref, rows, cols, keep(128), value), keep)

    def moved_view(s, first, last):
        start = pl.multiple_of((first // 16) * 16, 16)
        shift = first - start
        rows = pl.ds(start, 272)

        def load(ref, cols):
            return pltpu.roll(ref[rows, cols].astype(F32), 272 - shift, 0)[:256].astype(BF)

        def store(ref, cols, value):
            wide = jnp.concatenate([value.astype(F32), jnp.zeros((16, value.shape[1]), F32)], 0)
            put(ref, rows, cols, keep_of(272, shift, last - start)(128), pltpu.roll(wide, shift, 0))

        return (s, load, store, keep_of(256, 0, last - first))

    def large(s, carry):
        first, small = carry
        last = first + lengths[row, s]
        need = last - (first // 16) * 16
        spots[s] = first
        spots[s + 1] = last

        @pl.when(need <= 128)
        def _():
            spots[n_spans + 1 + small] = s

        @pl.when((need > 128) & (need <= 256))
        def _():
            run([view(s, first, last, 256)], 256)

        @pl.when(need > 256)
        def _():
            run([moved_view(s, first, last)], 256)

        return last, small + (need <= 128).astype(jnp.int32)

    _, count = lax.fori_loop(0, n_spans, large, (jnp.int32(0), jnp.int32(0)))

    def joint(i, carry):
        views = []
        for k in range(JOIN):
            s = spots[n_spans + 1 + jnp.minimum(i * JOIN + k, count - 1)]
            views.append(view(s, spots[s], spots[s + 1], 128))
        run(views, 128)
        return carry

    lax.fori_loop(0, (count + JOIN - 1) // JOIN, joint, 0)


def pick(pair):
    return pair[0] + lax.axis_index("section") * (pair[1] - pair[0])


def row_kernel(f_rows, b_rows, names, *refs):
    r = dict(zip(names, refs))
    lengths = r["lengths"]
    fused = b_rows[1] >= 0
    with_arr = f_rows[1] >= 0
    v_x = r["v_x"]
    T, D = v_x.shape
    FF = r["w_up"].shape[1]
    n_tiles = T // TILE
    sem_in, sem_out = r["sem_in"], r["sem_out"]
    section = lax.axis_index("section")
    v_proj, v_att, v_slope, v_lse, v_mixed = [r["v_" + k] for k in ("proj", "att", "slope", "lse", "mixed")]
    v_gelu = r.get("v_gelu")
    w_qkv, w_out, w_up, w_down = r["w_qkv"], r["w_out"], r["w_up"], r["w_down"]
    ins, outs = {}, {}

    def load(key, source, target):
        k = ins.setdefault(key, len(ins))
        return pltpu.make_async_copy(source, target, sem_in.at[k])

    def load_tile(key, source, target, t):
        return load((key, t), source.at[tile_rows(t)], target.at[tile_rows(t)])

    def sends(t, pairs):
        rows = tile_rows(t)
        copies = []
        for key, source, target in pairs:
            k = outs.setdefault(key, len(outs))
            copies.append(pltpu.make_async_copy(source.at[rows], target.at[rows], sem_out.at[k, t]))
        return copies

    if "vec" in r:
        r["vec"][...] = jnp.zeros_like(r["vec"])

    def hidden(rows):
        h = v_x[rows, :].astype(F32)
        return h + r["arr"][rows, :].astype(F32) if with_arr else h

    def forward(row):
        c_x = [load_tile("x", r["x"].at[row], v_x, t) for t in range(n_tiles)]
        c_qkv = load("wqkv", r["wqkv"], w_qkv)
        later = [load("wo", r["wo"], w_out), load("wu", r["wu"], w_up), load("wd", r["wd"], w_down)]
        for c in c_x + [c_qkv]:
            c.start()
        for c in later:
            c.start()
        if fused:
            @pl.when(section == 1)
            def _():
                for t in range(n_tiles):
                    load_tile("cot", r["cot"].at[row], r["v_cot"], t).start()
        pairs_a = [("proj", v_proj, r["proj"].at[row])] if f_rows[0] >= 0 else []
        pairs_b = [("out", r["v_out"], r["out"].at[row]), ("gelu", v_gelu, r["gelu"].at[row])]
        pairs_c = []
        if f_rows[0] >= 0:
            pairs_c = [("snd", r["v_out"], r["snd"]), ("att", v_att, r["att"].at[row]), ("slope", v_slope, r["slope"].at[row])]

        def keep_for_encoder(t, pairs, act):
            if pairs:
                @pl.when(section == 0)
                def _():
                    for c in sends(t, pairs):
                        act(c)

        for t in range(n_tiles):
            c_x[t].wait()
            if t == 0:
                c_qkv.wait()
            rows = pl.ds(t * TILE, TILE)
            first = (norm_parts(hidden(rows))[0] * r["n1g"][...] + r["n1b"][...]).astype(BF)
            v_proj[rows, :] = dot(first, w_qkv[...]).astype(BF)
            keep_for_encoder(t, pairs_a, lambda c: c.start())

        def run(views, window):
            n_pairs = D // 128
            eighth = jnp.asarray(0.125, BF)
            q, k, v, score = [], [], [], []
            for span, load, store, keep in views:
                mask, one = mask_lanes(keep, window)
                for p in range(n_pairs):
                    pair_q = stack_pair(load(v_proj, slice(p * 128, p * 128 + 128)) * eighth)
                    pair_k = load(v_proj, slice(D + p * 128, D + p * 128 + 128))
                    v.append(load(v_proj, slice(2 * D + p * 128, 2 * D + p * 128 + 128)))
                    q.append(jnp.concatenate([pair_q, one], 1))
                    k.append(jnp.concatenate([pair_k, mask], 1))
            score = [dot_nt(a, b) for a, b in zip(k, q)]
            raised, sums = [], []
            for i, s in enumerate(score):
                parts, totals, peaks = [], [], []
                for j in range(0, 2 * window, 128):
                    block = s[:, j:j + 128]
                    peak = jnp.max(block, 0, keepdims=True)
                    e = jnp.exp(block - peak)
                    totals.append(jnp.sum(e, 0, keepdims=True))
                    peaks.append(peak)
                    parts.append(e.astype(BF))
                raised.append(jnp.concatenate(parts, 1))
                sums.append(jnp.concatenate(totals, 1))
                at = views[i // n_pairs][0] * n_pairs + i % n_pairs
                v_lse[pl.ds(at, 1), :2 * window] = jnp.concatenate(peaks, 1) + jnp.log(sums[i])
            outs = [dot_tn(a, b) for a, b in zip(v, raised)]
            for i, o in enumerate(outs):
                o = o * (1.0 / sums[i])
                o = jnp.concatenate([o[:64, :window], o[64:, window:]], 0).T
                p = i % n_pairs
                views[i // n_pairs][2](v_mixed, slice(p * 128, p * 128 + 128), o)

        for_spans(lengths, row, T, r["spots"], run)
        c_mixed = pltpu.make_async_copy(v_mixed, r["mixed"].at[row], r["sem_mixed"].at[0])
        c_mixed.start()
        if f_rows[0] >= 0:
            c_lse = pltpu.make_async_copy(v_lse, r["lse"].at[row], r["sem_mixed"].at[1])
            c_lse.start()
        for c in later:
            c.wait()

        def post_tile(t, carry):
            rows = tile_rows(t)
            a = hidden(rows) + dot(v_mixed[rows, :], w_out[...]) + r["bo"][...]
            v_att[rows, :] = a
            second = (norm_parts(a)[0] * r["n2g"][...] + r["n2b"][...]).astype(BF)
            u = dot(second, w_up[...]) + r["bu"][...]
            for c in range(0, FF, CHUNK):
                cc = slice(c, c + CHUNK)
                b = u[:, cc]
                square = b * b
                half = 0.5 + 0.5 * jnp.tanh(b * (GELU_C + (GELU_C * 0.044715) * square))
                v_gelu[rows, cc] = (b * half).astype(BF)
                rise = b * (2.0 * GELU_C + (6.0 * GELU_C * 0.044715) * square)
                v_slope[rows, cc] = (half + (half * (1.0 - half)) * rise).astype(BF)
            r["v_out"][rows, :] = (a + r["bd"][...] + dot(v_gelu[rows, :], w_down[...])).astype(BF)
            for c in sends(t, pairs_b):
                c.start()
            keep_for_encoder(t, pairs_c, lambda c: c.start())
            return carry

        lax.fori_loop(0, n_tiles, post_tile, 0)

        def finish():
            c_mixed.wait()
            if f_rows[0] >= 0:
                c_lse.wait()
            for t in range(n_tiles):
                for c in sends(t, pairs_b):
                    c.wait()
                keep_for_encoder(t, pairs_a + pairs_c, lambda c: c.wait())

        return finish

    def backward(row):
        v_cot, v_gl, v_second, v_al = [r["v_" + k] for k in ("cot", "gl", "second", "al")]
        v_da, v_dmix, v_dproj, v_first, v_dh, vec = [r[k] for k in ("v_da", "v_dmix", "v_dproj", "v_first", "v_dh", "vec")]
        if not fused:
            c_wd = load("wd", r["wd"], w_down)
            c_wu = load("wu", r["wu"], w_up)
            c_wo = load("wo", r["wo"], w_out)
            c_att = load("att", r["att"].at[row], v_att)
            late = [load("proj", r["proj"].at[row], v_proj), load("wqkv", r["wqkv"], w_qkv), load("x", r["x"].at[row], v_x),
                    load("mixed", r["mixed"].at[row], v_mixed), load("lse", r["lse"].at[row], v_lse)]

            def tile_loads(t):
                return [load_tile("cot", r["cot"].at[row], v_cot, t), load_tile("slope", r["slope"].at[row], v_slope, t)]

            for c in tile_loads(0) + [c_wd, c_wu, c_att, c_wo]:
                c.start()
            for t in range(1, n_tiles):
                for c in tile_loads(t):
                    c.start()
            for c in late:
                c.start()

        pairs_a = [("gl", v_gl, r["gl"].at[row]), ("ul", v_slope, r["ul"].at[row]),
                   ("second", v_second, r["second"].at[row]), ("al", v_al, r["al"].at[row])]
        pairs_b = [("first", v_first, r["first"].at[row]), ("dproj", v_dproj, r["dproj"].at[row]),
                   ("dh", v_dh, r["dh"].at[row])]
        if fused:
            pairs_b.append(("bsnd", r["v_bsnd"], r["bsnd"]))
        text_end = T - lengths[row, lengths.shape[1] - 1]

        def pre_tile(t):
            rows = pl.ds(t * TILE, TILE)
            if fused:
                load_tile("cot", r["cot"].at[row], v_cot, t).wait()
            else:
                for c in tile_loads(t):
                    c.wait()
                if t == 0:
                    c_wd.wait()
            pos = t * TILE + lax.broadcasted_iota(jnp.int32, (TILE, 1), 0)
            in_text = (pos < text_end).astype(F32)
            g = v_cot[rows, :].astype(F32) * in_text
            if not fused:
                g = g + r["ret"][rows, :].astype(F32)
            g_low = g.astype(BF)
            v_gl[rows, :] = g_low
            vec[5:6, :] += colsum(g)
            back = dot_nt(g_low, w_down[...])
            for c in range(0, FF, CHUNK):
                cc = slice(c, c + CHUNK)
                ug = back[:, cc] * v_slope[rows, cc].astype(F32)
                vec[6 + c // CHUNK:7 + c // CHUNK, :] += colsum(ug)
                v_slope[rows, cc] = ug.astype(BF)
            if not fused and t == 0:
                c_wu.wait()
            sg = dot_nt(v_slope[rows, :], w_up[...])
            if not fused and t == 0:
                c_att.wait()
                c_wo.wait()
            hat, rstd = norm_parts(v_att[rows, :])
            v_second[rows, :] = (hat * r["n2g"][...] + r["n2b"][...]).astype(BF)
            vec[3:4, :] += colsum(sg * hat)
            vec[4:5, :] += colsum(sg)
            a = g + norm_pull(sg, hat, rstd, r["n2g"][...])
            vec[2:3, :] += colsum(a)
            v_da[rows, :] = a
            a_low = a.astype(BF)
            v_al[rows, :] = a_low
            v_dmix[rows, :] = dot_nt(a_low, w_out[...]).astype(BF)
            for c in sends(t, pairs_a):
                c.start()

        for t in range(n_tiles):
            pre_tile(t)
        if not fused:
            for c in (late[0], late[3], late[4]):
                c.wait()

        def run(views, window):
            n_pairs = D // 128
            chains = range(len(views) * n_pairs)
            zero = jnp.zeros((window, 128), BF)
            eighth = jnp.asarray(0.125, BF)
            lane = lax.broadcasted_iota(jnp.int32, (8, 128), 1)
            head = lax.broadcasted_iota(jnp.int32, (8, 128), 0)
            half_sum = jnp.where(lane // 64 == head, 1.0, 0.0).astype(BF)

            def cols(third, i):
                p = i % n_pairs
                return slice(third * D + p * 128, third * D + p * 128 + 128)

            def load(i, ref, third):
                return views[i // n_pairs][1](ref, cols(third, i))

            extra = [mask_lanes(keep, window) for _, _, _, keep in views]
            q = [stack_pair(load(i, v_proj, 0) * eighth) for i in chains]
            k = [load(i, v_proj, 1) for i in chains]
            v = [load(i, v_proj, 2) for i in chains]
            pulled = [jnp.where(views[i // n_pairs][3](128), load(i, v_dmix, 0), zero) for i in chains]
            do = [stack_pair(d) for d in pulled]
            score = [dot_nt(jnp.concatenate([k[i], extra[i // n_pairs][0]], 1),
                            jnp.concatenate([q[i], extra[i // n_pairs][1]], 1)) for i in chains]
            pulls = [dot_nt(v[i], do[i]) for i in chains]
            inner = []
            for i in chains:
                product = pulled[i].astype(F32) * load(i, v_mixed, 0).astype(F32)
                high = product.astype(BF)
                both = dot_nt(half_sum, high) + dot_nt(half_sum, (product - high.astype(F32)).astype(BF))
                inner.append(jnp.concatenate([both[0:1], both[1:2]], 1))

            def soft(i):
                prob_parts, ds_parts = [], []
                lse = v_lse[pl.ds(views[i // n_pairs][0] * n_pairs + i % n_pairs, 1), :2 * window]
                for j in range(0, 2 * window, 128):
                    prob = jnp.exp(score[i][:, j:j + 128] - lse[:, j:j + 128])
                    ds_parts.append((prob * (pulls[i][:, j:j + 128] - inner[i][:, j:j + 128])).astype(BF))
                    prob_parts.append(prob.astype(BF))
                return jnp.concatenate(prob_parts, 1), jnp.concatenate(ds_parts, 1)

            def mix(i, prob, push):
                store = views[i // n_pairs][2]
                store(v_dproj, cols(2, i), dot(prob, do[i]))
                store(v_dproj, cols(1, i), dot(push, q[i]))
                dq = dot_tn(k[i] * eighth, push)
                store(v_dproj, cols(0, i), jnp.concatenate([dq[:64, :window], dq[64:, window:]], 0).T)

            ahead = soft(0)
            for i in chains:
                now = ahead
                if i + 1 < len(chains):
                    ahead = soft(i + 1)
                mix(i, *now)

        for_spans(lengths, row, T, r["spots"], run)
        if not fused:
            late[1].wait()
            late[2].wait()

        def fin_tile(t, carry):
            rows = tile_rows(t)
            fg = dot_nt(v_dproj[rows, :], w_qkv[...])
            hat, rstd = norm_parts(hidden(rows))
            v_first[rows, :] = (hat * r["n1g"][...] + r["n1b"][...]).astype(BF)
            vec[0:1, :] += colsum(fg * hat)
            vec[1:2, :] += colsum(fg)
            d = v_da[rows, :] + norm_pull(fg, hat, rstd, r["n1g"][...])
            v_dh[rows, :] = d
            if fused:
                r["v_bsnd"][rows, :] = d.astype(BF)
            for c in sends(t, pairs_b):
                c.start()
            return carry

        lax.fori_loop(0, n_tiles, fin_tile, 0)
        for t in range(n_tiles):
            for c in sends(t, pairs_a) + sends(t, pairs_b):
                c.wait()

    if f_rows != (NONE, NONE):
        f_row = pick(f_rows)

        @pl.when(f_row >= 0)
        def _():
            finish = forward(f_row)
            if fused:
                @pl.when(section == 1)
                def _():
                    backward(f_row)
            finish()
    else:
        b_row = pick(b_rows)

        @pl.when(b_row >= 0)
        def _():
            backward(b_row)


def row_slot(f_rows, b_rows, lengths, x, cot, arr, ret, w, bufs):
    n, T, D = x.shape
    FF = w["wu"].shape[1]
    S, V = jax.ShapeDtypeStruct, pltpu.VMEM
    does_f, does_b = max(f_rows) >= 0, max(b_rows) >= 0
    saves = f_rows[0] >= 0
    fused = b_rows[1] >= 0
    ins = {"lengths": (lengths, SMEM), "x": (x, ANY)}
    if does_b:
        ins["cot"] = (cot, ANY)
    if arr is not None:
        ins["arr"] = (arr, VMEM)
    if ret is not None:
        ins["ret"] = (ret, VMEM)
        ins.update({k: (bufs[k], ANY) for k in ("proj", "att", "slope", "mixed", "lse")})
    ins.update({k: (w[k], ANY) for k in ("wqkv", "wo", "wu", "wd")})
    ins.update({k: (w[k], VMEM) for k in ("n1g", "n1b", "bo", "n2g", "n2b", "bu", "bd")})
    wide = {"out": (D, BF), "mixed": (D, BF), "proj": (3 * D, BF), "att": (D, F32), "slope": (FF, BF), "dh": (D, F32),
            "first": (D, BF), "dproj": (3 * D, BF), "al": (D, BF), "second": (D, BF), "ul": (FF, BF), "gelu": (FF, BF),
            "gl": (D, BF)}
    keys = (["out", "mixed", "gelu"] if does_f else []) + (["proj", "att", "slope", "lse"] if saves else [])
    if does_b:
        keys += ["dh", "first", "dproj", "al", "second", "ul", "gl"]
    spans = lengths.shape[1] * D // 128
    outs = {k: (S((n, T, wide[k][0]), wide[k][1]) if k in wide else S((n, spans, CHUNK), F32), ANY) for k in keys}
    if saves:
        outs["snd"] = (S((T, D), BF), ANY)
    if fused:
        outs["bsnd"] = (S((T, D), BF), ANY)
    if does_b:
        outs["vec"] = (S((16, CHUNK), F32), VMEM)
    alias = [k for k in keys if k in bufs]
    scratch = {"v_x": V((T, D), BF), "w_qkv": V((D, 3 * D), BF), "w_out": V((D, D), BF), "w_up": V((D, FF), BF),
               "w_down": V((FF, D), BF), "v_proj": V((T, 3 * D), BF), "v_att": V((T, D), F32), "v_slope": V((T, FF), BF),
               "v_lse": V((spans, CHUNK), F32), "v_mixed": V((T, D), BF)}
    if does_f:
        scratch.update({"v_out": V((T, D), BF), "v_gelu": V((T, FF), BF)})
    if does_b:
        scratch.update({"v_" + k: V((T, wide[k][0]), wide[k][1])
                        for k in ("dh", "first", "dproj", "al", "second", "gl")})
        scratch.update({"v_cot": V((T, D), BF), "v_dmix": V((T, D), BF), "v_da": V((T, D), F32)})
    if fused:
        scratch["v_bsnd"] = V((T, D), BF)
    scratch.update({"sem_in": pltpu.SemaphoreType.DMA((24,)), "sem_out": pltpu.SemaphoreType.DMA((18, T // TILE)),
                    "spots": pltpu.SMEM((2 * lengths.shape[1] + 2,), jnp.int32), "sem_mixed": pltpu.SemaphoreType.DMA((2,))})
    names = list(ins) + ["alias_" + k for k in alias] + list(outs) + list(scratch)
    values = [v for v, _ in ins.values()] + [bufs[k] for k in alias]
    results = pl.pallas_call(
        functools.partial(row_kernel, f_rows, b_rows, names),
        out_shape=[o for o, _ in outs.values()],
        in_specs=[m for _, m in ins.values()] + [ANY] * len(alias),
        out_specs=[m for _, m in outs.values()],
        input_output_aliases={len(ins) + i: list(outs).index(k) for i, k in enumerate(alias)},
        scratch_shapes=list(scratch.values()),
        compiler_params=pltpu.CompilerParams(vmem_limit_bytes=(48 if does_b else 60) * 2**20),
        cost_estimate=pl.CostEstimate(flops=8 * 10**9 * does_f + 14 * 10**9 * does_b, bytes_accessed=20 * 2**20,
                                      transcendentals=0),
        name="row_" + "f" * does_f + "b" * does_b,
    )(*values)
    got = dict(zip(outs, results))
    send = (got.get("snd"), got.get("bsnd"))
    if None in send:
        send = send[0] if send[1] is None else send[1]
    return {**bufs, **{k: got[k] for k in keys}}, send, got.get("vec")


def reduce_kernel(n, *refs):
    bits = n.bit_length() - 1
    (gelu_any, gl_any, second_any, ul_any, mixed_any, al_any, first_any, dproj_any, vec_a, vec_b, vec_c, vec_d) = refs[:12]
    (wd_out, wu_out, wo_out, wqkv_out, vec_out) = refs[12:17]
    left, right, total, final, *rest = refs[17:]
    inbox = rest[:bits]
    (vec_box, vec_tmp, sem_load, sem_store, rs_send, rs_recv, ag_send, ag_recv, vec_send, vec_recv) = rest[bits:]
    n_chunks = total.shape[0]
    FF = gelu_any.shape[2]
    D = gl_any.shape[2]
    T = gl_any.shape[1]
    rows = gl_any.shape[0]
    ff_chunks = FF // CHUNK
    me = lax.axis_index("dp")
    size = total.shape[1]
    value = [(me // 2**b) % 2 for b in range(bits)]
    partner = [me + (1 - 2 * value[b]) * 2**b for b in range(bits)]
    base = [sum(value[i] * (size >> (i + 1)) for i in range(b)) for b in range(bits + 1)]

    barrier = pltpu.get_barrier_semaphore()
    for b in range(bits):
        pl.semaphore_signal(barrier, inc=1, device_id={"dp": partner[b]}, device_id_type=MESH)
    pl.semaphore_wait(barrier, bits)

    def halve(c, b):
        half = size >> (b + 1)
        away = pl.multiple_of(base[b] + (1 - value[b]) * half, half)
        return pltpu.make_async_remote_copy(
            src_ref=total.at[c, pl.ds(away, half)], dst_ref=inbox[b].at[c],
            send_sem=rs_send.at[c, b], recv_sem=rs_recv.at[c, b],
            device_id={"dp": partner[b]}, device_id_type=MESH,
        )

    def double(c, b):
        half = size >> (b + 1)
        here = final.at[c, pl.ds(pl.multiple_of(base[b + 1], half), half)]
        return pltpu.make_async_remote_copy(
            src_ref=here, dst_ref=here,
            send_sem=ag_send.at[c, b], recv_sem=ag_recv.at[c, b],
            device_id={"dp": partner[b]}, device_id_type=MESH,
        )

    def add_in(c, b):
        half = size >> (b + 1)
        mine = pl.ds(pl.multiple_of(base[b + 1], half), half)
        target = total if b + 1 < bits else final
        target[c, mine, :] = (total[c, mine, :].astype(F32) + inbox[b][c].astype(F32)).astype(BF)

    def load(c, slot, act):
        def both(a, b):
            for k, (source, target) in enumerate(((a, left), (b, right))):
                act(pltpu.make_async_copy(source, target.at[slot], sem_load.at[k, slot]))

        def cols(ref, j):
            return ref.at[:, :, pl.ds(pl.multiple_of(j * CHUNK, CHUNK), CHUNK)]

        @pl.when(c < ff_chunks)
        def _():
            both(cols(gelu_any, c), gl_any)

        @pl.when((c >= ff_chunks) & (c < 2 * ff_chunks))
        def _():
            both(second_any, cols(ul_any, c - ff_chunks))

        @pl.when(c == 2 * ff_chunks)
        def _():
            both(mixed_any, al_any)

        @pl.when((c > 2 * ff_chunks) & (c < n_chunks))
        def _():
            both(first_any, cols(dproj_any, c - 2 * ff_chunks - 1))

    def store(c, act):
        def block(target):
            act(pltpu.make_async_copy(final.at[c], target, sem_store.at[c]))

        def cols(ref, j):
            return ref.at[:, pl.ds(pl.multiple_of(j * CHUNK, CHUNK), CHUNK)]

        @pl.when((c >= 0) & (c < ff_chunks))
        def _():
            block(wd_out.at[pl.ds(pl.multiple_of(c * CHUNK, CHUNK), CHUNK)])

        @pl.when((c >= ff_chunks) & (c < 2 * ff_chunks))
        def _():
            block(cols(wu_out, c - ff_chunks))

        @pl.when(c == 2 * ff_chunks)
        def _():
            block(wo_out)

        @pl.when(c > 2 * ff_chunks)
        def _():
            block(cols(wqkv_out, c - 2 * ff_chunks - 1))

    def vec_copy(b):
        return pltpu.make_async_remote_copy(
            src_ref=vec_tmp.at[b], dst_ref=vec_box.at[b],
            send_sem=vec_send.at[b], recv_sem=vec_recv.at[b],
            device_id={"dp": partner[b]}, device_id_type=MESH,
        )

    vec_tmp[0] = vec_a[...] + vec_b[...] + vec_c[...] + vec_d[...]
    vec_copy(0).start()
    load(jnp.int32(0), 0, lambda c: c.start())

    gaps = [1, 2] + [1 + b % 2 for b in range(2, bits)]
    lags = [0]
    for gap in gaps[:bits] + gaps[bits - 1::-1]:
        lags.append(lags[-1] + gap)

    def slot_step(t, carry):
        def stage_of(lag, act):
            c = t - lag

            @pl.when((c >= 0) & (c < n_chunks))
            def _():
                act(c)

        def make(c):
            slot = lax.rem(c, 2)
            load(c + 1, 1 - slot, lambda d: d.start())
            load(c, slot, lambda d: d.wait())
            a = left[slot].reshape(rows * T, CHUNK)
            b = right[slot].reshape(rows * T, CHUNK)
            total[c] = dot_tn(a, b).astype(BF)
            halve(c, 0).start()

        def reduce_step(b):
            def act(c):
                halve(c, b).wait()
                add_in(c, b)
                if b + 1 < bits:
                    halve(c, b + 1).start()
                else:
                    double(c, b).start()
            return act

        def gather_step(b):
            def act(c):
                double(c, b).wait()
                double(c, b - 1).start()
            return act

        def finish(c):
            double(c, 0).wait()
            store(c, lambda d: d.start())

        acts = [make] + [reduce_step(b) for b in range(bits)] + [gather_step(b) for b in range(bits - 1, 0, -1)] + [finish]
        for lag, act in zip(lags, acts):
            stage_of(lag, act)
        return carry

    lax.fori_loop(0, n_chunks + lags[-1], slot_step, 0)
    for b in range(bits):
        vec_copy(b).wait()
        merged = vec_tmp[b] + vec_box[b]
        if b + 1 < bits:
            vec_tmp[b + 1] = merged
            vec_copy(b + 1).start()
        else:
            vec_out[...] = merged
    for c in range(n_chunks):
        store(jnp.int32(c), lambda d: d.wait())


def weight_grads(n, bufs, vecs):
    gl, ul = bufs["gl"], bufs["ul"]
    rows, T, D = gl.shape
    FF = ul.shape[2]
    bits = n.bit_length() - 1
    n_chunks = 2 * (FF // CHUNK) + 1 + 3 * D // CHUNK
    size = CHUNK
    S, V, DMA = jax.ShapeDtypeStruct, pltpu.VMEM, pltpu.SemaphoreType.DMA
    return pl.pallas_call(
        functools.partial(reduce_kernel, n),
        out_shape=[S((FF, D), BF), S((D, FF), BF), S((D, D), BF), S((D, 3 * D), BF), S((16, CHUNK), F32)],
        in_specs=[ANY] * 8 + [VMEM] * 4,
        out_specs=[ANY] * 4 + [VMEM],
        scratch_shapes=[
            V((2, rows, T, CHUNK), BF), V((2, rows, T, CHUNK), BF), V((n_chunks, size, CHUNK), BF),
            V((n_chunks, size, CHUNK), BF),
            *[V((n_chunks, size >> (b + 1), CHUNK), BF) for b in range(bits)],
            V((bits, 16, CHUNK), F32), V((bits, 16, CHUNK), F32),
            DMA((2, 2)), DMA((n_chunks,)), DMA((n_chunks, bits)), DMA((n_chunks, bits)), DMA((n_chunks, bits)),
            DMA((n_chunks, bits)), DMA((bits,)), DMA((bits,)),
        ],
        compiler_params=pltpu.CompilerParams(vmem_limit_bytes=52 * 2**20, collective_id=0, has_side_effects=True),
        cost_estimate=pl.CostEstimate(flops=13 * 10**9, bytes_accessed=60 * 2**20, transcendentals=0),
        name="weight_grads",
    )(*[bufs[k] for k in ("gelu", "gl", "second", "ul", "mixed", "al", "first", "dproj")], *vecs)


def body(inputs, cotangent, lengths, norm1_gain, norm1_bias, weight_qkv, weight_out, bias_out, norm2_gain, norm2_bias,
         weight_up, bias_up, weight_down, bias_down):
    w = dict(n1g=norm1_gain, n1b=norm1_bias, wqkv=weight_qkv[0], wo=weight_out[0], bo=bias_out, n2g=norm2_gain,
             n2b=norm2_bias, wu=weight_up[0], bu=bias_up, wd=weight_down[0], bd=bias_down)
    x, cot = inputs[0], cotangent[0]
    n = lax.axis_size("dp")

    def ahead(block):
        return lax.ppermute(block, "section", [(0, 1)])

    def back(block):
        return lax.ppermute(block, "section", [(1, 0)])

    bufs, send_a, _ = row_slot((0, NONE), (NONE, NONE), lengths, x, cot, None, None, w, {})
    row_0 = ahead(send_a)
    bufs, send_b, _ = row_slot((1, NONE), (NONE, NONE), lengths, x, cot, None, None, w, bufs)
    row_1 = ahead(send_b)
    bufs, back_b, vec_b = row_slot((NONE, 0), (NONE, 0), lengths, x, cot, row_0, None, w, bufs)
    ret_0 = back(back_b)
    bufs, back_d, vec_d = row_slot((NONE, 1), (NONE, 1), lengths, x, cot, row_1, None, w, bufs)
    ret_1 = back(back_d)
    bufs, _, vec_e = row_slot((NONE, NONE), (0, NONE), lengths, x, cot, None, ret_0, w, bufs)
    bufs, _, vec_g = row_slot((NONE, NONE), (1, NONE), lengths, x, cot, None, ret_1, w, bufs)
    wd, wu, wo, wqkv, vec = weight_grads(n, bufs, (vec_b, vec_d, vec_e, vec_g))

    def wide(v):
        return v.astype(F32)[None]

    return (bufs["out"][None], bufs["dh"][None], vec[0:1], vec[1:2], wide(wqkv), wide(wo), vec[2:3], vec[3:4], vec[4:5],
            wide(wu), vec[6:10].reshape(1, -1), wide(wd), vec[5:6])


def solution(mesh):
    matrix, row = P("section", None, None), P("section", None)
    data = P("section", "dp", None, None)
    return jax.shard_map(
        body,
        mesh=mesh,
        in_specs=(data, data, P("dp", None), row, row, matrix, matrix, row, row, row, matrix, row, matrix, row),
        out_specs=(data, data, row, row, matrix, matrix, row, row, row, matrix, row, matrix, row),
        check_vma=False,
    )
```

```python
import functools

import jax
import jax.numpy as jnp
from jax import lax
from jax.experimental import pallas as pl
from jax.experimental.pallas import tpu as pltpu
from jax.sharding import PartitionSpec as P

EPSILON = 1e-05
GELU_C = 0.7978845608028654
MASKED = -1e30
TILE = 512
CHUNK = 512
JOIN = 3
WINDOWS = (128, 192, 256, 272)
LSE_WIDTH = 640
NONE = -4
BF = jnp.bfloat16
F32 = jnp.float32
MESH = pl.DeviceIdType.MESH
ANY = pl.BlockSpec(memory_space=pl.ANY)
VMEM = pl.BlockSpec(memory_space=pltpu.VMEM)
SMEM = pl.BlockSpec(memory_space=pltpu.SMEM)


def dot(a, b):
    return jnp.dot(a, b, preferred_element_type=F32)


def dot_nt(a, b):
    return lax.dot_general(a, b, (((1,), (1,)), ((), ())), preferred_element_type=F32)


def dot_tn(a, b):
    return lax.dot_general(a, b, (((0,), (0,)), ((), ())), preferred_element_type=F32)


def norm_parts(v):
    centred = v - jnp.mean(v, -1, keepdims=True)
    rstd = lax.rsqrt(jnp.mean(centred * centred, -1, keepdims=True) + EPSILON)
    return centred * rstd, rstd


def norm_pull(grad, hat, rstd, gain):
    scaled = grad * gain
    return rstd * (
        scaled
        - jnp.mean(scaled, -1, keepdims=True)
        - hat * jnp.mean(scaled * hat, -1, keepdims=True)
    )


def colsum(v):
    return jnp.sum(v, 0, keepdims=True)


def stack_pair(block):
    lane = lax.broadcasted_iota(jnp.int32, block.shape, 1)
    zero = jnp.zeros_like(block)
    low = lane < 64
    return jnp.concatenate([jnp.where(low, block, zero), jnp.where(low, zero, block)], 0)


def unstack_pair(both):
    rows = both.shape[0] // 2
    lane = lax.broadcasted_iota(jnp.int32, (rows, 128), 1)
    return jnp.where(lane < 64, both[:rows], both[rows:])


def mask_lanes(keep, window):
    lane = lax.broadcasted_iota(jnp.int32, (window, 128), 1)
    mask = jnp.where(keep(128) | (lane > 0), 0.0, MASKED).astype(BF)
    one = jnp.where(lax.broadcasted_iota(jnp.int32, (2 * window, 128), 1) == 0, 1.0, 0.0).astype(BF)
    return mask, one


def tile_rows(t):
    return pl.ds(pl.multiple_of(t * TILE, TILE), TILE)


def for_spans(lengths, row, length, spots, run):
    n_spans = lengths.shape[1]

    def keep_of(window, low, high):
        def keep(width):
            pos = lax.broadcasted_iota(jnp.int32, (window, width), 0)
            return (pos >= low) & (pos < high)

        return keep

    def put(ref, rows, cols, keep, value):
        ref[rows, cols] = jnp.where(keep, value.astype(BF), ref[rows, cols])

    def view(s, first, last, window):
        start = pl.multiple_of(jnp.minimum((first // 16) * 16, length - window), 16)
        rows = pl.ds(start, window)
        keep = keep_of(window, first - start, last - start)
        return (s, lambda ref, cols: ref[rows, cols],
                lambda ref, cols, value: put(ref, rows, cols, keep(128), value), keep)

    def large(s, carry):
        first, small = carry
        last = first + lengths[row, s]
        need = last - (first // 16) * 16
        spots[s] = first
        spots[s + 1] = last

        @pl.when(need <= WINDOWS[0])
        def _():
            spots[n_spans + 1 + small] = s

        for below, window in zip(WINDOWS, WINDOWS[1:]):
            @pl.when((need > below) & (need <= window))
            def _():
                run([view(s, first, last, window)], window)

        return last, small + (need <= WINDOWS[0]).astype(jnp.int32)

    _, count = lax.fori_loop(0, n_spans, large, (jnp.int32(0), jnp.int32(0)))

    def joint(i, carry):
        views = []
        for k in range(JOIN):
            s = spots[n_spans + 1 + jnp.minimum(i * JOIN + k, count - 1)]
            views.append(view(s, spots[s], spots[s + 1], WINDOWS[0]))
        run(views, WINDOWS[0])
        return carry

    lax.fori_loop(0, (count + JOIN - 1) // JOIN, joint, 0)


def pick(pair):
    return pair[0] + lax.axis_index("section") * (pair[1] - pair[0])


def row_kernel(f_rows, b_rows, names, *refs):
    r = dict(zip(names, refs))
    lengths = r["lengths"]
    fused = b_rows[1] >= 0
    with_arr = f_rows[1] >= 0
    v_x = r["v_x"]
    T, D = v_x.shape
    FF = r["w_up"].shape[1]
    n_tiles = T // TILE
    sem_in, sem_out = r["sem_in"], r["sem_out"]
    section = lax.axis_index("section")
    v_proj, v_att, v_slope, v_lse, v_mixed = [r["v_" + k] for k in ("proj", "att", "slope", "lse", "mixed")]
    v_gelu = r.get("v_gelu")
    w_qkv, w_out, w_up, w_down = r["w_qkv"], r["w_out"], r["w_up"], r["w_down"]
    ins, outs = {}, {}

    def load(key, source, target):
        k = ins.setdefault(key, len(ins))
        return pltpu.make_async_copy(source, target, sem_in.at[k])

    def load_tile(key, source, target, t):
        return load((key, t), source.at[tile_rows(t)], target.at[tile_rows(t)])

    def sends(t, pairs):
        rows = tile_rows(t)
        copies = []
        for key, source, target in pairs:
            k = outs.setdefault(key, len(outs))
            copies.append(pltpu.make_async_copy(source.at[rows], target.at[rows], sem_out.at[k, t]))
        return copies

    if "vec" in r:
        r["vec"][...] = jnp.zeros_like(r["vec"])

    def hidden(rows):
        h = v_x[rows, :].astype(F32)
        return h + r["arr"][rows, :].astype(F32) if with_arr else h

    def forward(row):
        c_x = [load_tile("x", r["x"].at[row], v_x, t) for t in range(n_tiles)]
        c_qkv = load("wqkv", r["wqkv"], w_qkv)
        later = [load("wo", r["wo"], w_out), load("wu", r["wu"], w_up), load("wd", r["wd"], w_down)]
        for c in c_x + [c_qkv]:
            c.start()
        for c in later:
            c.start()
        if fused:
            @pl.when(section == 1)
            def _():
                for t in range(n_tiles):
                    load_tile("cot", r["cot"].at[row], r["v_cot"], t).start()
        pairs_a = [("proj", v_proj, r["proj"].at[row])] if f_rows[0] >= 0 else []
        pairs_b = [("out", r["v_out"], r["out"].at[row]), ("gelu", v_gelu, r["gelu"].at[row])]
        pairs_c = []
        if f_rows[0] >= 0:
            pairs_c = [("snd", r["v_out"], r["snd"]), ("att", v_att, r["att"].at[row]), ("slope", v_slope, r["slope"].at[row])]

        def keep_for_encoder(t, pairs, act):
            if pairs:
                @pl.when(section == 0)
                def _():
                    for c in sends(t, pairs):
                        act(c)

        for t in range(n_tiles):
            c_x[t].wait()
            if t == 0:
                c_qkv.wait()
            rows = pl.ds(t * TILE, TILE)
            first = (norm_parts(hidden(rows))[0] * r["n1g"][...] + r["n1b"][...]).astype(BF)
            v_proj[rows, :] = dot(first, w_qkv[...]).astype(BF)
            keep_for_encoder(t, pairs_a, lambda c: c.start())

        def run(views, window):
            n_pairs = D // 128
            eighth = jnp.asarray(0.125, BF)
            q, k, v, score = [], [], [], []
            for span, load, store, keep in views:
                mask, one = mask_lanes(keep, window)
                for p in range(n_pairs):
                    pair_q = stack_pair(load(v_proj, slice(p * 128, p * 128 + 128)) * eighth)
                    pair_k = load(v_proj, slice(D + p * 128, D + p * 128 + 128))
                    v.append(load(v_proj, slice(2 * D + p * 128, 2 * D + p * 128 + 128)))
                    q.append(jnp.concatenate([pair_q, one], 1))
                    k.append(jnp.concatenate([pair_k, mask], 1))
            score = [dot_nt(a, b) for a, b in zip(k, q)]
            raised, sums = [], []
            for i, s in enumerate(score):
                parts, totals, peaks = [], [], []
                for j in range(0, 2 * window, 128):
                    block = s[:, j:min(j + 128, 2 * window)]
                    peak = jnp.max(block, 0, keepdims=True)
                    e = jnp.exp(block - peak)
                    totals.append(jnp.sum(e, 0, keepdims=True))
                    peaks.append(peak)
                    parts.append(e.astype(BF))
                raised.append(jnp.concatenate(parts, 1))
                sums.append(jnp.concatenate(totals, 1))
                at = views[i // n_pairs][0] * n_pairs + i % n_pairs
                v_lse[pl.ds(at, 1), :2 * window] = jnp.concatenate(peaks, 1) + jnp.log(sums[i])
            outs = [dot_tn(a, b) for a, b in zip(v, raised)]
            for i, o in enumerate(outs):
                o = o * (1.0 / sums[i])
                o = jnp.concatenate([o[:64, :window], o[64:, window:]], 0).T
                p = i % n_pairs
                views[i // n_pairs][2](v_mixed, slice(p * 128, p * 128 + 128), o)

        for_spans(lengths, row, T, r["spots"], run)
        c_mixed = pltpu.make_async_copy(v_mixed, r["mixed"].at[row], r["sem_mixed"].at[0])
        c_mixed.start()
        if f_rows[0] >= 0:
            c_lse = pltpu.make_async_copy(v_lse, r["lse"].at[row], r["sem_mixed"].at[1])
            c_lse.start()
        for c in later:
            c.wait()

        def post_tile(t, carry):
            rows = tile_rows(t)
            a = hidden(rows) + dot(v_mixed[rows, :], w_out[...]) + r["bo"][...]
            v_att[rows, :] = a
            second = (norm_parts(a)[0] * r["n2g"][...] + r["n2b"][...]).astype(BF)
            u = dot(second, w_up[...]) + r["bu"][...]
            for c in range(0, FF, CHUNK):
                cc = slice(c, c + CHUNK)
                b = u[:, cc].astype(BF)
                square = b * b
                half = 0.5 + 0.5 * jnp.tanh(b * (GELU_C + (GELU_C * 0.044715) * square))
                v_gelu[rows, cc] = b * half
                rise = b * (2.0 * GELU_C + (6.0 * GELU_C * 0.044715) * square)
                v_slope[rows, cc] = half + (half * (1.0 - half)) * rise
            r["v_out"][rows, :] = (a + r["bd"][...] + dot(v_gelu[rows, :], w_down[...])).astype(BF)
            for c in sends(t, pairs_b):
                c.start()
            keep_for_encoder(t, pairs_c, lambda c: c.start())
            return carry

        lax.fori_loop(0, n_tiles, post_tile, 0)

        def finish():
            c_mixed.wait()
            if f_rows[0] >= 0:
                c_lse.wait()
            for t in range(n_tiles):
                for c in sends(t, pairs_b):
                    c.wait()
                keep_for_encoder(t, pairs_a + pairs_c, lambda c: c.wait())

        return finish

    def backward(row):
        v_cot, v_gl, v_second, v_al = [r["v_" + k] for k in ("cot", "gl", "second", "al")]
        v_da, v_dmix, v_dproj, v_first, v_dh, vec = [r[k] for k in ("v_da", "v_dmix", "v_dproj", "v_first", "v_dh", "vec")]
        if not fused:
            c_wd = load("wd", r["wd"], w_down)
            c_wu = load("wu", r["wu"], w_up)
            c_wo = load("wo", r["wo"], w_out)
            c_att = load("att", r["att"].at[row], v_att)
            late = [load("proj", r["proj"].at[row], v_proj), load("wqkv", r["wqkv"], w_qkv), load("x", r["x"].at[row], v_x),
                    load("mixed", r["mixed"].at[row], v_mixed), load("lse", r["lse"].at[row], v_lse)]

            def tile_loads(t):
                return [load_tile("cot", r["cot"].at[row], v_cot, t), load_tile("slope", r["slope"].at[row], v_slope, t)]

            for c in tile_loads(0) + [c_wd, c_wu, c_att, c_wo]:
                c.start()
            for t in range(1, n_tiles):
                for c in tile_loads(t):
                    c.start()
            for c in late:
                c.start()

        pairs_a = [("gl", v_gl, r["gl"].at[row]), ("ul", v_slope, r["ul"].at[row]),
                   ("second", v_second, r["second"].at[row]), ("al", v_al, r["al"].at[row])]
        pairs_b = [("first", v_first, r["first"].at[row]), ("dproj", v_dproj, r["dproj"].at[row]),
                   ("dh", v_dh, r["dh"].at[row])]
        if fused:
            pairs_b.append(("bsnd", r["v_bsnd"], r["bsnd"]))
        text_end = T - lengths[row, lengths.shape[1] - 1]

        def pre_tile(t):
            rows = pl.ds(t * TILE, TILE)
            if fused:
                load_tile("cot", r["cot"].at[row], v_cot, t).wait()
            else:
                for c in tile_loads(t):
                    c.wait()
                if t == 0:
                    c_wd.wait()
            pos = t * TILE + lax.broadcasted_iota(jnp.int32, (TILE, 1), 0)
            in_text = (pos < text_end).astype(F32)
            g = v_cot[rows, :].astype(F32) * in_text
            if not fused:
                g = g + r["ret"][rows, :].astype(F32)
            g_low = g.astype(BF)
            v_gl[rows, :] = g_low
            vec[5:6, :] += colsum(g)
            back = dot_nt(g_low, w_down[...])
            for c in range(0, FF, CHUNK):
                cc = slice(c, c + CHUNK)
                ug = back[:, cc] * v_slope[rows, cc].astype(F32)
                vec[6 + c // CHUNK:7 + c // CHUNK, :] += colsum(ug)
                v_slope[rows, cc] = ug.astype(BF)
            if not fused and t == 0:
                c_wu.wait()
            sg = dot_nt(v_slope[rows, :], w_up[...])
            if not fused and t == 0:
                c_att.wait()
                c_wo.wait()
            hat, rstd = norm_parts(v_att[rows, :])
            v_second[rows, :] = (hat * r["n2g"][...] + r["n2b"][...]).astype(BF)
            vec[3:4, :] += colsum(sg * hat)
            vec[4:5, :] += colsum(sg)
            a = g + norm_pull(sg, hat, rstd, r["n2g"][...])
            vec[2:3, :] += colsum(a)
            v_da[rows, :] = a
            a_low = a.astype(BF)
            v_al[rows, :] = a_low
            v_dmix[rows, :] = dot_nt(a_low, w_out[...]).astype(BF)
            for c in sends(t, pairs_a):
                c.start()

        for t in range(n_tiles):
            pre_tile(t)
        if not fused:
            for c in (late[0], late[3], late[4]):
                c.wait()

        def run(views, window):
            n_pairs = D // 128
            chains = range(len(views) * n_pairs)
            zero = jnp.zeros((window, 128), BF)
            eighth = jnp.asarray(0.125, BF)
            lane = lax.broadcasted_iota(jnp.int32, (8, 128), 1)
            head = lax.broadcasted_iota(jnp.int32, (8, 128), 0)
            half_sum = jnp.where(lane // 64 == head, 1.0, 0.0).astype(BF)

            def cols(third, i):
                p = i % n_pairs
                return slice(third * D + p * 128, third * D + p * 128 + 128)

            def load(i, ref, third):
                return views[i // n_pairs][1](ref, cols(third, i))

            extra = [mask_lanes(keep, window) for _, _, _, keep in views]
            q = [stack_pair(load(i, v_proj, 0) * eighth) for i in chains]
            k = [load(i, v_proj, 1) for i in chains]
            v = [load(i, v_proj, 2) for i in chains]
            pulled = [jnp.where(views[i // n_pairs][3](128), load(i, v_dmix, 0), zero) for i in chains]
            do = [stack_pair(d) for d in pulled]
            score = [dot_nt(jnp.concatenate([k[i], extra[i // n_pairs][0]], 1),
                            jnp.concatenate([q[i], extra[i // n_pairs][1]], 1)) for i in chains]
            pulls = [dot_nt(v[i], do[i]) for i in chains]
            inner = []
            for i in chains:
                product = pulled[i].astype(F32) * load(i, v_mixed, 0).astype(F32)
                high = product.astype(BF)
                both = dot_nt(half_sum, high) + dot_nt(half_sum, (product - high.astype(F32)).astype(BF))
                inner.append(jnp.concatenate([both[0:1], both[1:2]], 1))

            def soft(i):
                prob_parts, ds_parts = [], []
                lse = v_lse[pl.ds(views[i // n_pairs][0] * n_pairs + i % n_pairs, 1), :2 * window]
                for j in range(0, 2 * window, 128):
                    part = slice(j, min(j + 128, 2 * window))
                    prob = jnp.exp(score[i][:, part] - lse[:, part])
                    ds_parts.append((prob * (pulls[i][:, part] - inner[i][:, part])).astype(BF))
                    prob_parts.append(prob.astype(BF))
                return jnp.concatenate(prob_parts, 1), jnp.concatenate(ds_parts, 1)

            def mix(i, prob, push):
                store = views[i // n_pairs][2]
                store(v_dproj, cols(2, i), dot(prob, do[i]))
                store(v_dproj, cols(1, i), dot(push, q[i]))
                dq = dot_tn(k[i] * eighth, push)
                store(v_dproj, cols(0, i), jnp.concatenate([dq[:64, :window], dq[64:, window:]], 0).T)

            ahead = soft(0)
            for i in chains:
                now = ahead
                if i + 1 < len(chains):
                    ahead = soft(i + 1)
                mix(i, *now)

        for_spans(lengths, row, T, r["spots"], run)
        if not fused:
            late[1].wait()
            late[2].wait()

        def fin_tile(t, carry):
            rows = tile_rows(t)
            fg = dot_nt(v_dproj[rows, :], w_qkv[...])
            hat, rstd = norm_parts(hidden(rows))
            v_first[rows, :] = (hat * r["n1g"][...] + r["n1b"][...]).astype(BF)
            vec[0:1, :] += colsum(fg * hat)
            vec[1:2, :] += colsum(fg)
            d = v_da[rows, :] + norm_pull(fg, hat, rstd, r["n1g"][...])
            v_dh[rows, :] = d
            if fused:
                r["v_bsnd"][rows, :] = d.astype(BF)
            for c in sends(t, pairs_b):
                c.start()
            return carry

        lax.fori_loop(0, n_tiles, fin_tile, 0)
        for t in range(n_tiles):
            for c in sends(t, pairs_a) + sends(t, pairs_b):
                c.wait()

    if f_rows != (NONE, NONE):
        f_row = pick(f_rows)

        @pl.when(f_row >= 0)
        def _():
            finish = forward(f_row)
            if fused:
                @pl.when(section == 1)
                def _():
                    backward(f_row)
            finish()
    else:
        b_row = pick(b_rows)

        @pl.when(b_row >= 0)
        def _():
            backward(b_row)


def row_slot(f_rows, b_rows, lengths, x, cot, arr, ret, w, bufs):
    n, T, D = x.shape
    FF = w["wu"].shape[1]
    S, V = jax.ShapeDtypeStruct, pltpu.VMEM
    does_f, does_b = max(f_rows) >= 0, max(b_rows) >= 0
    saves = f_rows[0] >= 0
    fused = b_rows[1] >= 0
    ins = {"lengths": (lengths, SMEM), "x": (x, ANY)}
    if does_b:
        ins["cot"] = (cot, ANY)
    if arr is not None:
        ins["arr"] = (arr, VMEM)
    if ret is not None:
        ins["ret"] = (ret, VMEM)
        ins.update({k: (bufs[k], ANY) for k in ("proj", "att", "slope", "mixed", "lse")})
    ins.update({k: (w[k], ANY) for k in ("wqkv", "wo", "wu", "wd")})
    ins.update({k: (w[k], VMEM) for k in ("n1g", "n1b", "bo", "n2g", "n2b", "bu", "bd")})
    wide = {"out": (D, BF), "mixed": (D, BF), "proj": (3 * D, BF), "att": (D, F32), "slope": (FF, BF), "dh": (D, F32),
            "first": (D, BF), "dproj": (3 * D, BF), "al": (D, BF), "second": (D, BF), "ul": (FF, BF), "gelu": (FF, BF),
            "gl": (D, BF)}
    keys = (["out", "mixed", "gelu"] if does_f else []) + (["proj", "att", "slope", "lse"] if saves else [])
    if does_b:
        keys += ["dh", "first", "dproj", "al", "second", "ul", "gl"]
    spans = lengths.shape[1] * D // 128
    outs = {k: (S((n, T, wide[k][0]), wide[k][1]) if k in wide else S((n, spans, LSE_WIDTH), F32), ANY) for k in keys}
    if saves:
        outs["snd"] = (S((T, D), BF), ANY)
    if fused:
        outs["bsnd"] = (S((T, D), BF), ANY)
    if does_b:
        outs["vec"] = (S((16, CHUNK), F32), VMEM)
    alias = [k for k in keys if k in bufs]
    scratch = {"v_x": V((T, D), BF), "w_qkv": V((D, 3 * D), BF), "w_out": V((D, D), BF), "w_up": V((D, FF), BF),
               "w_down": V((FF, D), BF), "v_proj": V((T, 3 * D), BF), "v_att": V((T, D), F32), "v_slope": V((T, FF), BF),
               "v_lse": V((spans, LSE_WIDTH), F32), "v_mixed": V((T, D), BF)}
    if does_f:
        scratch.update({"v_out": V((T, D), BF), "v_gelu": V((T, FF), BF)})
    if does_b:
        scratch.update({"v_" + k: V((T, wide[k][0]), wide[k][1])
                        for k in ("dh", "first", "dproj", "al", "second", "gl")})
        scratch.update({"v_cot": V((T, D), BF), "v_dmix": V((T, D), BF), "v_da": V((T, D), F32)})
    if fused:
        scratch["v_bsnd"] = V((T, D), BF)
    scratch.update({"sem_in": pltpu.SemaphoreType.DMA((24,)), "sem_out": pltpu.SemaphoreType.DMA((18, T // TILE)),
                    "spots": pltpu.SMEM((2 * lengths.shape[1] + 2,), jnp.int32), "sem_mixed": pltpu.SemaphoreType.DMA((2,))})
    names = list(ins) + ["alias_" + k for k in alias] + list(outs) + list(scratch)
    values = [v for v, _ in ins.values()] + [bufs[k] for k in alias]
    results = pl.pallas_call(
        functools.partial(row_kernel, f_rows, b_rows, names),
        out_shape=[o for o, _ in outs.values()],
        in_specs=[m for _, m in ins.values()] + [ANY] * len(alias),
        out_specs=[m for _, m in outs.values()],
        input_output_aliases={len(ins) + i: list(outs).index(k) for i, k in enumerate(alias)},
        scratch_shapes=list(scratch.values()),
        compiler_params=pltpu.CompilerParams(vmem_limit_bytes=(48 if does_b else 60) * 2**20),
        cost_estimate=pl.CostEstimate(flops=8 * 10**9 * does_f + 14 * 10**9 * does_b, bytes_accessed=20 * 2**20,
                                      transcendentals=0),
        name="row_" + "f" * does_f + "b" * does_b,
    )(*values)
    got = dict(zip(outs, results))
    send = (got.get("snd"), got.get("bsnd"))
    if None in send:
        send = send[0] if send[1] is None else send[1]
    return {**bufs, **{k: got[k] for k in keys}}, send, got.get("vec")


def reduce_kernel(n, *refs):
    bits = n.bit_length() - 1
    (gelu_any, gl_any, second_any, ul_any, mixed_any, al_any, first_any, dproj_any, vec_a, vec_b, vec_c, vec_d) = refs[:12]
    result, vec_out = refs[12:14]
    left, right, total, final, *rest = refs[14:]
    inbox = rest[:bits]
    (vec_box, vec_tmp, sem_load, sem_store, rs_send, rs_recv, ag_send, ag_recv, vec_send, vec_recv) = rest[bits:]
    n_chunks = total.shape[0]
    FF = gelu_any.shape[2]
    D = gl_any.shape[2]
    T = gl_any.shape[1]
    rows = gl_any.shape[0]
    ff_chunks = FF // CHUNK
    me = lax.axis_index("dp")
    size = total.shape[1]
    value = [(me // 2**b) % 2 for b in range(bits)]
    partner = [me + (1 - 2 * value[b]) * 2**b for b in range(bits)]
    base = [sum(value[i] * (size >> (i + 1)) for i in range(b)) for b in range(bits + 1)]

    barrier = pltpu.get_barrier_semaphore()
    for b in range(bits):
        pl.semaphore_signal(barrier, inc=1, device_id={"dp": partner[b]}, device_id_type=MESH)
    pl.semaphore_wait(barrier, bits)

    def halve(c, b):
        half = size >> (b + 1)
        away = pl.multiple_of(base[b] + (1 - value[b]) * half, half)
        return pltpu.make_async_remote_copy(
            src_ref=total.at[c, pl.ds(away, half)], dst_ref=inbox[b].at[c],
            send_sem=rs_send.at[c, b], recv_sem=rs_recv.at[c, b],
            device_id={"dp": partner[b]}, device_id_type=MESH,
        )

    def double(c, b):
        half = size >> (b + 1)
        here = final.at[c, pl.ds(pl.multiple_of(base[b + 1], half), half)]
        return pltpu.make_async_remote_copy(
            src_ref=here, dst_ref=here,
            send_sem=ag_send.at[c, b], recv_sem=ag_recv.at[c, b],
            device_id={"dp": partner[b]}, device_id_type=MESH,
        )

    def add_in(c, b):
        half = size >> (b + 1)
        mine = pl.ds(pl.multiple_of(base[b + 1], half), half)
        target = total if b + 1 < bits else final
        target[c, mine, :] = (total[c, mine, :].astype(F32) + inbox[b][c].astype(F32)).astype(BF)

    def load(c, slot, act):
        def both(a, b):
            for k, (source, target) in enumerate(((a, left), (b, right))):
                act(pltpu.make_async_copy(source, target.at[slot], sem_load.at[k, slot]))

        def cols(ref, j):
            return ref.at[:, :, pl.ds(pl.multiple_of(j * CHUNK, CHUNK), CHUNK)]

        @pl.when(c < ff_chunks)
        def _():
            both(cols(gelu_any, c), gl_any)

        @pl.when((c >= ff_chunks) & (c < 2 * ff_chunks))
        def _():
            both(second_any, cols(ul_any, c - ff_chunks))

        @pl.when(c == 2 * ff_chunks)
        def _():
            both(mixed_any, al_any)

        @pl.when((c > 2 * ff_chunks) & (c < n_chunks))
        def _():
            both(first_any, cols(dproj_any, c - 2 * ff_chunks - 1))

    def publish(c):
        return pltpu.make_async_copy(final.at[c], result.at[c], sem_store.at[c])

    def vec_copy(b):
        return pltpu.make_async_remote_copy(
            src_ref=vec_tmp.at[b], dst_ref=vec_box.at[b],
            send_sem=vec_send.at[b], recv_sem=vec_recv.at[b],
            device_id={"dp": partner[b]}, device_id_type=MESH,
        )

    vec_tmp[0] = vec_a[...] + vec_b[...] + vec_c[...] + vec_d[...]
    vec_copy(0).start()
    load(jnp.int32(0), 0, lambda c: c.start())

    gaps = [1, 2] + [1 + b % 2 for b in range(2, bits)]
    lags = [0]
    for gap in gaps[:bits] + gaps[bits - 1::-1]:
        lags.append(lags[-1] + gap)

    def slot_step(t, carry):
        def stage_of(lag, act):
            c = t - lag

            @pl.when((c >= 0) & (c < n_chunks))
            def _():
                act(c)

        def make(c):
            slot = lax.rem(c, 2)
            load(c + 1, 1 - slot, lambda d: d.start())
            load(c, slot, lambda d: d.wait())
            a = left[slot].reshape(rows * T, CHUNK)
            b = right[slot].reshape(rows * T, CHUNK)
            total[c] = dot_tn(a, b).astype(BF)
            halve(c, 0).start()

        def reduce_step(b):
            def act(c):
                halve(c, b).wait()
                add_in(c, b)
                if b + 1 < bits:
                    halve(c, b + 1).start()
                else:
                    double(c, b).start()
            return act

        def gather_step(b):
            def act(c):
                double(c, b).wait()
                double(c, b - 1).start()
            return act

        def finish(c):
            double(c, 0).wait()
            publish(c).start()

        acts = [make] + [reduce_step(b) for b in range(bits)] + [gather_step(b) for b in range(bits - 1, 0, -1)] + [finish]
        for lag, act in zip(lags, acts):
            stage_of(lag, act)
        return carry

    lax.fori_loop(0, n_chunks + lags[-1], slot_step, 0)
    for b in range(bits):
        vec_copy(b).wait()
        merged = vec_tmp[b] + vec_box[b]
        if b + 1 < bits:
            vec_tmp[b + 1] = merged
            vec_copy(b + 1).start()
        else:
            vec_out[...] = merged
    for c in range(n_chunks):
        publish(c).wait()


def wide_kernel(chunks, wd, wu, wo, wqkv, held, stage, sem_in, sem):
    blocks = [(w, r, c) for w in (wd, wu, wo, wqkv) for r in range(0, w.shape[1], CHUNK) for c in range(0, w.shape[2], CHUNK)]
    loads = [pltpu.make_async_copy(chunks.at[k], held.at[k], sem_in.at[k]) for k in range(len(blocks))]
    for c in loads:
        c.start()
    copies = []
    for k, (w, r, c) in enumerate(blocks):
        loads[k].wait()
        stage[k] = held[k].astype(F32)
        copies.append(pltpu.make_async_copy(stage.at[k], w.at[0, pl.ds(r, CHUNK), pl.ds(c, CHUNK)], sem.at[k]))
        copies[k].start()
    for c in copies:
        c.wait()


def widen(chunks, shapes):
    n = chunks.shape[0]
    return pl.pallas_call(
        wide_kernel,
        out_shape=[jax.ShapeDtypeStruct((1, *shape), F32) for shape in shapes],
        in_specs=[ANY],
        out_specs=[ANY] * len(shapes),
        scratch_shapes=[pltpu.VMEM(chunks.shape, BF), pltpu.VMEM(chunks.shape, F32),
                        pltpu.SemaphoreType.DMA((n,)), pltpu.SemaphoreType.DMA((n,))],
        compiler_params=pltpu.CompilerParams(vmem_limit_bytes=60 * 2**20),
        name="widen",
    )(chunks)


def weight_grads(n, bufs, vecs):
    gl, ul = bufs["gl"], bufs["ul"]
    rows, T, D = gl.shape
    FF = ul.shape[2]
    bits = n.bit_length() - 1
    n_chunks = 2 * (FF // CHUNK) + 1 + 3 * D // CHUNK
    size = CHUNK
    S, V, DMA = jax.ShapeDtypeStruct, pltpu.VMEM, pltpu.SemaphoreType.DMA
    return pl.pallas_call(
        functools.partial(reduce_kernel, n),
        out_shape=[S((n_chunks, CHUNK, CHUNK), BF), S((16, CHUNK), F32)],
        in_specs=[ANY] * 8 + [VMEM] * 4,
        out_specs=[ANY, VMEM],
        scratch_shapes=[
            V((2, rows, T, CHUNK), BF), V((2, rows, T, CHUNK), BF), V((n_chunks, size, CHUNK), BF),
            V((n_chunks, size, CHUNK), BF),
            *[V((n_chunks, size >> (b + 1), CHUNK), BF) for b in range(bits)],
            V((bits, 16, CHUNK), F32), V((bits, 16, CHUNK), F32),
            DMA((2, 2)), DMA((n_chunks,)), DMA((n_chunks, bits)), DMA((n_chunks, bits)), DMA((n_chunks, bits)),
            DMA((n_chunks, bits)), DMA((bits,)), DMA((bits,)),
        ],
        compiler_params=pltpu.CompilerParams(vmem_limit_bytes=60 * 2**20, collective_id=0, has_side_effects=True),
        cost_estimate=pl.CostEstimate(flops=13 * 10**9, bytes_accessed=60 * 2**20, transcendentals=0),
        name="weight_grads",
    )(*[bufs[k] for k in ("gelu", "gl", "second", "ul", "mixed", "al", "first", "dproj")], *vecs)


def body(inputs, cotangent, lengths, norm1_gain, norm1_bias, weight_qkv, weight_out, bias_out, norm2_gain, norm2_bias,
         weight_up, bias_up, weight_down, bias_down):
    w = dict(n1g=norm1_gain, n1b=norm1_bias, wqkv=weight_qkv[0], wo=weight_out[0], bo=bias_out, n2g=norm2_gain,
             n2b=norm2_bias, wu=weight_up[0], bu=bias_up, wd=weight_down[0], bd=bias_down)
    x, cot = inputs[0], cotangent[0]
    n = lax.axis_size("dp")

    def ahead(block):
        return lax.ppermute(block, "section", [(0, 1)])

    def back(block):
        return lax.ppermute(block, "section", [(1, 0)])

    bufs, send_a, _ = row_slot((0, NONE), (NONE, NONE), lengths, x, cot, None, None, w, {})
    row_0 = ahead(send_a)
    bufs, send_b, _ = row_slot((1, NONE), (NONE, NONE), lengths, x, cot, None, None, w, bufs)
    row_1 = ahead(send_b)
    bufs, back_b, vec_b = row_slot((NONE, 0), (NONE, 0), lengths, x, cot, row_0, None, w, bufs)
    ret_0 = back(back_b)
    bufs, back_d, vec_d = row_slot((NONE, 1), (NONE, 1), lengths, x, cot, row_1, None, w, bufs)
    ret_1 = back(back_d)
    bufs, _, vec_e = row_slot((NONE, NONE), (0, NONE), lengths, x, cot, None, ret_0, w, bufs)
    bufs, _, vec_g = row_slot((NONE, NONE), (1, NONE), lengths, x, cot, None, ret_1, w, bufs)
    chunks, vec = weight_grads(n, bufs, (vec_b, vec_d, vec_e, vec_g))

    wd, wu, wo, wqkv = widen(chunks, [w[k].shape for k in ("wd", "wu", "wo", "wqkv")])
    return (bufs["out"][None], bufs["dh"][None], vec[0:1], vec[1:2], wqkv, wo, vec[2:3], vec[3:4], vec[4:5],
            wu, vec[6:10].reshape(1, -1), wd, vec[5:6])


def solution(mesh):
    matrix, row = P("section", None, None), P("section", None)
    data = P("section", "dp", None, None)
    return jax.shard_map(
        body,
        mesh=mesh,
        in_specs=(data, data, P("dp", None), row, row, matrix, matrix, row, row, row, matrix, row, matrix, row),
        out_specs=(data, data, row, row, matrix, matrix, row, row, row, matrix, row, matrix, row),
        check_vma=False,
    )
```

```python
import functools

import jax
import jax.numpy as jnp
from jax import lax
from jax.experimental import pallas as pl
from jax.experimental.pallas import tpu as pltpu
from jax.sharding import PartitionSpec as P

EPSILON = 1e-05
GELU_C = 0.7978845608028654
MASKED = -1e30
TILE = 512
CHUNK = 512
JOIN = 3
WINDOWS = (128, 160, 192, 256, 272)
LSE_WIDTH = 640
NONE = -4
BF = jnp.bfloat16
F32 = jnp.float32
MESH = pl.DeviceIdType.MESH
ANY = pl.BlockSpec(memory_space=pl.ANY)
VMEM = pl.BlockSpec(memory_space=pltpu.VMEM)
SMEM = pl.BlockSpec(memory_space=pltpu.SMEM)


def dot(a, b):
    return jnp.dot(a, b, preferred_element_type=F32)


def dot_nt(a, b):
    return lax.dot_general(a, b, (((1,), (1,)), ((), ())), preferred_element_type=F32)


def dot_tn(a, b):
    return lax.dot_general(a, b, (((0,), (0,)), ((), ())), preferred_element_type=F32)


def norm_parts(v):
    centred = v - jnp.mean(v, -1, keepdims=True)
    rstd = lax.rsqrt(jnp.mean(centred * centred, -1, keepdims=True) + EPSILON)
    return centred * rstd, rstd


def norm_pull(grad, hat, rstd, gain):
    scaled = grad * gain
    return rstd * (
        scaled
        - jnp.mean(scaled, -1, keepdims=True)
        - hat * jnp.mean(scaled * hat, -1, keepdims=True)
    )


def colsum(v):
    return jnp.sum(v, 0, keepdims=True)


def stack_pair(block):
    lane = lax.broadcasted_iota(jnp.int32, block.shape, 1)
    zero = jnp.zeros_like(block)
    low = lane < 64
    return jnp.concatenate([jnp.where(low, block, zero), jnp.where(low, zero, block)], 0)


def unstack_pair(both):
    rows = both.shape[0] // 2
    lane = lax.broadcasted_iota(jnp.int32, (rows, 128), 1)
    return jnp.where(lane < 64, both[:rows], both[rows:])


def mask_lanes(keep, window):
    lane = lax.broadcasted_iota(jnp.int32, (window, 128), 1)
    mask = jnp.where(keep(128) | (lane > 0), 0.0, MASKED).astype(BF)
    one = jnp.where(lax.broadcasted_iota(jnp.int32, (2 * window, 128), 1) == 0, 1.0, 0.0).astype(BF)
    return mask, one


def tile_rows(t):
    return pl.ds(pl.multiple_of(t * TILE, TILE), TILE)


def for_spans(lengths, row, length, spots, run):
    n_spans = lengths.shape[1]

    def keep_of(window, low, high):
        def keep(width):
            pos = lax.broadcasted_iota(jnp.int32, (window, width), 0)
            return (pos >= low) & (pos < high)

        return keep

    def put(ref, rows, cols, keep, value):
        ref[rows, cols] = jnp.where(keep, value.astype(BF), ref[rows, cols])

    def view(s, first, last, window):
        start = pl.multiple_of(jnp.minimum((first // 16) * 16, length - window), 16)
        rows = pl.ds(start, window)
        keep = keep_of(window, first - start, last - start)
        return (s, lambda ref, cols: ref[rows, cols],
                lambda ref, cols, value: put(ref, rows, cols, keep(128), value), keep)

    def large(s, carry):
        first, small = carry
        last = first + lengths[row, s]
        need = last - (first // 16) * 16
        spots[s] = first
        spots[s + 1] = last

        @pl.when(need <= WINDOWS[0])
        def _():
            spots[n_spans + 1 + small] = s

        for below, window in zip(WINDOWS, WINDOWS[1:]):
            @pl.when((need > below) & (need <= window))
            def _():
                run([view(s, first, last, window)], window)

        return last, small + (need <= WINDOWS[0]).astype(jnp.int32)

    _, count = lax.fori_loop(0, n_spans, large, (jnp.int32(0), jnp.int32(0)))

    def joint(i, carry):
        views = []
        for k in range(JOIN):
            s = spots[n_spans + 1 + jnp.minimum(i * JOIN + k, count - 1)]
            views.append(view(s, spots[s], spots[s + 1], WINDOWS[0]))
        run(views, WINDOWS[0])
        return carry

    lax.fori_loop(0, (count + JOIN - 1) // JOIN, joint, 0)


def pick(pair):
    return pair[0] + lax.axis_index("section") * (pair[1] - pair[0])


def row_kernel(f_rows, b_rows, names, *refs):
    r = dict(zip(names, refs))
    lengths = r["lengths"]
    fused = b_rows[1] >= 0
    with_arr = f_rows[1] >= 0
    v_x = r["v_x"]
    T, D = v_x.shape
    FF = r["w_up"].shape[1]
    n_tiles = T // TILE
    sem_in, sem_out = r["sem_in"], r["sem_out"]
    section = lax.axis_index("section")
    v_proj, v_att, v_slope, v_lse, v_mixed = [r["v_" + k] for k in ("proj", "att", "slope", "lse", "mixed")]
    v_gelu = r.get("v_gelu")
    w_qkv, w_out, w_up, w_down = r["w_qkv"], r["w_out"], r["w_up"], r["w_down"]
    ins, outs = {}, {}

    def load(key, source, target):
        k = ins.setdefault(key, len(ins))
        return pltpu.make_async_copy(source, target, sem_in.at[k])

    def load_tile(key, source, target, t):
        return load((key, t), source.at[tile_rows(t)], target.at[tile_rows(t)])

    def sends(t, pairs):
        rows = tile_rows(t)
        copies = []
        for key, source, target in pairs:
            k = outs.setdefault(key, len(outs))
            copies.append(pltpu.make_async_copy(source.at[rows], target.at[rows], sem_out.at[k, t]))
        return copies

    if "vec" in r:
        r["vec"][...] = jnp.zeros_like(r["vec"])

    def hidden(rows):
        h = v_x[rows, :].astype(F32)
        return h + r["arr"][rows, :].astype(F32) if with_arr else h

    def forward(row):
        c_x = [load_tile("x", r["x"].at[row], v_x, t) for t in range(n_tiles)]
        c_qkv = load("wqkv", r["wqkv"], w_qkv)
        later = [load("wo", r["wo"], w_out), load("wu", r["wu"], w_up), load("wd", r["wd"], w_down)]
        for c in c_x + [c_qkv]:
            c.start()
        for c in later:
            c.start()
        if fused:
            @pl.when(section == 1)
            def _():
                for t in range(n_tiles):
                    load_tile("cot", r["cot"].at[row], r["v_cot"], t).start()
        pairs_a = [("proj", v_proj, r["proj"].at[row])] if f_rows[0] >= 0 else []
        pairs_b = [("out", r["v_out"], r["out"].at[row]), ("gelu", v_gelu, r["gelu"].at[row])]
        pairs_c = []
        if f_rows[0] >= 0:
            pairs_c = [("snd", r["v_out"], r["snd"]), ("att", v_att, r["att"].at[row]), ("slope", v_slope, r["slope"].at[row])]

        def keep_for_encoder(t, pairs, act):
            if pairs:
                @pl.when(section == 0)
                def _():
                    for c in sends(t, pairs):
                        act(c)

        for t in range(n_tiles):
            c_x[t].wait()
            if t == 0:
                c_qkv.wait()
            rows = pl.ds(t * TILE, TILE)
            first = (norm_parts(hidden(rows))[0] * r["n1g"][...] + r["n1b"][...]).astype(BF)
            v_proj[rows, :] = dot(first, w_qkv[...]).astype(BF)
            keep_for_encoder(t, pairs_a, lambda c: c.start())

        def run(views, window):
            n_pairs = D // 128
            eighth = jnp.asarray(0.125, BF)
            q, k, v, score = [], [], [], []
            for span, load, store, keep in views:
                mask, one = mask_lanes(keep, window)
                for p in range(n_pairs):
                    pair_q = stack_pair(load(v_proj, slice(p * 128, p * 128 + 128)) * eighth)
                    pair_k = load(v_proj, slice(D + p * 128, D + p * 128 + 128))
                    v.append(load(v_proj, slice(2 * D + p * 128, 2 * D + p * 128 + 128)))
                    q.append(jnp.concatenate([pair_q, one], 1))
                    k.append(jnp.concatenate([pair_k, mask], 1))
            score = [dot_nt(a, b) for a, b in zip(k, q)]
            raised, sums = [], []
            for i, s in enumerate(score):
                parts, totals, peaks = [], [], []
                for j in range(0, 2 * window, 128):
                    block = s[:, j:min(j + 128, 2 * window)]
                    peak = jnp.max(block, 0, keepdims=True)
                    e = jnp.exp(block - peak)
                    totals.append(jnp.sum(e, 0, keepdims=True))
                    peaks.append(peak)
                    parts.append(e.astype(BF))
                raised.append(jnp.concatenate(parts, 1))
                sums.append(jnp.concatenate(totals, 1))
                at = views[i // n_pairs][0] * n_pairs + i % n_pairs
                v_lse[pl.ds(at, 1), :2 * window] = jnp.concatenate(peaks, 1) + jnp.log(sums[i])
            outs = [dot_tn(a, b) for a, b in zip(v, raised)]
            for i, o in enumerate(outs):
                o = o * (1.0 / sums[i])
                o = jnp.concatenate([o[:64, :window], o[64:, window:]], 0).T
                p = i % n_pairs
                views[i // n_pairs][2](v_mixed, slice(p * 128, p * 128 + 128), o)

        for_spans(lengths, row, T, r["spots"], run)
        c_mixed = pltpu.make_async_copy(v_mixed, r["mixed"].at[row], r["sem_mixed"].at[0])
        c_mixed.start()
        if f_rows[0] >= 0:
            c_lse = pltpu.make_async_copy(v_lse, r["lse"].at[row], r["sem_mixed"].at[1])
            c_lse.start()
        for c in later:
            c.wait()

        def post_tile(t, carry):
            rows = tile_rows(t)
            a = hidden(rows) + dot(v_mixed[rows, :], w_out[...]) + r["bo"][...]
            v_att[rows, :] = a
            second = (norm_parts(a)[0] * r["n2g"][...] + r["n2b"][...]).astype(BF)
            u = dot(second, w_up[...]) + r["bu"][...]
            for c in range(0, FF, CHUNK):
                cc = slice(c, c + CHUNK)
                b = u[:, cc].astype(BF)
                square = b * b
                half = 0.5 + 0.5 * jnp.tanh(b * (GELU_C + (GELU_C * 0.044715) * square))
                v_gelu[rows, cc] = b * half
                rise = b * (2.0 * GELU_C + (6.0 * GELU_C * 0.044715) * square)
                v_slope[rows, cc] = half + (half * (1.0 - half)) * rise
            r["v_out"][rows, :] = (a + r["bd"][...] + dot(v_gelu[rows, :], w_down[...])).astype(BF)
            for c in sends(t, pairs_b):
                c.start()
            keep_for_encoder(t, pairs_c, lambda c: c.start())
            return carry

        lax.fori_loop(0, n_tiles, post_tile, 0)

        def finish():
            c_mixed.wait()
            if f_rows[0] >= 0:
                c_lse.wait()
            for t in range(n_tiles):
                for c in sends(t, pairs_b):
                    c.wait()
                keep_for_encoder(t, pairs_a + pairs_c, lambda c: c.wait())

        return finish

    def backward(row):
        v_cot, v_gl, v_second, v_al = [r["v_" + k] for k in ("cot", "gl", "second", "al")]
        v_da, v_dmix, v_dproj, v_first, v_dh, vec = [r[k] for k in ("v_da", "v_dmix", "v_dproj", "v_first", "v_dh", "vec")]
        if not fused:
            c_wd = load("wd", r["wd"], w_down)
            c_wu = load("wu", r["wu"], w_up)
            c_wo = load("wo", r["wo"], w_out)
            c_att = load("att", r["att"].at[row], v_att)
            late = [load("proj", r["proj"].at[row], v_proj), load("wqkv", r["wqkv"], w_qkv), load("x", r["x"].at[row], v_x),
                    load("mixed", r["mixed"].at[row], v_mixed), load("lse", r["lse"].at[row], v_lse)]

            def tile_loads(t):
                return [load_tile("cot", r["cot"].at[row], v_cot, t), load_tile("slope", r["slope"].at[row], v_slope, t)]

            for c in tile_loads(0) + [c_wd, c_wu, c_att, c_wo]:
                c.start()
            for t in range(1, n_tiles):
                for c in tile_loads(t):
                    c.start()
            for c in late:
                c.start()

        pairs_a = [("gl", v_gl, r["gl"].at[row]), ("ul", v_slope, r["ul"].at[row]),
                   ("second", v_second, r["second"].at[row]), ("al", v_al, r["al"].at[row])]
        pairs_b = [("first", v_first, r["first"].at[row]), ("dproj", v_dproj, r["dproj"].at[row]),
                   ("dh", v_dh, r["dh"].at[row])]
        if fused:
            pairs_b.append(("bsnd", r["v_bsnd"], r["bsnd"]))
        text_end = T - lengths[row, lengths.shape[1] - 1]

        def pre_tile(t):
            rows = pl.ds(t * TILE, TILE)
            if fused:
                load_tile("cot", r["cot"].at[row], v_cot, t).wait()
            else:
                for c in tile_loads(t):
                    c.wait()
                if t == 0:
                    c_wd.wait()
            pos = t * TILE + lax.broadcasted_iota(jnp.int32, (TILE, 1), 0)
            in_text = (pos < text_end).astype(F32)
            g = v_cot[rows, :].astype(F32) * in_text
            if not fused:
                g = g + r["ret"][rows, :].astype(F32)
            g_low = g.astype(BF)
            v_gl[rows, :] = g_low
            vec[5:6, :] += colsum(g)
            back = dot_nt(g_low, w_down[...])
            for c in range(0, FF, CHUNK):
                cc = slice(c, c + CHUNK)
                ug = back[:, cc] * v_slope[rows, cc].astype(F32)
                vec[6 + c // CHUNK:7 + c // CHUNK, :] += colsum(ug)
                v_slope[rows, cc] = ug.astype(BF)
            if not fused and t == 0:
                c_wu.wait()
            sg = dot_nt(v_slope[rows, :], w_up[...])
            if not fused and t == 0:
                c_att.wait()
                c_wo.wait()
            hat, rstd = norm_parts(v_att[rows, :])
            v_second[rows, :] = (hat * r["n2g"][...] + r["n2b"][...]).astype(BF)
            vec[3:4, :] += colsum(sg * hat)
            vec[4:5, :] += colsum(sg)
            a = g + norm_pull(sg, hat, rstd, r["n2g"][...])
            vec[2:3, :] += colsum(a)
            v_da[rows, :] = a
            a_low = a.astype(BF)
            v_al[rows, :] = a_low
            v_dmix[rows, :] = dot_nt(a_low, w_out[...]).astype(BF)
            for c in sends(t, pairs_a):
                c.start()

        for t in range(n_tiles):
            pre_tile(t)
        if not fused:
            for c in (late[0], late[3], late[4]):
                c.wait()

        def run(views, window):
            n_pairs = D // 128
            chains = range(len(views) * n_pairs)
            zero = jnp.zeros((window, 128), BF)
            eighth = jnp.asarray(0.125, BF)
            lane = lax.broadcasted_iota(jnp.int32, (8, 128), 1)
            head = lax.broadcasted_iota(jnp.int32, (8, 128), 0)
            half_sum = jnp.where(lane // 64 == head, 1.0, 0.0).astype(BF)

            def cols(third, i):
                p = i % n_pairs
                return slice(third * D + p * 128, third * D + p * 128 + 128)

            def load(i, ref, third):
                return views[i // n_pairs][1](ref, cols(third, i))

            extra = [mask_lanes(keep, window) for _, _, _, keep in views]
            q = [stack_pair(load(i, v_proj, 0) * eighth) for i in chains]
            k = [load(i, v_proj, 1) for i in chains]
            v = [load(i, v_proj, 2) for i in chains]
            pulled = [jnp.where(views[i // n_pairs][3](128), load(i, v_dmix, 0), zero) for i in chains]
            do = [stack_pair(d) for d in pulled]
            score = [dot_nt(jnp.concatenate([k[i], extra[i // n_pairs][0]], 1),
                            jnp.concatenate([q[i], extra[i // n_pairs][1]], 1)) for i in chains]
            pulls = [dot_nt(v[i], do[i]) for i in chains]
            inner = []
            for i in chains:
                product = pulled[i].astype(F32) * load(i, v_mixed, 0).astype(F32)
                high = product.astype(BF)
                both = dot_nt(half_sum, high) + dot_nt(half_sum, (product - high.astype(F32)).astype(BF))
                inner.append(jnp.concatenate([both[0:1], both[1:2]], 1))

            def soft(i):
                prob_parts, ds_parts = [], []
                lse = v_lse[pl.ds(views[i // n_pairs][0] * n_pairs + i % n_pairs, 1), :2 * window]
                for j in range(0, 2 * window, 128):
                    part = slice(j, min(j + 128, 2 * window))
                    prob = jnp.exp(score[i][:, part] - lse[:, part])
                    ds_parts.append((prob * (pulls[i][:, part] - inner[i][:, part])).astype(BF))
                    prob_parts.append(prob.astype(BF))
                return jnp.concatenate(prob_parts, 1), jnp.concatenate(ds_parts, 1)

            def mix(i, prob, push):
                store = views[i // n_pairs][2]
                store(v_dproj, cols(2, i), dot(prob, do[i]))
                store(v_dproj, cols(1, i), dot(push, q[i]))
                dq = dot_tn(k[i] * eighth, push)
                store(v_dproj, cols(0, i), jnp.concatenate([dq[:64, :window], dq[64:, window:]], 0).T)

            ahead = soft(0)
            for i in chains:
                now = ahead
                if i + 1 < len(chains):
                    ahead = soft(i + 1)
                mix(i, *now)

        for_spans(lengths, row, T, r["spots"], run)
        if not fused:
            late[1].wait()
            late[2].wait()

        def fin_tile(t, carry):
            rows = tile_rows(t)
            fg = dot_nt(v_dproj[rows, :], w_qkv[...])
            hat, rstd = norm_parts(hidden(rows))
            v_first[rows, :] = (hat * r["n1g"][...] + r["n1b"][...]).astype(BF)
            vec[0:1, :] += colsum(fg * hat)
            vec[1:2, :] += colsum(fg)
            d = v_da[rows, :] + norm_pull(fg, hat, rstd, r["n1g"][...])
            v_dh[rows, :] = d
            if fused:
                r["v_bsnd"][rows, :] = d.astype(BF)
            for c in sends(t, pairs_b):
                c.start()
            return carry

        lax.fori_loop(0, n_tiles, fin_tile, 0)
        for t in range(n_tiles):
            for c in sends(t, pairs_a) + sends(t, pairs_b):
                c.wait()

    if f_rows != (NONE, NONE):
        f_row = pick(f_rows)

        @pl.when(f_row >= 0)
        def _():
            finish = forward(f_row)
            if fused:
                @pl.when(section == 1)
                def _():
                    backward(f_row)
            finish()
    else:
        b_row = pick(b_rows)

        @pl.when(b_row >= 0)
        def _():
            backward(b_row)


def row_slot(f_rows, b_rows, lengths, x, cot, arr, ret, w, bufs):
    n, T, D = x.shape
    FF = w["wu"].shape[1]
    S, V = jax.ShapeDtypeStruct, pltpu.VMEM
    does_f, does_b = max(f_rows) >= 0, max(b_rows) >= 0
    saves = f_rows[0] >= 0
    fused = b_rows[1] >= 0
    ins = {"lengths": (lengths, SMEM), "x": (x, ANY)}
    if does_b:
        ins["cot"] = (cot, ANY)
    if arr is not None:
        ins["arr"] = (arr, VMEM)
    if ret is not None:
        ins["ret"] = (ret, VMEM)
        ins.update({k: (bufs[k], ANY) for k in ("proj", "att", "slope", "mixed", "lse")})
    ins.update({k: (w[k], ANY) for k in ("wqkv", "wo", "wu", "wd")})
    ins.update({k: (w[k], VMEM) for k in ("n1g", "n1b", "bo", "n2g", "n2b", "bu", "bd")})
    wide = {"out": (D, BF), "mixed": (D, BF), "proj": (3 * D, BF), "att": (D, F32), "slope": (FF, BF), "dh": (D, F32),
            "first": (D, BF), "dproj": (3 * D, BF), "al": (D, BF), "second": (D, BF), "ul": (FF, BF), "gelu": (FF, BF),
            "gl": (D, BF)}
    keys = (["out", "mixed", "gelu"] if does_f else []) + (["proj", "att", "slope", "lse"] if saves else [])
    if does_b:
        keys += ["dh", "first", "dproj", "al", "second", "ul", "gl"]
    spans = lengths.shape[1] * D // 128
    outs = {k: (S((n, T, wide[k][0]), wide[k][1]) if k in wide else S((n, spans, LSE_WIDTH), F32), ANY) for k in keys}
    if saves:
        outs["snd"] = (S((T, D), BF), ANY)
    if fused:
        outs["bsnd"] = (S((T, D), BF), ANY)
    if does_b:
        outs["vec"] = (S((16, CHUNK), F32), VMEM)
    alias = [k for k in keys if k in bufs]
    scratch = {"v_x": V((T, D), BF), "w_qkv": V((D, 3 * D), BF), "w_out": V((D, D), BF), "w_up": V((D, FF), BF),
               "w_down": V((FF, D), BF), "v_proj": V((T, 3 * D), BF), "v_att": V((T, D), F32), "v_slope": V((T, FF), BF),
               "v_lse": V((spans, LSE_WIDTH), F32), "v_mixed": V((T, D), BF)}
    if does_f:
        scratch.update({"v_out": V((T, D), BF), "v_gelu": V((T, FF), BF)})
    if does_b:
        scratch.update({"v_" + k: V((T, wide[k][0]), wide[k][1])
                        for k in ("dh", "first", "dproj", "al", "second", "gl")})
        scratch.update({"v_cot": V((T, D), BF), "v_dmix": V((T, D), BF), "v_da": V((T, D), F32)})
    if fused:
        scratch["v_bsnd"] = V((T, D), BF)
    scratch.update({"sem_in": pltpu.SemaphoreType.DMA((24,)), "sem_out": pltpu.SemaphoreType.DMA((18, T // TILE)),
                    "spots": pltpu.SMEM((2 * lengths.shape[1] + 2,), jnp.int32), "sem_mixed": pltpu.SemaphoreType.DMA((2,))})
    names = list(ins) + ["alias_" + k for k in alias] + list(outs) + list(scratch)
    values = [v for v, _ in ins.values()] + [bufs[k] for k in alias]
    results = pl.pallas_call(
        functools.partial(row_kernel, f_rows, b_rows, names),
        out_shape=[o for o, _ in outs.values()],
        in_specs=[m for _, m in ins.values()] + [ANY] * len(alias),
        out_specs=[m for _, m in outs.values()],
        input_output_aliases={len(ins) + i: list(outs).index(k) for i, k in enumerate(alias)},
        scratch_shapes=list(scratch.values()),
        compiler_params=pltpu.CompilerParams(vmem_limit_bytes=(48 if does_b else 60) * 2**20),
        cost_estimate=pl.CostEstimate(flops=8 * 10**9 * does_f + 14 * 10**9 * does_b, bytes_accessed=20 * 2**20,
                                      transcendentals=0),
        name="row_" + "f" * does_f + "b" * does_b,
    )(*values)
    got = dict(zip(outs, results))
    send = (got.get("snd"), got.get("bsnd"))
    if None in send:
        send = send[0] if send[1] is None else send[1]
    return {**bufs, **{k: got[k] for k in keys}}, send, got.get("vec")


def reduce_kernel(n, *refs):
    bits = n.bit_length() - 1
    (gelu_any, gl_any, second_any, ul_any, mixed_any, al_any, first_any, dproj_any, vec_a, vec_b, vec_c, vec_d) = refs[:12]
    result, vec_out = refs[12:14]
    left, right, total, final, *rest = refs[14:]
    inbox = rest[:bits]
    (vec_box, vec_tmp, sem_load, sem_store, rs_send, rs_recv, ag_send, ag_recv, vec_send, vec_recv) = rest[bits:]
    n_chunks = total.shape[0]
    FF = gelu_any.shape[2]
    D = gl_any.shape[2]
    T = gl_any.shape[1]
    rows = gl_any.shape[0]
    ff_chunks = FF // CHUNK
    me = lax.axis_index("dp")
    size = total.shape[1]
    value = [(me // 2**b) % 2 for b in range(bits)]
    partner = [me + (1 - 2 * value[b]) * 2**b for b in range(bits)]
    base = [sum(value[i] * (size >> (i + 1)) for i in range(b)) for b in range(bits + 1)]

    def halve(c, b):
        half = size >> (b + 1)
        away = pl.multiple_of(base[b] + (1 - value[b]) * half, half)
        return pltpu.make_async_remote_copy(
            src_ref=total.at[c, pl.ds(away, half)], dst_ref=inbox[b].at[c],
            send_sem=rs_send.at[c, b], recv_sem=rs_recv.at[c, b],
            device_id={"dp": partner[b]}, device_id_type=MESH,
        )

    def double(c, b):
        half = size >> (b + 1)
        here = final.at[c, pl.ds(pl.multiple_of(base[b + 1], half), half)]
        return pltpu.make_async_remote_copy(
            src_ref=here, dst_ref=here,
            send_sem=ag_send.at[c, b], recv_sem=ag_recv.at[c, b],
            device_id={"dp": partner[b]}, device_id_type=MESH,
        )

    def add_in(c, b):
        half = size >> (b + 1)
        mine = pl.ds(pl.multiple_of(base[b + 1], half), half)
        target = total if b + 1 < bits else final
        target[c, mine, :] = (total[c, mine, :].astype(F32) + inbox[b][c].astype(F32)).astype(BF)

    def load(c, slot, act):
        def both(a, b):
            for k, (source, target) in enumerate(((a, left), (b, right))):
                act(pltpu.make_async_copy(source, target.at[slot], sem_load.at[k, slot]))

        def cols(ref, j):
            return ref.at[:, :, pl.ds(pl.multiple_of(j * CHUNK, CHUNK), CHUNK)]

        @pl.when(c < ff_chunks)
        def _():
            both(cols(gelu_any, c), gl_any)

        @pl.when((c >= ff_chunks) & (c < 2 * ff_chunks))
        def _():
            both(second_any, cols(ul_any, c - ff_chunks))

        @pl.when(c == 2 * ff_chunks)
        def _():
            both(mixed_any, al_any)

        @pl.when((c > 2 * ff_chunks) & (c < n_chunks))
        def _():
            both(first_any, cols(dproj_any, c - 2 * ff_chunks - 1))

    def publish(c):
        return pltpu.make_async_copy(final.at[c], result.at[c], sem_store.at[c])

    def vec_copy(b):
        return pltpu.make_async_remote_copy(
            src_ref=vec_tmp.at[b], dst_ref=vec_box.at[b],
            send_sem=vec_send.at[b], recv_sem=vec_recv.at[b],
            device_id={"dp": partner[b]}, device_id_type=MESH,
        )

    load(jnp.int32(0), 0, lambda c: c.start())
    vec_tmp[0] = vec_a[...] + vec_b[...] + vec_c[...] + vec_d[...]
    barrier = pltpu.get_barrier_semaphore()
    for b in range(bits):
        pl.semaphore_signal(barrier, inc=1, device_id={"dp": partner[b]}, device_id_type=MESH)
    pl.semaphore_wait(barrier, bits)
    vec_copy(0).start()

    gaps = [1, 2] + [1 + b % 2 for b in range(2, bits)]
    lags = [0]
    for gap in gaps[:bits] + gaps[bits - 1::-1]:
        lags.append(lags[-1] + gap)

    def slot_step(t, carry):
        def stage_of(lag, act):
            c = t - lag

            @pl.when((c >= 0) & (c < n_chunks))
            def _():
                act(c)

        def make(c):
            slot = lax.rem(c, 2)
            load(c + 1, 1 - slot, lambda d: d.start())
            load(c, slot, lambda d: d.wait())
            a = left[slot].reshape(rows * T, CHUNK)
            b = right[slot].reshape(rows * T, CHUNK)
            total[c] = dot_tn(a, b).astype(BF)
            halve(c, 0).start()

        def reduce_step(b):
            def act(c):
                halve(c, b).wait()
                add_in(c, b)
                if b + 1 < bits:
                    halve(c, b + 1).start()
                else:
                    double(c, b).start()
            return act

        def gather_step(b):
            def act(c):
                double(c, b).wait()
                double(c, b - 1).start()
            return act

        def finish(c):
            double(c, 0).wait()
            publish(c).start()

        acts = [make] + [reduce_step(b) for b in range(bits)] + [gather_step(b) for b in range(bits - 1, 0, -1)] + [finish]
        for lag, act in zip(lags, acts):
            stage_of(lag, act)
        return carry

    lax.fori_loop(0, n_chunks + lags[-1], slot_step, 0)
    for b in range(bits):
        vec_copy(b).wait()
        merged = vec_tmp[b] + vec_box[b]
        if b + 1 < bits:
            vec_tmp[b + 1] = merged
            vec_copy(b + 1).start()
        else:
            vec_out[...] = merged
    for c in range(n_chunks):
        publish(c).wait()


def wide_kernel(chunks, vec, wd, wu, wo, wqkv, n1g, n1b, bo, n2g, n2b, bd, bu, held, stage, sem_in, sem):
    blocks = [(w, r, c) for w in (wd, wu, wo, wqkv) for r in range(0, w.shape[1], CHUNK) for c in range(0, w.shape[2], CHUNK)]
    loads = [pltpu.make_async_copy(chunks.at[k], held.at[k], sem_in.at[k]) for k in range(len(blocks))]
    for c in loads:
        c.start()
    for i, small in enumerate((n1g, n1b, bo, n2g, n2b, bd)):
        small[...] = vec[i:i + 1, :]
    for i in range(bu.shape[1] // CHUNK):
        bu[:, i * CHUNK:(i + 1) * CHUNK] = vec[6 + i:7 + i, :]
    copies = []
    for k, (w, r, c) in enumerate(blocks):
        loads[k].wait()
        stage[k] = held[k].astype(F32)
        copies.append(pltpu.make_async_copy(stage.at[k], w.at[0, pl.ds(r, CHUNK), pl.ds(c, CHUNK)], sem.at[k]))
        copies[k].start()
    for c in copies:
        c.wait()


def widen(chunks, vec, shapes, small_shapes):
    n = chunks.shape[0]
    return pl.pallas_call(
        wide_kernel,
        out_shape=[jax.ShapeDtypeStruct(shape, F32) for shape in [(1, *s) for s in shapes] + small_shapes],
        in_specs=[ANY, VMEM],
        out_specs=[ANY] * len(shapes) + [VMEM] * len(small_shapes),
        scratch_shapes=[pltpu.VMEM(chunks.shape, BF), pltpu.VMEM(chunks.shape, F32),
                        pltpu.SemaphoreType.DMA((n,)), pltpu.SemaphoreType.DMA((n,))],
        compiler_params=pltpu.CompilerParams(vmem_limit_bytes=60 * 2**20),
        name="widen",
    )(chunks, vec)


def weight_grads(n, bufs, vecs):
    gl, ul = bufs["gl"], bufs["ul"]
    rows, T, D = gl.shape
    FF = ul.shape[2]
    bits = n.bit_length() - 1
    n_chunks = 2 * (FF // CHUNK) + 1 + 3 * D // CHUNK
    size = CHUNK
    S, V, DMA = jax.ShapeDtypeStruct, pltpu.VMEM, pltpu.SemaphoreType.DMA
    return pl.pallas_call(
        functools.partial(reduce_kernel, n),
        out_shape=[S((n_chunks, CHUNK, CHUNK), BF), S((16, CHUNK), F32)],
        in_specs=[ANY] * 8 + [VMEM] * 4,
        out_specs=[ANY, VMEM],
        scratch_shapes=[
            V((2, rows, T, CHUNK), BF), V((2, rows, T, CHUNK), BF), V((n_chunks, size, CHUNK), BF),
            V((n_chunks, size, CHUNK), BF),
            *[V((n_chunks, size >> (b + 1), CHUNK), BF) for b in range(bits)],
            V((bits, 16, CHUNK), F32), V((bits, 16, CHUNK), F32),
            DMA((2, 2)), DMA((n_chunks,)), DMA((n_chunks, bits)), DMA((n_chunks, bits)), DMA((n_chunks, bits)),
            DMA((n_chunks, bits)), DMA((bits,)), DMA((bits,)),
        ],
        compiler_params=pltpu.CompilerParams(vmem_limit_bytes=62 * 2**20, collective_id=0, has_side_effects=True),
        cost_estimate=pl.CostEstimate(flops=13 * 10**9, bytes_accessed=60 * 2**20, transcendentals=0),
        name="weight_grads",
    )(*[bufs[k] for k in ("gelu", "gl", "second", "ul", "mixed", "al", "first", "dproj")], *vecs)


def body(inputs, cotangent, lengths, norm1_gain, norm1_bias, weight_qkv, weight_out, bias_out, norm2_gain, norm2_bias,
         weight_up, bias_up, weight_down, bias_down):
    w = dict(n1g=norm1_gain, n1b=norm1_bias, wqkv=weight_qkv[0], wo=weight_out[0], bo=bias_out, n2g=norm2_gain,
             n2b=norm2_bias, wu=weight_up[0], bu=bias_up, wd=weight_down[0], bd=bias_down)
    x, cot = inputs[0], cotangent[0]
    n = lax.axis_size("dp")

    def ahead(block):
        return lax.ppermute(block, "section", [(0, 1)])

    def back(block):
        return lax.ppermute(block, "section", [(1, 0)])

    bufs, send_a, _ = row_slot((0, NONE), (NONE, NONE), lengths, x, cot, None, None, w, {})
    row_0 = ahead(send_a)
    bufs, send_b, _ = row_slot((1, NONE), (NONE, NONE), lengths, x, cot, None, None, w, bufs)
    row_1 = ahead(send_b)
    bufs, back_b, vec_b = row_slot((NONE, 0), (NONE, 0), lengths, x, cot, row_0, None, w, bufs)
    ret_0 = back(back_b)
    bufs, back_d, vec_d = row_slot((NONE, 1), (NONE, 1), lengths, x, cot, row_1, None, w, bufs)
    ret_1 = back(back_d)
    bufs, _, vec_e = row_slot((NONE, NONE), (0, NONE), lengths, x, cot, None, ret_0, w, bufs)
    bufs, _, vec_g = row_slot((NONE, NONE), (1, NONE), lengths, x, cot, None, ret_1, w, bufs)
    chunks, vec = weight_grads(n, bufs, (vec_b, vec_d, vec_e, vec_g))

    matrices, small = ("wd", "wu", "wo", "wqkv"), ("n1g", "n1b", "bo", "n2g", "n2b", "bd", "bu")
    g = dict(zip(matrices + small, widen(chunks, vec, [w[k].shape for k in matrices], [w[k].shape for k in small])))
    order = ("n1g", "n1b", "wqkv", "wo", "bo", "n2g", "n2b", "wu", "bu", "wd", "bd")
    return (bufs["out"][None], bufs["dh"][None], *[g[k] for k in order])


def solution(mesh):
    matrix, row = P("section", None, None), P("section", None)
    data = P("section", "dp", None, None)
    return jax.shard_map(
        body,
        mesh=mesh,
        in_specs=(data, data, P("dp", None), row, row, matrix, matrix, row, row, row, matrix, row, matrix, row),
        out_specs=(data, data, row, row, matrix, matrix, row, row, row, matrix, row, matrix, row),
        check_vma=False,
    )
```

```python
import functools

import jax
import jax.numpy as jnp
from jax import lax
from jax.experimental import pallas as pl
from jax.experimental.pallas import tpu as pltpu
from jax.sharding import PartitionSpec as P

EPSILON = 1e-05
GELU_C = 0.7978845608028654
MASKED = -1e30
TILE = 512
CHUNK = 512
JOIN = 3
WINDOWS = (128, 160, 192, 224, 256, 272)
LSE_WIDTH = 640
NONE = -4
BF = jnp.bfloat16
F32 = jnp.float32
MESH = pl.DeviceIdType.MESH
ANY = pl.BlockSpec(memory_space=pl.ANY)
VMEM = pl.BlockSpec(memory_space=pltpu.VMEM)
SMEM = pl.BlockSpec(memory_space=pltpu.SMEM)


def dot(a, b):
    return jnp.dot(a, b, preferred_element_type=F32)


def dot_nt(a, b):
    return lax.dot_general(a, b, (((1,), (1,)), ((), ())), preferred_element_type=F32)


def dot_tn(a, b):
    return lax.dot_general(a, b, (((0,), (0,)), ((), ())), preferred_element_type=F32)


def norm_parts(v):
    centred = v - jnp.mean(v, -1, keepdims=True)
    rstd = lax.rsqrt(jnp.mean(centred * centred, -1, keepdims=True) + EPSILON)
    return centred * rstd, rstd


def norm_pull(grad, hat, rstd, gain):
    scaled = grad * gain
    return rstd * (
        scaled
        - jnp.mean(scaled, -1, keepdims=True)
        - hat * jnp.mean(scaled * hat, -1, keepdims=True)
    )


def colsum(v):
    return jnp.sum(v, 0, keepdims=True)


def stack_pair(block):
    lane = lax.broadcasted_iota(jnp.int32, block.shape, 1)
    zero = jnp.zeros_like(block)
    low = lane < 64
    return jnp.concatenate([jnp.where(low, block, zero), jnp.where(low, zero, block)], 0)


def unstack_pair(both):
    rows = both.shape[0] // 2
    lane = lax.broadcasted_iota(jnp.int32, (rows, 128), 1)
    return jnp.where(lane < 64, both[:rows], both[rows:])


def mask_lanes(keep, window):
    lane = lax.broadcasted_iota(jnp.int32, (window, 128), 1)
    mask = jnp.where(keep(128) | (lane > 0), 0.0, MASKED).astype(BF)
    one = jnp.where(lax.broadcasted_iota(jnp.int32, (2 * window, 128), 1) == 0, 1.0, 0.0).astype(BF)
    return mask, one


def tile_rows(t):
    return pl.ds(pl.multiple_of(t * TILE, TILE), TILE)


def for_spans(lengths, row, length, spots, run):
    n_spans = lengths.shape[1]

    def keep_of(window, low, high):
        def keep(width):
            pos = lax.broadcasted_iota(jnp.int32, (window, width), 0)
            return (pos >= low) & (pos < high)

        return keep

    def put(ref, rows, cols, keep, value):
        ref[rows, cols] = jnp.where(keep, value.astype(BF), ref[rows, cols])

    def view(s, first, last, window):
        start = pl.multiple_of(jnp.minimum((first // 16) * 16, length - window), 16)
        rows = pl.ds(start, window)
        keep = keep_of(window, first - start, last - start)
        return (s, lambda ref, cols: ref[rows, cols],
                lambda ref, cols, value: put(ref, rows, cols, keep(128), value), keep)

    def large(s, carry):
        first, small = carry
        last = first + lengths[row, s]
        need = last - (first // 16) * 16
        spots[s] = first
        spots[s + 1] = last

        @pl.when(need <= WINDOWS[0])
        def _():
            spots[n_spans + 1 + small] = s

        for below, window in zip(WINDOWS, WINDOWS[1:]):
            @pl.when((need > below) & (need <= window))
            def _():
                run([view(s, first, last, window)], window)

        return last, small + (need <= WINDOWS[0]).astype(jnp.int32)

    _, count = lax.fori_loop(0, n_spans, large, (jnp.int32(0), jnp.int32(0)))

    def joint(i, carry):
        views = []
        for k in range(JOIN):
            s = spots[n_spans + 1 + jnp.minimum(i * JOIN + k, count - 1)]
            views.append(view(s, spots[s], spots[s + 1], WINDOWS[0]))
        run(views, WINDOWS[0])
        return carry

    lax.fori_loop(0, (count + JOIN - 1) // JOIN, joint, 0)


def pick(pair):
    return pair[0] + lax.axis_index("section") * (pair[1] - pair[0])


def row_kernel(f_rows, b_rows, names, *refs):
    r = dict(zip(names, refs))
    lengths = r["lengths"]
    fused = b_rows[1] >= 0
    with_arr = f_rows[1] >= 0
    v_x = r["v_x"]
    T, D = v_x.shape
    FF = r["w_up"].shape[1]
    n_tiles = T // TILE
    sem_in, sem_out = r["sem_in"], r["sem_out"]
    section = lax.axis_index("section")
    v_proj, v_att, v_slope, v_lse, v_mixed = [r["v_" + k] for k in ("proj", "att", "slope", "lse", "mixed")]
    v_gelu = r.get("v_gelu")
    w_qkv, w_out, w_up, w_down = r["w_qkv"], r["w_out"], r["w_up"], r["w_down"]
    ins, outs = {}, {}

    def load(key, source, target):
        k = ins.setdefault(key, len(ins))
        return pltpu.make_async_copy(source, target, sem_in.at[k])

    def load_tile(key, source, target, t):
        return load((key, t), source.at[tile_rows(t)], target.at[tile_rows(t)])

    def sends(t, pairs):
        rows = tile_rows(t)
        copies = []
        for key, source, target in pairs:
            k = outs.setdefault(key, len(outs))
            copies.append(pltpu.make_async_copy(source.at[rows], target.at[rows], sem_out.at[k, t]))
        return copies

    if "vec" in r:
        r["vec"][...] = jnp.zeros_like(r["vec"])

    def hidden(rows):
        h = v_x[rows, :].astype(F32)
        return h + r["arr"][rows, :].astype(F32) if with_arr else h

    def forward(row):
        c_x = [load_tile("x", r["x"].at[row], v_x, t) for t in range(n_tiles)]
        c_qkv = load("wqkv", r["wqkv"], w_qkv)
        later = [load("wo", r["wo"], w_out), load("wu", r["wu"], w_up), load("wd", r["wd"], w_down)]
        for c in c_x + [c_qkv]:
            c.start()
        for c in later:
            c.start()
        if fused:
            @pl.when(section == 1)
            def _():
                for t in range(n_tiles):
                    load_tile("cot", r["cot"].at[row], r["v_cot"], t).start()
        pairs_a = [("proj", v_proj, r["proj"].at[row])] if f_rows[0] >= 0 else []
        pairs_b = [("out", r["v_out"], r["out"].at[row]), ("gelu", v_gelu, r["gelu"].at[row])]
        pairs_c = []
        if f_rows[0] >= 0:
            pairs_c = [("snd", r["v_out"], r["snd"]), ("att", v_att, r["att"].at[row]), ("slope", v_slope, r["slope"].at[row])]

        def keep_for_encoder(t, pairs, act):
            if pairs:
                @pl.when(section == 0)
                def _():
                    for c in sends(t, pairs):
                        act(c)

        for t in range(n_tiles):
            c_x[t].wait()
            if t == 0:
                c_qkv.wait()
            rows = pl.ds(t * TILE, TILE)
            first = (norm_parts(hidden(rows))[0] * r["n1g"][...] + r["n1b"][...]).astype(BF)
            v_proj[rows, :] = dot(first, w_qkv[...]).astype(BF)
            keep_for_encoder(t, pairs_a, lambda c: c.start())

        def run(views, window):
            n_pairs = D // 128
            eighth = jnp.asarray(0.125, BF)
            q, k, v, score = [], [], [], []
            for span, load, store, keep in views:
                mask, one = mask_lanes(keep, window)
                for p in range(n_pairs):
                    pair_q = stack_pair(load(v_proj, slice(p * 128, p * 128 + 128)) * eighth)
                    pair_k = load(v_proj, slice(D + p * 128, D + p * 128 + 128))
                    v.append(load(v_proj, slice(2 * D + p * 128, 2 * D + p * 128 + 128)))
                    q.append(jnp.concatenate([pair_q, one], 1))
                    k.append(jnp.concatenate([pair_k, mask], 1))
            score = [dot_nt(a, b) for a, b in zip(k, q)]
            raised, sums = [], []
            for i, s in enumerate(score):
                parts, totals, peaks = [], [], []
                for j in range(0, 2 * window, 128):
                    block = s[:, j:min(j + 128, 2 * window)]
                    peak = jnp.max(block, 0, keepdims=True)
                    e = jnp.exp(block - peak)
                    totals.append(jnp.sum(e, 0, keepdims=True))
                    peaks.append(peak)
                    parts.append(e.astype(BF))
                raised.append(jnp.concatenate(parts, 1))
                sums.append(jnp.concatenate(totals, 1))
                at = views[i // n_pairs][0] * n_pairs + i % n_pairs
                v_lse[pl.ds(at, 1), :2 * window] = jnp.concatenate(peaks, 1) + jnp.log(sums[i])
            outs = [dot_tn(a, b) for a, b in zip(v, raised)]
            for i, o in enumerate(outs):
                o = o * (1.0 / sums[i])
                o = jnp.concatenate([o[:64, :window], o[64:, window:]], 0).T
                p = i % n_pairs
                views[i // n_pairs][2](v_mixed, slice(p * 128, p * 128 + 128), o)

        for_spans(lengths, row, T, r["spots"], run)
        c_mixed = pltpu.make_async_copy(v_mixed, r["mixed"].at[row], r["sem_mixed"].at[0])
        c_mixed.start()
        if f_rows[0] >= 0:
            c_lse = pltpu.make_async_copy(v_lse, r["lse"].at[row], r["sem_mixed"].at[1])
            c_lse.start()
        for c in later:
            c.wait()

        def post_tile(t, carry):
            rows = tile_rows(t)
            a = hidden(rows) + dot(v_mixed[rows, :], w_out[...]) + r["bo"][...]
            v_att[rows, :] = a
            second = (norm_parts(a)[0] * r["n2g"][...] + r["n2b"][...]).astype(BF)
            u = dot(second, w_up[...]) + r["bu"][...]
            for c in range(0, FF, CHUNK):
                cc = slice(c, c + CHUNK)
                b = u[:, cc].astype(BF)
                square = b * b
                half = 0.5 + 0.5 * jnp.tanh(b * (GELU_C + (GELU_C * 0.044715) * square))
                v_gelu[rows, cc] = b * half
                rise = b * (2.0 * GELU_C + (6.0 * GELU_C * 0.044715) * square)
                v_slope[rows, cc] = half + (half * (1.0 - half)) * rise
            r["v_out"][rows, :] = (a + r["bd"][...] + dot(v_gelu[rows, :], w_down[...])).astype(BF)
            for c in sends(t, pairs_b):
                c.start()
            keep_for_encoder(t, pairs_c, lambda c: c.start())
            return carry

        lax.fori_loop(0, n_tiles, post_tile, 0)

        def finish():
            c_mixed.wait()
            if f_rows[0] >= 0:
                c_lse.wait()
            for t in range(n_tiles):
                for c in sends(t, pairs_b):
                    c.wait()
                keep_for_encoder(t, pairs_a + pairs_c, lambda c: c.wait())

        return finish

    def backward(row):
        v_cot, v_gl, v_second, v_al = [r["v_" + k] for k in ("cot", "gl", "second", "al")]
        v_da, v_dmix, v_dproj, v_first, v_dh, vec = [r[k] for k in ("v_da", "v_dmix", "v_dproj", "v_first", "v_dh", "vec")]
        if not fused:
            c_wd = load("wd", r["wd"], w_down)
            c_wu = load("wu", r["wu"], w_up)
            c_wo = load("wo", r["wo"], w_out)
            c_att = load("att", r["att"].at[row], v_att)
            late = [load("proj", r["proj"].at[row], v_proj), load("wqkv", r["wqkv"], w_qkv), load("x", r["x"].at[row], v_x),
                    load("mixed", r["mixed"].at[row], v_mixed), load("lse", r["lse"].at[row], v_lse)]

            def tile_loads(t):
                return [load_tile("cot", r["cot"].at[row], v_cot, t), load_tile("slope", r["slope"].at[row], v_slope, t)]

            for c in tile_loads(0) + [c_wd, c_wu, c_att, c_wo]:
                c.start()
            for t in range(1, n_tiles):
                for c in tile_loads(t):
                    c.start()
            for c in late:
                c.start()

        pairs_a = [("gl", v_gl, r["gl"].at[row]), ("ul", v_slope, r["ul"].at[row]),
                   ("second", v_second, r["second"].at[row]), ("al", v_al, r["al"].at[row])]
        pairs_b = [("first", v_first, r["first"].at[row]), ("dproj", v_dproj, r["dproj"].at[row]),
                   ("dh", v_dh, r["dh"].at[row])]
        if fused:
            pairs_b.append(("bsnd", r["v_bsnd"], r["bsnd"]))
        text_end = T - lengths[row, lengths.shape[1] - 1]

        def pre_tile(t):
            rows = pl.ds(t * TILE, TILE)
            if fused:
                load_tile("cot", r["cot"].at[row], v_cot, t).wait()
            else:
                for c in tile_loads(t):
                    c.wait()
                if t == 0:
                    c_wd.wait()
            pos = t * TILE + lax.broadcasted_iota(jnp.int32, (TILE, 1), 0)
            in_text = (pos < text_end).astype(F32)
            g = v_cot[rows, :].astype(F32) * in_text
            if not fused:
                g = g + r["ret"][rows, :].astype(F32)
            g_low = g.astype(BF)
            v_gl[rows, :] = g_low
            vec[5:6, :] += colsum(g)
            back = dot_nt(g_low, w_down[...])
            for c in range(0, FF, CHUNK):
                cc = slice(c, c + CHUNK)
                ug = back[:, cc] * v_slope[rows, cc].astype(F32)
                vec[6 + c // CHUNK:7 + c // CHUNK, :] += colsum(ug)
                v_slope[rows, cc] = ug.astype(BF)
            if not fused and t == 0:
                c_wu.wait()
            sg = dot_nt(v_slope[rows, :], w_up[...])
            if not fused and t == 0:
                c_att.wait()
                c_wo.wait()
            hat, rstd = norm_parts(v_att[rows, :])
            v_second[rows, :] = (hat * r["n2g"][...] + r["n2b"][...]).astype(BF)
            vec[3:4, :] += colsum(sg * hat)
            vec[4:5, :] += colsum(sg)
            a = g + norm_pull(sg, hat, rstd, r["n2g"][...])
            vec[2:3, :] += colsum(a)
            v_da[rows, :] = a
            a_low = a.astype(BF)
            v_al[rows, :] = a_low
            v_dmix[rows, :] = dot_nt(a_low, w_out[...]).astype(BF)
            for c in sends(t, pairs_a):
                c.start()

        for t in range(n_tiles):
            pre_tile(t)
        if not fused:
            for c in (late[0], late[3], late[4]):
                c.wait()

        def run(views, window):
            n_pairs = D // 128
            chains = range(len(views) * n_pairs)
            zero = jnp.zeros((window, 128), BF)
            eighth = jnp.asarray(0.125, BF)
            lane = lax.broadcasted_iota(jnp.int32, (8, 128), 1)
            head = lax.broadcasted_iota(jnp.int32, (8, 128), 0)
            half_sum = jnp.where(lane // 64 == head, 1.0, 0.0).astype(BF)

            def cols(third, i):
                p = i % n_pairs
                return slice(third * D + p * 128, third * D + p * 128 + 128)

            def load(i, ref, third):
                return views[i // n_pairs][1](ref, cols(third, i))

            extra = [mask_lanes(keep, window) for _, _, _, keep in views]
            q = [stack_pair(load(i, v_proj, 0) * eighth) for i in chains]
            k = [load(i, v_proj, 1) for i in chains]
            v = [load(i, v_proj, 2) for i in chains]
            pulled = [jnp.where(views[i // n_pairs][3](128), load(i, v_dmix, 0), zero) for i in chains]
            do = [stack_pair(d) for d in pulled]
            score = [dot_nt(jnp.concatenate([k[i], extra[i // n_pairs][0]], 1),
                            jnp.concatenate([q[i], extra[i // n_pairs][1]], 1)) for i in chains]
            pulls = [dot_nt(v[i], do[i]) for i in chains]
            inner = []
            for i in chains:
                product = pulled[i].astype(F32) * load(i, v_mixed, 0).astype(F32)
                high = product.astype(BF)
                both = dot_nt(half_sum, high) + dot_nt(half_sum, (product - high.astype(F32)).astype(BF))
                inner.append(jnp.concatenate([both[0:1], both[1:2]], 1))

            def soft(i):
                prob_parts, ds_parts = [], []
                lse = v_lse[pl.ds(views[i // n_pairs][0] * n_pairs + i % n_pairs, 1), :2 * window]
                for j in range(0, 2 * window, 128):
                    part = slice(j, min(j + 128, 2 * window))
                    prob = jnp.exp(score[i][:, part] - lse[:, part])
                    ds_parts.append((prob * (pulls[i][:, part] - inner[i][:, part])).astype(BF))
                    prob_parts.append(prob.astype(BF))
                return jnp.concatenate(prob_parts, 1), jnp.concatenate(ds_parts, 1)

            def mix(i, prob, push):
                store = views[i // n_pairs][2]
                store(v_dproj, cols(2, i), dot(prob, do[i]))
                store(v_dproj, cols(1, i), dot(push, q[i]))
                dq = dot_tn(k[i] * eighth, push)
                store(v_dproj, cols(0, i), jnp.concatenate([dq[:64, :window], dq[64:, window:]], 0).T)

            ahead = soft(0)
            for i in chains:
                now = ahead
                if i + 1 < len(chains):
                    ahead = soft(i + 1)
                mix(i, *now)

        for_spans(lengths, row, T, r["spots"], run)
        if not fused:
            late[1].wait()
            late[2].wait()

        def fin_tile(t, carry):
            rows = tile_rows(t)
            fg = dot_nt(v_dproj[rows, :], w_qkv[...])
            hat, rstd = norm_parts(hidden(rows))
            v_first[rows, :] = (hat * r["n1g"][...] + r["n1b"][...]).astype(BF)
            vec[0:1, :] += colsum(fg * hat)
            vec[1:2, :] += colsum(fg)
            d = v_da[rows, :] + norm_pull(fg, hat, rstd, r["n1g"][...])
            v_dh[rows, :] = d
            if fused:
                r["v_bsnd"][rows, :] = d.astype(BF)
            for c in sends(t, pairs_b):
                c.start()
            return carry

        lax.fori_loop(0, n_tiles, fin_tile, 0)
        for t in range(n_tiles):
            for c in sends(t, pairs_a) + sends(t, pairs_b):
                c.wait()

    if f_rows != (NONE, NONE):
        f_row = pick(f_rows)

        @pl.when(f_row >= 0)
        def _():
            finish = forward(f_row)
            if fused:
                @pl.when(section == 1)
                def _():
                    backward(f_row)
            finish()
    else:
        b_row = pick(b_rows)

        @pl.when(b_row >= 0)
        def _():
            backward(b_row)


def row_slot(f_rows, b_rows, lengths, x, cot, arr, ret, w, bufs):
    n, T, D = x.shape
    FF = w["wu"].shape[1]
    S, V = jax.ShapeDtypeStruct, pltpu.VMEM
    does_f, does_b = max(f_rows) >= 0, max(b_rows) >= 0
    saves = f_rows[0] >= 0
    fused = b_rows[1] >= 0
    ins = {"lengths": (lengths, SMEM), "x": (x, ANY)}
    if does_b:
        ins["cot"] = (cot, ANY)
    if arr is not None:
        ins["arr"] = (arr, VMEM)
    if ret is not None:
        ins["ret"] = (ret, VMEM)
        ins.update({k: (bufs[k], ANY) for k in ("proj", "att", "slope", "mixed", "lse")})
    ins.update({k: (w[k], ANY) for k in ("wqkv", "wo", "wu", "wd")})
    ins.update({k: (w[k], VMEM) for k in ("n1g", "n1b", "bo", "n2g", "n2b", "bu", "bd")})
    wide = {"out": (D, BF), "mixed": (D, BF), "proj": (3 * D, BF), "att": (D, F32), "slope": (FF, BF), "dh": (D, F32),
            "first": (D, BF), "dproj": (3 * D, BF), "al": (D, BF), "second": (D, BF), "ul": (FF, BF), "gelu": (FF, BF),
            "gl": (D, BF)}
    keys = (["out", "mixed", "gelu"] if does_f else []) + (["proj", "att", "slope", "lse"] if saves else [])
    if does_b:
        keys += ["dh", "first", "dproj", "al", "second", "ul", "gl"]
    spans = lengths.shape[1] * D // 128
    outs = {k: (S((n, T, wide[k][0]), wide[k][1]) if k in wide else S((n, spans, LSE_WIDTH), F32), ANY) for k in keys}
    if saves:
        outs["snd"] = (S((T, D), BF), ANY)
    if fused:
        outs["bsnd"] = (S((T, D), BF), ANY)
    if does_b:
        outs["vec"] = (S((16, CHUNK), F32), VMEM)
    alias = [k for k in keys if k in bufs]
    scratch = {"v_x": V((T, D), BF), "w_qkv": V((D, 3 * D), BF), "w_out": V((D, D), BF), "w_up": V((D, FF), BF),
               "w_down": V((FF, D), BF), "v_proj": V((T, 3 * D), BF), "v_att": V((T, D), F32), "v_slope": V((T, FF), BF),
               "v_lse": V((spans, LSE_WIDTH), F32), "v_mixed": V((T, D), BF)}
    if does_f:
        scratch.update({"v_out": V((T, D), BF), "v_gelu": V((T, FF), BF)})
    if does_b:
        scratch.update({"v_" + k: V((T, wide[k][0]), wide[k][1])
                        for k in ("dh", "first", "dproj", "al", "second", "gl")})
        scratch.update({"v_cot": V((T, D), BF), "v_dmix": V((T, D), BF), "v_da": V((T, D), F32)})
    if fused:
        scratch["v_bsnd"] = V((T, D), BF)
    scratch.update({"sem_in": pltpu.SemaphoreType.DMA((24,)), "sem_out": pltpu.SemaphoreType.DMA((18, T // TILE)),
                    "spots": pltpu.SMEM((2 * lengths.shape[1] + 2,), jnp.int32), "sem_mixed": pltpu.SemaphoreType.DMA((2,))})
    names = list(ins) + ["alias_" + k for k in alias] + list(outs) + list(scratch)
    values = [v for v, _ in ins.values()] + [bufs[k] for k in alias]
    results = pl.pallas_call(
        functools.partial(row_kernel, f_rows, b_rows, names),
        out_shape=[o for o, _ in outs.values()],
        in_specs=[m for _, m in ins.values()] + [ANY] * len(alias),
        out_specs=[m for _, m in outs.values()],
        input_output_aliases={len(ins) + i: list(outs).index(k) for i, k in enumerate(alias)},
        scratch_shapes=list(scratch.values()),
        compiler_params=pltpu.CompilerParams(vmem_limit_bytes=(48 if does_b else 60) * 2**20),
        cost_estimate=pl.CostEstimate(flops=8 * 10**9 * does_f + 14 * 10**9 * does_b, bytes_accessed=20 * 2**20,
                                      transcendentals=0),
        name="row_" + "f" * does_f + "b" * does_b,
    )(*values)
    got = dict(zip(outs, results))
    send = (got.get("snd"), got.get("bsnd"))
    if None in send:
        send = send[0] if send[1] is None else send[1]
    return {**bufs, **{k: got[k] for k in keys}}, send, got.get("vec")


def reduce_kernel(n, *refs):
    bits = n.bit_length() - 1
    (gelu_any, gl_any, second_any, ul_any, mixed_any, al_any, first_any, dproj_any, vec_a, vec_b, vec_c, vec_d) = refs[:12]
    result, vec_out = refs[12:14]
    left, right, total, final, *rest = refs[14:]
    inbox = rest[:bits]
    (vec_box, vec_tmp, sem_load, sem_store, rs_send, rs_recv, ag_send, ag_recv, vec_send, vec_recv) = rest[bits:]
    n_chunks = total.shape[0]
    FF = gelu_any.shape[2]
    D = gl_any.shape[2]
    T = gl_any.shape[1]
    rows = gl_any.shape[0]
    ff_chunks = FF // CHUNK
    me = lax.axis_index("dp")
    size = total.shape[1]
    value = [(me // 2**b) % 2 for b in range(bits)]
    partner = [me + (1 - 2 * value[b]) * 2**b for b in range(bits)]
    base = [sum(value[i] * (size >> (i + 1)) for i in range(b)) for b in range(bits + 1)]

    def halve(c, b):
        half = size >> (b + 1)
        away = pl.multiple_of(base[b] + (1 - value[b]) * half, half)
        return pltpu.make_async_remote_copy(
            src_ref=total.at[c, pl.ds(away, half)], dst_ref=inbox[b].at[c],
            send_sem=rs_send.at[c, b], recv_sem=rs_recv.at[c, b],
            device_id={"dp": partner[b]}, device_id_type=MESH,
        )

    def double(c, b):
        half = size >> (b + 1)
        here = final.at[c, pl.ds(pl.multiple_of(base[b + 1], half), half)]
        return pltpu.make_async_remote_copy(
            src_ref=here, dst_ref=here,
            send_sem=ag_send.at[c, b], recv_sem=ag_recv.at[c, b],
            device_id={"dp": partner[b]}, device_id_type=MESH,
        )

    def add_in(c, b):
        half = size >> (b + 1)
        mine = pl.ds(pl.multiple_of(base[b + 1], half), half)
        target = total if b + 1 < bits else final
        target[c, mine, :] = (total[c, mine, :].astype(F32) + inbox[b][c].astype(F32)).astype(BF)

    def load(c, slot, act):
        def both(a, b):
            for k, (source, target) in enumerate(((a, left), (b, right))):
                act(pltpu.make_async_copy(source, target.at[slot], sem_load.at[k, slot]))

        def cols(ref, j):
            return ref.at[:, :, pl.ds(pl.multiple_of(j * CHUNK, CHUNK), CHUNK)]

        @pl.when(c < ff_chunks)
        def _():
            both(cols(gelu_any, c), gl_any)

        @pl.when((c >= ff_chunks) & (c < 2 * ff_chunks))
        def _():
            both(second_any, cols(ul_any, c - ff_chunks))

        @pl.when(c == 2 * ff_chunks)
        def _():
            both(mixed_any, al_any)

        @pl.when((c > 2 * ff_chunks) & (c < n_chunks))
        def _():
            both(first_any, cols(dproj_any, c - 2 * ff_chunks - 1))

    def publish(c):
        return pltpu.make_async_copy(final.at[c], result.at[c], sem_store.at[c])

    def vec_copy(b):
        return pltpu.make_async_remote_copy(
            src_ref=vec_tmp.at[b], dst_ref=vec_box.at[b],
            send_sem=vec_send.at[b], recv_sem=vec_recv.at[b],
            device_id={"dp": partner[b]}, device_id_type=MESH,
        )

    load(jnp.int32(0), 0, lambda c: c.start())
    vec_tmp[0] = vec_a[...] + vec_b[...] + vec_c[...] + vec_d[...]
    barrier = pltpu.get_barrier_semaphore()
    for b in range(bits):
        pl.semaphore_signal(barrier, inc=1, device_id={"dp": partner[b]}, device_id_type=MESH)
    pl.semaphore_wait(barrier, bits)
    vec_copy(0).start()

    gaps = [1, 2] + [1 + b % 2 for b in range(2, bits)]
    lags = [0]
    for gap in gaps[:bits] + gaps[bits - 1::-1]:
        lags.append(lags[-1] + gap)

    def slot_step(t, carry):
        def stage_of(lag, act):
            c = t - lag

            @pl.when((c >= 0) & (c < n_chunks))
            def _():
                act(c)

        def make(c):
            slot = lax.rem(c, 2)
            load(c + 1, 1 - slot, lambda d: d.start())
            load(c, slot, lambda d: d.wait())
            a = left[slot].reshape(rows * T, CHUNK)
            b = right[slot].reshape(rows * T, CHUNK)
            total[c] = dot_tn(a, b).astype(BF)
            halve(c, 0).start()

        def reduce_step(b):
            def act(c):
                halve(c, b).wait()
                add_in(c, b)
                if b + 1 < bits:
                    halve(c, b + 1).start()
                else:
                    double(c, b).start()
            return act

        def gather_step(b):
            def act(c):
                double(c, b).wait()
                double(c, b - 1).start()
            return act

        def finish(c):
            double(c, 0).wait()
            publish(c).start()

        acts = [make] + [reduce_step(b) for b in range(bits)] + [gather_step(b) for b in range(bits - 1, 0, -1)] + [finish]
        for lag, act in zip(lags, acts):
            stage_of(lag, act)
        return carry

    lax.fori_loop(0, n_chunks + lags[-1], slot_step, 0)
    for b in range(bits):
        vec_copy(b).wait()
        merged = vec_tmp[b] + vec_box[b]
        if b + 1 < bits:
            vec_tmp[b + 1] = merged
            vec_copy(b + 1).start()
        else:
            vec_out[...] = merged
    for c in range(n_chunks):
        publish(c).wait()


def wide_kernel(chunks, vec, wd, wu, wo, wqkv, n1g, n1b, bo, n2g, n2b, bd, bu, held, stage, sem_in, sem):
    blocks = [(w, r, c) for w in (wd, wu, wo, wqkv) for r in range(0, w.shape[1], CHUNK) for c in range(0, w.shape[2], CHUNK)]
    loads = [pltpu.make_async_copy(chunks.at[k], held.at[k], sem_in.at[k]) for k in range(len(blocks))]
    for c in loads:
        c.start()
    for i, small in enumerate((n1g, n1b, bo, n2g, n2b, bd)):
        small[...] = vec[i:i + 1, :]
    for i in range(bu.shape[1] // CHUNK):
        bu[:, i * CHUNK:(i + 1) * CHUNK] = vec[6 + i:7 + i, :]
    copies = []
    for k, (w, r, c) in enumerate(blocks):
        loads[k].wait()
        stage[k] = held[k].astype(F32)
        copies.append(pltpu.make_async_copy(stage.at[k], w.at[0, pl.ds(r, CHUNK), pl.ds(c, CHUNK)], sem.at[k]))
        copies[k].start()
    for c in copies:
        c.wait()


def widen(chunks, vec, shapes, small_shapes):
    n = chunks.shape[0]
    return pl.pallas_call(
        wide_kernel,
        out_shape=[jax.ShapeDtypeStruct(shape, F32) for shape in [(1, *s) for s in shapes] + small_shapes],
        in_specs=[ANY, VMEM],
        out_specs=[ANY] * len(shapes) + [VMEM] * len(small_shapes),
        scratch_shapes=[pltpu.VMEM(chunks.shape, BF), pltpu.VMEM(chunks.shape, F32),
                        pltpu.SemaphoreType.DMA((n,)), pltpu.SemaphoreType.DMA((n,))],
        compiler_params=pltpu.CompilerParams(vmem_limit_bytes=60 * 2**20),
        name="widen",
    )(chunks, vec)


def weight_grads(n, bufs, vecs):
    gl, ul = bufs["gl"], bufs["ul"]
    rows, T, D = gl.shape
    FF = ul.shape[2]
    bits = n.bit_length() - 1
    n_chunks = 2 * (FF // CHUNK) + 1 + 3 * D // CHUNK
    size = CHUNK
    S, V, DMA = jax.ShapeDtypeStruct, pltpu.VMEM, pltpu.SemaphoreType.DMA
    return pl.pallas_call(
        functools.partial(reduce_kernel, n),
        out_shape=[S((n_chunks, CHUNK, CHUNK), BF), S((16, CHUNK), F32)],
        in_specs=[ANY] * 8 + [VMEM] * 4,
        out_specs=[ANY, VMEM],
        scratch_shapes=[
            V((2, rows, T, CHUNK), BF), V((2, rows, T, CHUNK), BF), V((n_chunks, size, CHUNK), BF),
            V((n_chunks, size, CHUNK), BF),
            *[V((n_chunks, size >> (b + 1), CHUNK), BF) for b in range(bits)],
            V((bits, 16, CHUNK), F32), V((bits, 16, CHUNK), F32),
            DMA((2, 2)), DMA((n_chunks,)), DMA((n_chunks, bits)), DMA((n_chunks, bits)), DMA((n_chunks, bits)),
            DMA((n_chunks, bits)), DMA((bits,)), DMA((bits,)),
        ],
        compiler_params=pltpu.CompilerParams(vmem_limit_bytes=62 * 2**20, collective_id=0, has_side_effects=True),
        cost_estimate=pl.CostEstimate(flops=13 * 10**9, bytes_accessed=60 * 2**20, transcendentals=0),
        name="weight_grads",
    )(*[bufs[k] for k in ("gelu", "gl", "second", "ul", "mixed", "al", "first", "dproj")], *vecs)


def body(inputs, cotangent, lengths, norm1_gain, norm1_bias, weight_qkv, weight_out, bias_out, norm2_gain, norm2_bias,
         weight_up, bias_up, weight_down, bias_down):
    w = dict(n1g=norm1_gain, n1b=norm1_bias, wqkv=weight_qkv[0], wo=weight_out[0], bo=bias_out, n2g=norm2_gain,
             n2b=norm2_bias, wu=weight_up[0], bu=bias_up, wd=weight_down[0], bd=bias_down)
    x, cot = inputs[0], cotangent[0]
    n = lax.axis_size("dp")

    def ahead(block):
        return lax.ppermute(block, "section", [(0, 1)])

    def back(block):
        return lax.ppermute(block, "section", [(1, 0)])

    bufs, send_a, _ = row_slot((0, NONE), (NONE, NONE), lengths, x, cot, None, None, w, {})
    row_0 = ahead(send_a)
    bufs, send_b, _ = row_slot((1, NONE), (NONE, NONE), lengths, x, cot, None, None, w, bufs)
    row_1 = ahead(send_b)
    bufs, back_b, vec_b = row_slot((NONE, 0), (NONE, 0), lengths, x, cot, row_0, None, w, bufs)
    ret_0 = back(back_b)
    bufs, back_d, vec_d = row_slot((NONE, 1), (NONE, 1), lengths, x, cot, row_1, None, w, bufs)
    ret_1 = back(back_d)
    bufs, _, vec_e = row_slot((NONE, NONE), (0, NONE), lengths, x, cot, None, ret_0, w, bufs)
    bufs, _, vec_g = row_slot((NONE, NONE), (1, NONE), lengths, x, cot, None, ret_1, w, bufs)
    chunks, vec = weight_grads(n, bufs, (vec_b, vec_d, vec_e, vec_g))

    matrices, small = ("wd", "wu", "wo", "wqkv"), ("n1g", "n1b", "bo", "n2g", "n2b", "bd", "bu")
    g = dict(zip(matrices + small, widen(chunks, vec, [w[k].shape for k in matrices], [w[k].shape for k in small])))
    order = ("n1g", "n1b", "wqkv", "wo", "bo", "n2g", "n2b", "wu", "bu", "wd", "bd")
    return (bufs["out"][None], bufs["dh"][None], *[g[k] for k in order])


def solution(mesh):
    matrix, row = P("section", None, None), P("section", None)
    data = P("section", "dp", None, None)
    return jax.shard_map(
        body,
        mesh=mesh,
        in_specs=(data, data, P("dp", None), row, row, matrix, matrix, row, row, row, matrix, row, matrix, row),
        out_specs=(data, data, row, row, matrix, matrix, row, row, row, matrix, row, matrix, row),
        check_vma=False,
    )
```
